32 devices in a mesh: wide: 8 (over z, y), narrow: 4 (over x, core).
Axes of the slice: x: 2, y: 2, z: 4, core: 2. Of those that a mesh axis runs over, the one named last changes fastest.
Arguments:
- tokens: bfloat16 [26624, 768], P(('wide', 'narrow')), may hold values from -6 to 6
- kinds: int32 [26624], P(('wide', 'narrow')), may hold values from 0 to 1
- lengths: int32 [128], P(('wide', 'narrow')), may hold values from 52 to 208, as said below
- query_weight: bfloat16 [768, 768], replicated, may hold values from -0.21875 to 0.21875
- key_weight: bfloat16 [768, 768], replicated, may hold values from -0.21875 to 0.21875
- value_weight: bfloat16 [768, 768], replicated, may hold values from -0.21875 to 0.21875
- output_weight: bfloat16 [768, 768], replicated, may hold values from -0.875 to 0.875
- inner_weight: bfloat16 [768, 768], replicated, may hold values from -0.21875 to 0.21875
- outer_weight: bfloat16 [768, 768], replicated, may hold values from -0.21875 to 0.21875
- query_bias: bfloat16 [768], replicated, may hold values from -1 to 1
- value_bias: bfloat16 [768], replicated, may hold values from -1 to 1
- output_bias: bfloat16 [768], replicated, may hold values from -1 to 1
- inner_bias: bfloat16 [768], replicated, may hold values from -1 to 1
- outer_bias: bfloat16 [768], replicated, may hold values from -1 to 1
- first_gain: bfloat16 [768], replicated, may hold values from 0.5 to 1.5
- first_shift: bfloat16 [768], replicated, may hold values from -1 to 1
- second_gain: bfloat16 [768], replicated, may hold values from 0.5 to 1.5
- second_shift: bfloat16 [768], replicated, may hold values from -1 to 1
- type_table: bfloat16 [2, 768], replicated, may hold values from -3 to 3
- cotangent: bfloat16 [26624, 768], P(('wide', 'narrow')), may hold values from -6 to 6
Outputs:
- layer_out: bfloat16 [26624, 768], P(('wide', 'narrow'))
- tokens_grad: bfloat16 [26624, 768], P(('wide', 'narrow'))
- query_grad: float32 [768, 768], replicated
- key_grad: float32 [768, 768], replicated
- value_grad: float32 [768, 768], replicated
- output_grad: float32 [768, 768], replicated
- inner_grad: float32 [768, 768], replicated
- outer_grad: float32 [768, 768], replicated
- query_bias_grad: float32 [768], replicated
- value_bias_grad: float32 [768], replicated
- output_bias_grad: float32 [768], replicated
- inner_bias_grad: float32 [768], replicated
- outer_bias_grad: float32 [768], replicated
- first_gain_grad: float32 [768], replicated
- first_shift_grad: float32 [768], replicated
- second_gain_grad: float32 [768], replicated
- second_shift_grad: float32 [768], replicated
- table_grad: float32 [2, 768], replicated
The draws below stay inside these ranges and needn't reach their ends.
Inputs may be any that keep to these rules, and one draw needn't show every extreme that they name: `lengths`: tokens of each molecule; the remaining of its 208 slots are padding. `kinds`: 0 marks a node token, 1 an edge token.
All inputs are finite; a program needn't handle non-finite values.
Results may differ from the reference program's by a relative error of at most 0.012.
Values sent between devices are 32-bit elements; how exact they have to be, the bound alone decides.
No kernel may reach another device: no remote copies, remote signals or barrier semaphores. Data moves between devices by JAX's collectives and lax.ppermute only.
A program may use at most 192 MiB of HBM per device.

```python
import math
import jax
import jax.numpy as jnp
from jax import lax

D = 768
H = 32
FF = 768
DH = 24
SLOT = 208
MOL_DEV = 4
MOLS = 128
TOKENS = 26624
N_WIDE = 8
N_NARROW = 4


def draw_lengths(key, part):
    key = jax.random.fold_in(key, 11)
    key_top, key_raw, key_pick = jax.random.split(key, 3)
    groups = MOLS // MOL_DEV
    lowest = SLOT // 4
    device_top = jax.random.randint(key_top, (groups,), SLOT // 2, SLOT + 1)
    row_top = jnp.repeat(device_top, MOL_DEV, total_repeat_length=MOLS)
    raw = jax.random.randint(key_raw, (MOLS,), 0, 1 << 20)
    drawn = lowest + raw % (row_top - lowest + 1)
    pick = jax.random.randint(key_pick, (), 0, MOLS)
    return jnp.where(jnp.arange(MOLS) == pick, SLOT, drawn).astype(jnp.int32)


def plant(values, own_key, low, high):
    index_at = [jax.random.randint(jax.random.fold_in(own_key, axis), (), 0, length) for axis, length in enumerate(values.shape)]
    main_axis = values.shape.index(max(values.shape))
    neighbour = index_at[:main_axis] + [(index_at[main_axis] + 1) % values.shape[main_axis]] + index_at[main_axis + 1:]
    return values.at[tuple(index_at)].set(low).at[tuple(neighbour)].set(high)


def block_scale(stream_key, shape, pieces, smallest, top_value):
    level = 1.0
    for dim, blocks in pieces:
        steps = jax.random.uniform(jax.random.fold_in(jax.random.fold_in(stream_key, 6), dim), (blocks,), jnp.float32, smallest / len(pieces), top_value / len(pieces))
        level = level * jnp.repeat(jnp.exp(steps), shape[dim] // blocks).reshape((-1,) + (1,) * (len(shape) - 1 - dim))
    return level


def centred(rng, shape, width, bound, shards=(), held_as=jnp.bfloat16):
    values = width * jax.random.normal(rng, shape, jnp.float32)
    if shards:
        values = values * block_scale(rng, shape, shards, -0.22, 0.18)
    return jnp.clip(values, -bound, bound).astype(held_as)


def setup_inputs(seed: int = 0) -> dict:
    seeds = jax.random.split(jax.random.key(seed), 21)
    return {
        "tokens": centred(seeds[0], (TOKENS, D), 1.0, 6.0, ((0, 32),)),
        "kinds": plant(jax.random.randint(seeds[1], (TOKENS,), 0, 2), jax.random.fold_in(seeds[1], 1), 0, 1).astype(jnp.int32),
        "lengths": draw_lengths(jax.random.fold_in(seeds[20], 71), 0),
        "query_weight": centred(seeds[3], (D, D), D ** -0.5, 0.21875),
        "key_weight": centred(seeds[4], (D, D), D ** -0.5, 0.21875),
        "value_weight": centred(seeds[5], (D, D), D ** -0.5, 0.21875),
        "output_weight": centred(seeds[6], (D, D), (D // 16) ** -0.5, 0.875),
        "inner_weight": centred(seeds[7], (D, FF), D ** -0.5, 0.21875),
        "outer_weight": centred(seeds[8], (FF, D), FF ** -0.5, 0.21875),
        "query_bias": centred(seeds[9], (D,), 0.2, 1.0),
        "value_bias": centred(seeds[10], (D,), 0.2, 1.0),
        "output_bias": centred(seeds[11], (D,), 0.2, 1.0),
        "inner_bias": centred(seeds[12], (FF,), 0.2, 1.0),
        "outer_bias": centred(seeds[13], (D,), 0.2, 1.0),
        "first_gain": jnp.clip(1.0 + 0.1 * jax.random.normal(seeds[14], (D,), jnp.float32), 0.5, 1.5).astype(jnp.bfloat16),
        "first_shift": centred(seeds[15], (D,), 0.2, 1.0),
        "second_gain": jnp.clip(1.0 + 0.1 * jax.random.normal(seeds[16], (D,), jnp.float32), 0.5, 1.5).astype(jnp.bfloat16),
        "second_shift": centred(seeds[17], (D,), 0.2, 1.0),
        "type_table": centred(seeds[18], (2, D), 0.5, 3.0),
        "cotangent": centred(seeds[19], (TOKENS, D), 1.0, 6.0, ((0, 32),)),
    }


@jax.custom_vjp
def low(v):
    return lax.optimization_barrier(v.astype(jnp.bfloat16)).astype(jnp.float32)

@jax.custom_vjp
def low_back(v):
    return v

def low_keep(v):
    return (low(v), None)

def low_pass(kept, grad):
    return (grad,)

def back_keep(v):
    return (v, None)

def back_low(kept, grad):
    return (low(grad),)
low.defvjp(low_keep, low_pass)
low_back.defvjp(back_keep, back_low)
HIGHEST = lax.Precision.HIGHEST

def matmul(left, right):
    return jnp.dot(left, right, precision=HIGHEST)

def layer_norm(values, gain, shift):
    average = lax.optimization_barrier(jnp.mean(values, -1, keepdims=True))
    centered = values - average
    spread = lax.optimization_barrier(jnp.mean(centered * centered, -1, keepdims=True))
    return centered * lax.rsqrt(spread + 1e-05) * gain + shift

def forward(params, tokens, kinds, valid):
    query_weight, key_weight, value_weight, output_weight, inner_weight, outer_weight, query_bias, value_bias, output_bias, inner_bias, outer_bias, first_gain, first_shift, second_gain, second_shift, type_table = params
    count = tokens.shape[0] // SLOT
    scale = 1.0 / math.sqrt(DH)
    start = tokens + jnp.where(kinds[:, None] == 1, type_table[1], type_table[0])
    first = low(layer_norm(start, first_gain, first_shift))
    query = low(low_back(matmul(first, query_weight) + query_bias)).reshape(count, SLOT, H, DH)
    keys = low(low_back(matmul(first, key_weight))).reshape(count, SLOT, H, DH)
    values = low(low_back(matmul(first, value_weight) + value_bias)).reshape(count, SLOT, H, DH)
    scores = low_back(jnp.einsum('mqhd,mkhd->mhqk', query, keys, precision=HIGHEST) * scale)
    keymask = valid.reshape(count, 1, 1, SLOT) > 0.5
    scores = jnp.where(keymask, scores, -1e+30)
    row_max = lax.optimization_barrier(jnp.max(scores, -1, keepdims=True))
    powered = jnp.exp(scores - row_max)
    probs = low(powered / lax.optimization_barrier(jnp.sum(powered, -1, keepdims=True)))
    mixed = jnp.einsum('mhqk,mkhd->mqhd', probs, values, precision=HIGHEST).reshape(count * SLOT, D)
    mixed = low(low_back(mixed))
    middle = start + low_back(matmul(mixed, output_weight) + output_bias)
    second = low(layer_norm(middle, second_gain, second_shift))
    inner = low_back(matmul(second, inner_weight) + inner_bias)
    act = low(jax.nn.gelu(inner))
    result = middle + matmul(act, outer_weight) + outer_bias
    return result * valid[:, None]

def reference(tokens, kinds, lengths, query_weight, key_weight, value_weight, output_weight, inner_weight, outer_weight, query_bias, value_bias, output_bias, inner_bias, outer_bias, first_gain, first_shift, second_gain, second_shift, type_table, cotangent):
    params = tuple((p.astype(jnp.float32) for p in (query_weight, key_weight, value_weight, output_weight, inner_weight, outer_weight, query_bias, value_bias, output_bias, inner_bias, outer_bias, first_gain, first_shift, second_gain, second_shift, type_table)))
    groups = MOLS // 16
    per_group = 16 * SLOT
    place = jnp.arange(SLOT, dtype=jnp.int32)
    valid = (place[None, :] < lengths[:, None]).astype(jnp.float32).reshape(-1)
    token_groups = tokens.astype(jnp.float32).reshape(groups, per_group, D)
    kind_groups = kinds.reshape(groups, per_group)
    valid_groups = valid.reshape(groups, per_group)
    grad_groups = cotangent.astype(jnp.float32).reshape(groups, per_group, D)

    def step(totals, item):
        token_part, kind_part, valid_part, grad_part = item

        def local(weights, inputs):
            return forward(weights, inputs, kind_part, valid_part)
        result, pull = jax.vjp(local, params, token_part)
        weight_grads, input_grad = pull(grad_part)
        totals = jax.tree.map(lambda a, b: a + b, totals, weight_grads)
        return (totals, (result.astype(jnp.bfloat16), input_grad.astype(jnp.bfloat16)))
    zeros = jax.tree.map(jnp.zeros_like, params)
    totals, (results, input_grads) = lax.scan(step, zeros, (token_groups, kind_groups, valid_groups, grad_groups))
    factor = 1.0 / (N_WIDE * N_NARROW)
    scaled = [g * factor for g in totals]
    return (results.reshape(TOKENS, D), input_grads.reshape(TOKENS, D), scaled[0], scaled[1], scaled[2], scaled[3], scaled[4], scaled[5], scaled[6], scaled[7], scaled[8], scaled[9], scaled[10], scaled[11], scaled[12], scaled[13], scaled[14], scaled[15])
```

```python
import functools
import math

import jax
import jax.numpy as jnp
import numpy as np
from jax import lax
from jax.experimental import pallas as pl
from jax.experimental.pallas import tpu as pltpu
from jax.sharding import PartitionSpec as P

D = 768
H = 32
DH = 24
SLOT = 208
GROUP = 16
HALF = GROUP * DH
SCALE = 1.0 / math.sqrt(DH)
LOG_SCALE = math.log2(math.e) / math.sqrt(DH)
AXES = ("wide", "narrow")
NN = (((1,), (0,)), ((), ()))
NT = (((1,), (1,)), ((), ()))
TN = (((0,), (0,)), ((), ()))
F32 = jnp.float32
BF16 = jnp.bfloat16
ANY = pl.BlockSpec(memory_space=pl.ANY)


def dot(left, right, dims=NN):
    return lax.dot_general(left, right, dims, preferred_element_type=F32)


def head_lanes():
    lanes = np.zeros((GROUP, 256), np.float32)
    for h in range(GROUP):
        begin = DH * h - 128 * window(h)
        lanes[h, begin : begin + DH] = 1
    return lanes


def window(h):
    return 0 if h < 10 else 1


def norm_parts(values):
    average = jnp.mean(values, -1, keepdims=True)
    centered = values - average
    inv_std = lax.rsqrt(jnp.mean(centered * centered, -1, keepdims=True) + 1e-05)
    return centered * inv_std, inv_std


def norm_back(grad_hat, normed, inv_std):
    return (
        grad_hat
        - jnp.mean(grad_hat, -1, keepdims=True)
        - normed * jnp.mean(grad_hat * normed, -1, keepdims=True)
    ) * inv_std


def embed(tokens_ref, kinds_ref, table_ref):
    edge = kinds_ref[...] == 1
    table = table_ref[...].astype(F32)
    return tokens_ref[...].astype(F32) + jnp.where(edge, table[1:2], table[0:1])


def key_bias(count):
    slot = lax.broadcasted_iota(jnp.int32, (SLOT, 256), 0)
    lane = lax.broadcasted_iota(jnp.int32, (SLOT, 256), 1)
    return [jnp.where((lane == spare) & (slot >= count), -1e30, 0.0).astype(BF16) for spare in (240, 0)]


def query_windows(query_ref, offset):
    lane = lax.broadcasted_iota(jnp.int32, (SLOT, 256), 1)
    result = []
    for w, spare in ((0, lane >= 240), (1, lane < 112)):
        ones = jnp.where(spare, 1.0, 0.0).astype(BF16)
        keep = jnp.where(spare, 0.0, 1.0).astype(BF16)
        result.append(query_ref[:, pl.ds(offset + 128 * w, 256)] * keep + ones)
    return result


def by_head(values, heads, extra):
    turned = values.astype(F32).T.reshape(heads, DH, SLOT)
    row = lax.broadcasted_iota(jnp.int32, (heads, 32 - DH, SLOT), 1)
    return jnp.concatenate([turned, jnp.where(row == 0, extra, 0.0)], 1).astype(BF16)


def attend_kernel(
    lengths_ref, tokens_ref, kinds_ref, table_ref, gain_ref, shift_ref, query_weight_ref, key_weight_ref,
    value_weight_ref, query_bias_ref, value_bias_ref, lanes_ref,
    first_ref, query_ref, keys_ref, values_ref, mixed_ref, stat_ref,
    turned_ref, scores_ref, out_ref,
):
    count = lengths_ref[pl.program_id(0)]
    normed, unused = norm_parts(embed(tokens_ref, kinds_ref, table_ref))
    first32 = normed * gain_ref[...].astype(F32) + shift_ref[...].astype(F32)
    first = first32.astype(BF16)
    first_ref[0] = first32.T.astype(BF16)
    query_ref[...] = (dot(first, query_weight_ref[...]) + query_bias_ref[...].astype(F32)).astype(BF16)
    keys_ref[...] = dot(first, key_weight_ref[...]).astype(BF16)
    values_ref[...] = (dot(first, value_weight_ref[...]) + value_bias_ref[...].astype(F32)).astype(BF16)
    turned_ref[...] = by_head(values_ref[...], H, 1.0)
    bias = key_bias(count)
    lag = 3

    def group(g, carry):
        offset = pl.multiple_of(g * HALF, 128)
        queries = query_windows(query_ref, offset)
        keys = [keys_ref[:, pl.ds(offset + 128 * w, 256)] for w in (0, 1)]

        def score(h):
            w = window(h)
            scores_ref[h % (lag + 1)] = dot(keys[w] * lanes_ref[h : h + 1, :] + bias[w], queries[w], NT)

        def mix(h):
            scores = scores_ref[h % (lag + 1)]
            top = jnp.max(scores, axis=0, keepdims=True)
            powered = jnp.exp2((scores - top) * LOG_SCALE).astype(BF16)
            out = dot(turned_ref[g * GROUP + h], powered)
            total = out[DH : DH + 1]
            out_ref[pl.ds(pl.multiple_of(g * HALF, 8) + h * DH, DH), :] = out[:DH] * (1.0 / total)
            stat_ref[0, g, h : h + 1] = top * LOG_SCALE + jnp.log2(total)

        for h in range(GROUP + lag):
            if h < GROUP:
                score(h)
            if h >= lag:
                mix(h - lag)
        return carry

    lax.fori_loop(0, 2, group, 0)
    mixed_ref[0] = out_ref[...].astype(BF16)


def gelu_parts(inner):
    root = math.sqrt(2.0 / math.pi)
    square = inner * inner
    bent = jnp.tanh(root * (inner + 0.044715 * inner * square))
    half = 0.5 * (1.0 + bent)
    slope = half + 0.5 * inner * (1.0 - bent * bent) * root * (1.0 + 3 * 0.044715 * square)
    return inner * half, slope


def dense_kernel(
    factor, lengths_ref, tokens_ref, kinds_ref, table_ref, mixed_ref, cotangent_ref, output_weight_ref,
    inner_weight_ref, outer_weight_ref, output_bias_ref, inner_bias_ref, outer_bias_ref, gain_ref, shift_ref,
    layer_ref, grad_middle_ref, grad_mixed_ref, outer_grad_ref, inner_grad_ref, output_grad_ref, vectors_ref,
):
    mol = pl.program_id(0)

    @pl.when(mol == 0)
    def start_sums():
        for ref in (outer_grad_ref, inner_grad_ref, output_grad_ref, vectors_ref):
            ref[...] = jnp.zeros_like(ref)

    valid = (lax.broadcasted_iota(jnp.int32, (SLOT, 1), 0) < lengths_ref[mol]).astype(F32)
    gain = gain_ref[...].astype(F32)
    mixed = mixed_ref[0]
    middle = (
        embed(tokens_ref, kinds_ref, table_ref)
        + dot(mixed, output_weight_ref[...], TN)
        + output_bias_ref[...].astype(F32)
    )
    normed, inv_std = norm_parts(middle)
    second = (normed * gain + shift_ref[...].astype(F32)).astype(BF16)
    inner = dot(second, inner_weight_ref[...]) + inner_bias_ref[...].astype(F32)
    act32, slope = gelu_parts(inner)
    act = act32.astype(BF16)
    grad_out = cotangent_ref[...].astype(F32) * valid
    grad_low = grad_out.astype(BF16)
    outer_grad_ref[...] += dot(act, grad_low, TN)
    grad_inner = (dot(grad_low, outer_weight_ref[...], NT) * slope).astype(BF16)
    inner_grad_ref[...] += dot(second, grad_inner, TN)
    layer = middle + dot(act, outer_weight_ref[...]) + outer_bias_ref[...].astype(F32)
    layer_ref[...] = (layer * valid).astype(BF16)
    grad_second = dot(grad_inner, inner_weight_ref[...], NT)
    grad_middle = grad_out + norm_back(grad_second * gain, normed, inv_std)
    grad_middle_ref[...] = grad_middle
    grad_attn = grad_middle.astype(BF16)
    output_grad_ref[...] += dot(mixed, grad_attn)
    grad_mixed_ref[...] = dot(grad_attn, output_weight_ref[...], NT).astype(BF16)
    sums = [
        grad_out,
        grad_inner.astype(F32),
        grad_second * normed,
        grad_second,
        grad_attn.astype(F32),
    ]
    for i, values in enumerate(sums):
        vectors_ref[i : i + 1] += jnp.sum(values, 0, keepdims=True)

    @pl.when(mol == pl.num_programs(0) - 1)
    def scale_sums():
        for ref in (outer_grad_ref, inner_grad_ref, output_grad_ref, vectors_ref):
            ref[...] = ref[...] * factor


def back_kernel(
    factor, lengths_ref, first_ref, query_ref, keys_ref, values_ref, grad_ref, stat_ref, lanes_ref,
    weight_grad_ref, vectors_ref, turned_grads_ref,
    turned_query_ref, turned_keys_ref, turned_out_ref, scores_ref, probs_ref, grads_ref,
):
    mol = pl.program_id(0)

    @pl.when(mol == 0)
    def start_sums():
        weight_grad_ref[...] = jnp.zeros_like(weight_grad_ref)
        vectors_ref[...] = jnp.zeros_like(vectors_ref)

    for source, target in (
        (query_ref, turned_query_ref),
        (keys_ref, turned_keys_ref),
        (grad_ref, turned_out_ref),
    ):
        target[...] = by_head(source[...], GROUP, 0.0)
    bias = key_bias(lengths_ref[mol])
    queries = query_windows(query_ref, 0)
    keys, values, outs = (
        [ref[:, 128 * w : 128 * w + 256] for w in (0, 1)] for ref in (keys_ref, values_ref, grad_ref)
    )
    lag = 2

    def score(h):
        w = window(h)
        lanes = lanes_ref[h : h + 1, :]
        scores_ref[h % (lag + 1)] = dot(keys[w] * lanes + bias[w], queries[w], NT)
        probs_ref[h % (lag + 1)] = dot(values[w] * lanes, outs[w], NT)

    def back(h):
        probs = jnp.exp2(scores_ref[h % (lag + 1)] * LOG_SCALE - stat_ref[0, 0, h : h + 1])
        grad_probs = probs_ref[h % (lag + 1)]
        shared = jnp.sum(probs * grad_probs, axis=0, keepdims=True)
        grad_scores = (probs * (grad_probs - shared)).astype(BF16)
        rows = slice(h * DH, (h + 1) * DH)
        grads_ref[0, rows] = dot(turned_keys_ref[h], grad_scores)[:DH] * SCALE
        grads_ref[1, rows] = dot(turned_query_ref[h], grad_scores, NT)[:DH] * SCALE
        grads_ref[2, rows] = dot(turned_out_ref[h], probs.astype(BF16), NT)[:DH]

    for h in range(GROUP + lag):
        if h < GROUP:
            score(h)
        if h >= lag:
            back(h - lag)
    ones = jnp.ones((8, SLOT), BF16)
    for i in range(3):
        grads = grads_ref[i].astype(BF16)
        turned_grads_ref[0, i] = grads
        columns = slice(i * HALF, (i + 1) * HALF)
        weight_grad_ref[:, columns] += dot(first_ref[0], grads, NT)
        vectors_ref[:, columns] += dot(ones, grads, NT)

    @pl.when(mol == pl.num_programs(0) - 1)
    def scale_sums():
        weight_grad_ref[...] = weight_grad_ref[...] * factor
        vectors_ref[...] = vectors_ref[...] * factor


def input_kernel(
    factor, tokens_ref, kinds_ref, table_ref, gain_ref, grads_low_ref, grads_high_ref, query_weight_ref,
    key_weight_ref, value_weight_ref, grad_middle_ref,
    tokens_grad_ref, vectors_ref,
):
    mol = pl.program_id(0)

    @pl.when(mol == 0)
    def start_sums():
        vectors_ref[...] = jnp.zeros_like(vectors_ref)

    total = jnp.zeros((D, SLOT), F32)
    for i, weight_ref in enumerate((query_weight_ref, key_weight_ref, value_weight_ref)):
        total = total + dot(weight_ref[:, :HALF], grads_low_ref[0, i])
        total = total + dot(weight_ref[:, HALF:], grads_high_ref[0, i])
    grad_first = total.T
    normed, inv_std = norm_parts(embed(tokens_ref, kinds_ref, table_ref))
    gain = gain_ref[...].astype(F32)
    grad_start = grad_middle_ref[...] + norm_back(grad_first * gain, normed, inv_std)
    tokens_grad_ref[...] = grad_start.astype(BF16)
    edge = kinds_ref[...] == 1
    sums = [
        grad_first * normed,
        grad_first,
        jnp.where(edge, 0.0, grad_start),
        jnp.where(edge, grad_start, 0.0),
    ]
    for i, values in enumerate(sums):
        vectors_ref[i : i + 1] += jnp.sum(values, 0, keepdims=True)

    @pl.when(mol == pl.num_programs(0) - 1)
    def scale_sums():
        vectors_ref[...] = vectors_ref[...] * factor


def whole(*shape):
    return pl.BlockSpec(shape, lambda i, *_: (0,) * len(shape))


def rows_of(width):
    return pl.BlockSpec((SLOT, width), lambda i, *_: (i, 0))


def mols_of(*shape):
    return pl.BlockSpec((1,) + shape, lambda i, *_: (i,) + (0,) * len(shape))


def shape_of(*shape, dtype=F32):
    return jax.ShapeDtypeStruct(shape, dtype)


def call(kernel, count, in_specs, out_specs, out_shape, scratch, args, flops, name):
    return pl.pallas_call(
        kernel,
        grid_spec=pltpu.PrefetchScalarGridSpec(
            num_scalar_prefetch=1,
            grid=(count,),
            in_specs=in_specs,
            out_specs=out_specs,
            scratch_shapes=scratch,
        ),
        out_shape=out_shape,
        compiler_params=pltpu.CompilerParams(
            dimension_semantics=("arbitrary",), vmem_limit_bytes=52 * 2**20
        ),
        cost_estimate=pl.CostEstimate(flops=flops, bytes_accessed=2**20, transcendentals=0),
        name=name,
    )(*args)


def bits_of(mesh_shape):
    narrow = mesh_shape["narrow"].bit_length() - 1
    wide = mesh_shape["wide"].bit_length() - 1
    y = (wide - 1) // 2
    return {
        "c": [0],
        "x": list(range(1, narrow)),
        "y": list(range(narrow, narrow + y)),
        "z": list(range(narrow + y, narrow + wide)),
    }


def swap(values, bit, devices):
    return lax.ppermute(values, AXES, [(i, i ^ (1 << bit)) for i in range(devices)])


def pick(values, *index):
    for i in index:
        values = lax.dynamic_index_in_dim(values, i, 0, keepdims=False)
    return values


def place_kernel(place_ref, own_ref, other_ref, *refs):
    outs = refs[-3:]
    step = pl.program_id(0)
    second = jnp.where(step // 4 == 0, place_ref[2], place_ref[1])
    level = place_ref[3]
    from_other = lax.rem(step // 2, 2) == 1

    def move(source):
        for i in range(2):
            for j in range(2):
                a = lax.bitwise_xor(i, second)
                b = lax.bitwise_xor(j, level)
                for k, out in enumerate(outs):
                    out[0, 0, 0, a, b] = source[0, 0, i, j, :, k * HALF : (k + 1) * HALF]

    @pl.when(jnp.logical_not(from_other))
    def own():
        move(own_ref)

    @pl.when(from_other)
    def other():
        move(other_ref)


def put_in_place(place, own, other, before, part):
    width = own.shape[-1]
    rows = own.shape[-2]

    def source(core):
        def index(step, place):
            half, mid, low = step // 4, lax.rem(step // 2, 2), lax.rem(step, 2)
            if core == 0:
                kept = jnp.where(mid == 0, low, 1)
            else:
                kept = jnp.where(mid == 1, low, 0)
            return (half, kept, 0, 0, 0, 0)

        return pl.BlockSpec((1, 1, 2, 2, rows, width), index)

    def target(step, place):
        half, mid, low = step // 4, lax.rem(step // 2, 2), lax.rem(step, 2)
        first = jnp.where(half == 0, place[1], place[2])
        return (half, lax.bitwise_xor(mid, place[0]), lax.bitwise_xor(low, first), 0, 0, 0, part)

    shape = (2, 2, 2, 2, 2, rows, D)
    aliases = {} if before is None else {3 + i: i for i in range(3)}
    extra = [] if before is None else list(before)
    return pl.pallas_call(
        place_kernel,
        grid_spec=pltpu.PrefetchScalarGridSpec(
            num_scalar_prefetch=1,
            grid=(8,),
            in_specs=[source(0), source(1)] + [ANY] * len(extra),
            out_specs=[pl.BlockSpec((1, 1, 1, 2, 2, rows, HALF), target)] * 3,
        ),
        out_shape=[shape_of(*shape)] * 3,
        input_output_aliases=aliases,
        compiler_params=pltpu.CompilerParams(vmem_limit_bytes=40 * 2**20),
        name="place",
    )(place, own, other, *extra)


def spread_sum(values, bits, me, devices):
    rows = values.shape[0] // 32
    width = values.shape[1]
    blocks = values.reshape(2, 2, 2, 2, 2, rows, width)
    core, x, y, z = (bits[k][0] for k in "cxyz")
    orders = ((x, y), (y, x))
    got = swap(lax.dynamic_index_in_dim(blocks, 1 - me[core], 1, keepdims=False), core, devices)
    kept = lax.dynamic_index_in_dim(blocks, me[core], 1, keepdims=False)
    parts = []
    for half, (first, second) in enumerate(orders):
        terms = [kept[half], got[half]]
        for bit in (first, second):
            sent = functools.reduce(jnp.add, [pick(t, 1 - me[bit]) for t in terms])
            terms = [pick(t, me[bit]) for t in terms] + [swap(sent, bit, devices)]
        parts.append(terms)
    sent = jnp.stack([functools.reduce(jnp.add, [pick(t, 1 - me[z]) for t in terms]) for terms in parts])
    total = jnp.stack([functools.reduce(jnp.add, [pick(t, me[z]) for t in terms]) for terms in parts])
    total = total + swap(sent, z, devices)
    for bit in bits["x"][1:] + bits["y"][1:] + bits["z"][1:]:
        total = total + swap(total, bit, devices)
    across = swap(total, z, devices)
    gathered = []
    for half, (first, second) in enumerate(orders):
        held = jnp.stack([total[half], across[half]])
        held = jnp.stack([held, swap(held, second, devices)])
        held = jnp.stack([held, swap(held, first, devices)])
        gathered.append(held)
    own = jnp.stack(gathered)
    return own, swap(own, core, devices)


def small_sum(values, devices):
    bit = 0
    while 1 << bit < devices:
        values = values + swap(values, bit, devices)
        bit += 1
    return values


def per_device(
    mesh_shape, tokens, kinds, lengths, query_weight, key_weight, value_weight, output_weight, inner_weight,
    outer_weight, query_bias, value_bias, output_bias, inner_bias, outer_bias, first_gain, first_shift,
    second_gain, second_shift, type_table, cotangent,
):
    count = lengths.shape[0]
    rows = tokens.shape[0]
    devices = mesh_shape["wide"] * mesh_shape["narrow"]
    factor = 1.0 / devices
    bits = bits_of(mesh_shape)
    index = lax.axis_index("wide") * mesh_shape["narrow"] + lax.axis_index("narrow")
    me = [(index >> bit) & 1 for bit in range(devices.bit_length() - 1)]
    place = jnp.stack([me[bits[k][0]] for k in "cxyz"]).astype(jnp.int32)
    kinds = kinds.reshape(rows, 1)
    row = lambda vector: vector.reshape(1, D)
    lanes = jnp.asarray(head_lanes(), BF16)
    vec = whole(1, D)
    weight = whole(D, D)
    unit = 2 * rows * D * D
    attention = 2 * rows * SLOT * D

    first, query, keys, values, mixed, stat = call(
        attend_kernel, count,
        [rows_of(D), rows_of(1), whole(2, D), vec, vec, weight, weight, weight, vec, vec, whole(GROUP, 256)],
        [mols_of(D, SLOT), rows_of(D), rows_of(D), rows_of(D), mols_of(D, SLOT), mols_of(2, GROUP, SLOT)],
        [shape_of(count, D, SLOT, dtype=BF16)] + [shape_of(rows, D, dtype=BF16)] * 3
        + [shape_of(count, D, SLOT, dtype=BF16), shape_of(count, 2, GROUP, SLOT)],
        [pltpu.VMEM((H, 32, SLOT), BF16), pltpu.VMEM((4, SLOT, SLOT), F32), pltpu.VMEM((D, SLOT), F32)],
        (lengths, tokens, kinds, type_table, row(first_gain), row(first_shift), query_weight, key_weight,
         value_weight, row(query_bias), row(value_bias), lanes),
        flops=3 * unit + 20 * attention, name="attend",
    )
    layer_out, grad_middle, grad_mixed, outer_grad, inner_grad, output_grad, dense_vectors = call(
        functools.partial(dense_kernel, factor), count,
        [rows_of(D), rows_of(1), whole(2, D), mols_of(D, SLOT), rows_of(D), weight, weight, weight,
         vec, vec, vec, vec, vec],
        [rows_of(D), rows_of(D), rows_of(D), weight, weight, weight, whole(8, D)],
        [shape_of(rows, D, dtype=BF16), shape_of(rows, D), shape_of(rows, D, dtype=BF16)]
        + [shape_of(D, D)] * 3 + [shape_of(8, D)],
        [],
        (lengths, tokens, kinds, type_table, mixed, cotangent, output_weight, inner_weight, outer_weight,
         row(output_bias), row(inner_bias), row(outer_bias), row(second_gain), row(second_shift)),
        flops=9 * unit, name="dense",
    )
    outer_grad, inner_grad, output_grad, dense_vectors = lax.psum(
        (outer_grad, inner_grad, output_grad, dense_vectors), AXES
    )
    grads, vectors, placed = [], [], None
    for part in range(2):
        half = pl.BlockSpec((SLOT, HALF), lambda i, *_, part=part: (i, part))
        weight_grad, bias_grad, turned = call(
            functools.partial(back_kernel, factor), count,
            [mols_of(D, SLOT), half, half, half, half,
             pl.BlockSpec((1, 1, GROUP, SLOT), lambda i, *_, part=part: (i, part, 0, 0)), whole(GROUP, 256)],
            [whole(D, 3 * HALF), whole(8, 3 * HALF), mols_of(3, HALF, SLOT)],
            [shape_of(D, 3 * HALF), shape_of(8, 3 * HALF), shape_of(count, 3, HALF, SLOT, dtype=BF16)],
            [pltpu.VMEM((GROUP, 32, SLOT), BF16)] * 3 + [pltpu.VMEM((3, SLOT, SLOT), F32)] * 2
            + [pltpu.VMEM((3, HALF, SLOT), F32)],
            (lengths, first, query, keys, values, grad_mixed, stat, lanes),
            flops=2 * unit + 20 * attention, name="back",
        )
        own, other = spread_sum(weight_grad, bits, me, devices)
        placed = put_in_place(place, own, other, placed, part)
        grads.append(turned)
        vectors.append(bias_grad)
    tokens_grad, input_vectors = call(
        lambda lengths_ref, *refs: input_kernel(factor, *refs), count,
        [rows_of(D), rows_of(1), whole(2, D), vec, mols_of(3, HALF, SLOT), mols_of(3, HALF, SLOT), weight, weight,
         weight, rows_of(D)],
        [rows_of(D), whole(8, D)],
        [shape_of(rows, D, dtype=BF16), shape_of(8, D)],
        [],
        (lengths, tokens, kinds, type_table, row(first_gain), grads[0], grads[1], query_weight, key_weight,
         value_weight, grad_middle),
        flops=3 * unit, name="input",
    )
    query_bias_grad, value_bias_grad = (
        jnp.concatenate([v[0, i * HALF : (i + 1) * HALF] for v in vectors]) for i in (0, 2)
    )
    small = small_sum(
        jnp.concatenate([input_vectors[:4], query_bias_grad[None], value_bias_grad[None], input_vectors[6:]]), devices
    )
    query_grad, key_grad, value_grad = (grad.reshape(D, D) for grad in placed)
    return (
        layer_out,
        tokens_grad,
        query_grad,
        key_grad,
        value_grad,
        output_grad,
        inner_grad,
        outer_grad,
        small[4],
        small[5],
        dense_vectors[4],
        dense_vectors[1],
        dense_vectors[0],
        small[0],
        small[1],
        dense_vectors[2],
        dense_vectors[3],
        small[2:4],
    )


def solution(mesh):
    split = P(AXES, None)
    return jax.shard_map(
        functools.partial(per_device, dict(mesh.shape)),
        mesh=mesh,
        in_specs=(split, P(AXES), P(AXES)) + (P(),) * 16 + (split,),
        out_specs=(split, split) + (P(),) * 16,
        check_vma=False,
    )
```

```python
import functools
import math

import jax
import jax.numpy as jnp
import numpy as np
from jax import lax
from jax.experimental import pallas as pl
from jax.experimental.pallas import tpu as pltpu
from jax.sharding import PartitionSpec as P

D = 768
H = 32
DH = 24
SLOT = 208
GROUP = 16
HALF = GROUP * DH
WIDE = 256
SCALE = 1.0 / math.sqrt(DH)
LOG_SCALE = math.log2(math.e) / math.sqrt(DH)
LN_2 = math.log(2.0)
AXES = ("wide", "narrow")
NN = (((1,), (0,)), ((), ()))
NT = (((1,), (1,)), ((), ()))
TN = (((0,), (0,)), ((), ()))
F32 = jnp.float32
BF16 = jnp.bfloat16
ANY = pl.BlockSpec(memory_space=pl.ANY)


def dot(left, right, dims=NN):
    return lax.dot_general(left, right, dims, preferred_element_type=F32)


def norm_parts(values):
    average = jnp.mean(values, -1, keepdims=True)
    centered = values - average
    inv_std = lax.rsqrt(jnp.mean(centered * centered, -1, keepdims=True) + 1e-05)
    return centered * inv_std, inv_std


def norm_back(grad_hat, normed, inv_std):
    return (
        grad_hat
        - jnp.mean(grad_hat, -1, keepdims=True)
        - normed * jnp.mean(grad_hat * normed, -1, keepdims=True)
    ) * inv_std


def row_of(ref):
    return ref[...].astype(F32).reshape(1, D)


def kinds_column(kinds_ref, edge_ref):
    @pl.when(pl.program_id(0) == 0)
    def turn():
        kinds = kinds_ref[...].astype(F32).reshape(1, -1)
        edge_ref[...] = jnp.broadcast_to(kinds, (8, kinds.shape[1])).T[:, :1]


def embed(tokens, edge, table_ref):
    table = table_ref[...].astype(F32)
    return tokens.astype(F32) + jnp.where(edge == 1, table[1:2], table[0:1])


def turn(values):
    return jnp.concatenate([values, jnp.zeros((WIDE - SLOT, values.shape[1]), F32)]).T


def with_rows(values, rows):
    index = lax.broadcasted_iota(jnp.int32, (8, WIDE), 0)
    extra = jnp.zeros((8, WIDE), F32)
    for i, row in enumerate(rows):
        extra = jnp.where(index == i, row, extra)
    if values.ndim == 3:
        extra = jnp.broadcast_to(extra, (values.shape[0], 8, WIDE))
    return jnp.concatenate([values, extra], -2).astype(BF16)


def split_row(row):
    high = row.astype(BF16).astype(F32)
    mid = (row - high).astype(BF16).astype(F32)
    return [high, mid, row - high - mid]


def attend_kernel(
    lengths_ref, place_ref, tokens_ref, kinds_ref, table_ref, gain_ref, shift_ref, query_bias_ref, value_bias_ref,
    query_weight_ref, key_weight_ref, value_weight_ref,
    first_ref, query_ref, keys_ref, values_ref, mixed_ref, stat_ref,
    edge_ref, scores_ref, out_ref,
):
    mol = pl.program_id(0)
    kinds_column(kinds_ref, edge_ref)
    edge = edge_ref[pl.ds(pl.multiple_of(mol * SLOT, 8), SLOT), :]
    normed, unused = norm_parts(embed(tokens_ref[...], edge, table_ref))
    first32 = normed * row_of(gain_ref) + row_of(shift_ref)
    first = first32.astype(BF16)
    first_ref[0] = turn(first32).astype(BF16)
    slot = lax.broadcasted_iota(jnp.int32, (1, WIDE), 1)
    bias = jnp.where(slot < lengths_ref[mol], 0.0, -1e30)
    ones = jnp.ones((1, WIDE), F32)
    query = (dot(first, query_weight_ref[...]) + row_of(query_bias_ref)) * LOG_SCALE
    keys = dot(first, key_weight_ref[...])
    values = dot(first, value_weight_ref[...]) + row_of(value_bias_ref)
    query_ref[0] = with_rows(turn(query).reshape(H, DH, WIDE), [ones])
    keys_ref[0] = with_rows(turn(keys).reshape(H, DH, WIDE), [bias, ones, ones, ones])
    values_ref[0] = with_rows(turn(values).reshape(H, DH, WIDE), [ones, ones, ones])
    lag = 3

    def score(h):
        scores_ref[h % (lag + 1)] = dot(keys_ref[0, h, :, :SLOT], query_ref[0, h], TN)

    def mix(h):
        scores = scores_ref[h % (lag + 1)]
        top = jnp.max(scores, axis=0, keepdims=True)
        powered = jnp.exp2(scores - top).astype(BF16)
        out = dot(values_ref[0, h, :, :SLOT], powered)
        total = out[DH : DH + 1]
        out_ref[h * DH : (h + 1) * DH, :] = out[:DH] * (1.0 / total)
        stat_ref[0, h // GROUP, h % GROUP : h % GROUP + 1] = top + jnp.log2(total)

    for h in range(H + lag):
        if h < H:
            score(h)
        if h >= lag:
            mix(h - lag)
    mixed_ref[0] = out_ref[...].astype(BF16)


def gelu_parts(inner):
    root = math.sqrt(2.0 / math.pi)
    square = inner * inner
    bent = jnp.tanh(root * (inner + 0.044715 * inner * square))
    half = 0.5 * (1.0 + bent)
    slope = half + 0.5 * inner * (1.0 - bent * bent) * root * (1.0 + 3 * 0.044715 * square)
    return inner * half, slope


def dense_kernel(
    factor, lengths_ref, place_ref, tokens_ref, kinds_ref, table_ref, mixed_ref, cotangent_ref, output_bias_ref,
    inner_bias_ref, outer_bias_ref, gain_ref, shift_ref, output_weight_ref, inner_weight_ref, outer_weight_ref,
    layer_ref, grad_middle_ref, grad_mixed_ref, kept_ref, sent_ref, vectors_ref,
    edge_ref, weight_grad_ref,
):
    step = pl.program_id(0)
    mols = mixed_ref.shape[0]
    rows = mols * SLOT

    @pl.when(step == 0)
    def start_sums():
        weight_grad_ref[...] = jnp.zeros_like(weight_grad_ref)
        vectors_ref[...] = jnp.zeros_like(vectors_ref)

    kinds_column(kinds_ref, edge_ref)
    edge = edge_ref[pl.ds(pl.multiple_of(step * rows, 8), rows), :]
    slot = lax.broadcasted_iota(jnp.int32, (SLOT, 1), 0)
    valid = jnp.concatenate([(slot < lengths_ref[step * mols + i]).astype(F32) for i in range(mols)])
    gain = row_of(gain_ref)
    mixed = jnp.concatenate([dot(mixed_ref[i], output_weight_ref[...], TN)[:SLOT] for i in range(mols)])
    middle = embed(tokens_ref[...], edge, table_ref) + mixed + row_of(output_bias_ref)
    normed, inv_std = norm_parts(middle)
    second = (normed * gain + row_of(shift_ref)).astype(BF16)
    inner = dot(second, inner_weight_ref[...]) + row_of(inner_bias_ref)
    act32, slope = gelu_parts(inner)
    act = act32.astype(BF16)
    grad_out = cotangent_ref[...].astype(F32) * valid
    grad_low = grad_out.astype(BF16)
    weight_grad_ref[:, :D] += dot(act, grad_low, TN)
    grad_inner = (dot(grad_low, outer_weight_ref[...], NT) * slope).astype(BF16)
    weight_grad_ref[:, D : 2 * D] += dot(second, grad_inner, TN)
    layer = middle + dot(act, outer_weight_ref[...]) + row_of(outer_bias_ref)
    layer_ref[...] = (layer * valid).astype(BF16)
    grad_second = dot(grad_inner, inner_weight_ref[...], NT)
    grad_middle = grad_out + norm_back(grad_second * gain, normed, inv_std)
    grad_middle_ref[...] = grad_middle
    pad = jnp.zeros((WIDE - SLOT, D), F32)
    for i in range(mols):
        grad_attn = jnp.concatenate([grad_middle[i * SLOT : (i + 1) * SLOT], pad]).astype(BF16)
        weight_grad_ref[:, 2 * D :] += dot(mixed_ref[i], grad_attn)
        grad_mixed_ref[i] = dot(output_weight_ref[...], grad_attn, NT).astype(BF16)
    sums = [
        grad_out,
        grad_inner.astype(F32),
        grad_second * normed,
        grad_second,
        grad_middle.astype(BF16).astype(F32),
    ]
    for i, values in enumerate(sums):
        vectors_ref[i : i + 1] += jnp.sum(values, 0, keepdims=True)

    @pl.when(step == pl.num_programs(0) - 1)
    def scale_sums():
        part_by_core(weight_grad_ref, kept_ref, sent_ref, place_ref[0], factor)
        vectors_ref[...] = vectors_ref[...] * factor


def part_by_core(total_ref, kept_ref, sent_ref, core, factor):
    rows = total_ref.shape[0] // 4
    for half in range(2):
        for target, which in ((kept_ref, core), (sent_ref, 1 - core)):
            begin = pl.multiple_of((half * 2 + which) * rows, 8)
            target[half] = total_ref[pl.ds(begin, rows), :] * factor


def back_kernel(
    begin, last, factor, lengths_ref, place_ref, first_ref, query_ref, keys_ref, values_ref, mixed_ref, grad_ref,
    stat_ref, *refs,
):
    inputs = refs[:2] if begin else ()
    outputs, scratch = refs[len(inputs) : -6], refs[-6:]
    mixed32_ref, grad32_ref, scores_ref, probs_ref, grads_ref, total_ref = scratch
    vectors_ref, turned_grads_ref = outputs[:2]
    step = pl.program_id(0)

    @pl.when(step == 0)
    def start_sums():
        grads_ref[...] = jnp.zeros_like(grads_ref)
        if begin:
            total_ref[...] = inputs[0][...]
            vectors_ref[...] = inputs[1][...]
        else:
            total_ref[...] = jnp.zeros_like(total_ref)
            vectors_ref[...] = jnp.zeros_like(vectors_ref)

    mixed32_ref[...] = mixed_ref[0].astype(F32)
    grad32_ref[...] = grad_ref[0].astype(F32)
    lag = 2

    def score(h):
        rows = slice(h * DH, (h + 1) * DH)
        stat = split_row(-stat_ref[0, 0, h : h + 1])
        query = with_rows(query_ref[0, h, :DH].astype(F32), [1.0] + stat)
        scores_ref[h % (lag + 1)] = dot(keys_ref[0, h, :, :SLOT], query, TN)
        grad = grad32_ref[rows]
        shared = split_row(-jnp.sum(grad * mixed32_ref[rows], axis=0, keepdims=True))
        probs_ref[h % (lag + 1)] = dot(values_ref[0, h, :, :SLOT], with_rows(grad, shared), TN)

    def back(h):
        rows = slice(h * DH, (h + 1) * DH)
        probs = jnp.exp2(scores_ref[h % (lag + 1)])
        grad_scores = (probs * probs_ref[h % (lag + 1)]).astype(BF16)
        grad = with_rows(grad32_ref[rows], [])
        grads_ref[0, rows] = dot(keys_ref[0, h, :, :SLOT], grad_scores)[:DH] * SCALE
        grads_ref[1, rows, :SLOT] = dot(query_ref[0, h], grad_scores, NT)[:DH] * LN_2
        grads_ref[2, rows, :SLOT] = dot(grad, probs.astype(BF16), NT)[:DH]

    for h in range(GROUP + lag):
        if h < GROUP:
            score(h)
        if h >= lag:
            back(h - lag)
    ones = jnp.ones((8, WIDE), BF16)
    for i in range(3):
        grads = grads_ref[i].astype(BF16)
        turned_grads_ref[0, i] = grads
        columns = slice(i * HALF, (i + 1) * HALF)
        total_ref[:, columns] += dot(first_ref[0], grads, NT)
        vectors_ref[:, columns] += dot(ones, grads, NT)

    @pl.when(step == pl.num_programs(0) - 1)
    def finish():
        if last:
            part_by_core(total_ref, outputs[2], outputs[3], place_ref[0], factor)
            vectors_ref[...] = vectors_ref[...] * factor
        else:
            outputs[2][...] = total_ref[...]


def input_kernel(
    factor, lengths_ref, place_ref, tokens_ref, kinds_ref, table_ref, gain_ref, low_0_ref, low_1_ref, high_0_ref,
    high_1_ref, query_weight_ref, key_weight_ref, value_weight_ref, grad_middle_ref,
    tokens_grad_ref, vectors_ref,
    edge_ref,
):
    mol = pl.program_id(0)

    @pl.when(mol == 0)
    def start_sums():
        vectors_ref[...] = jnp.zeros_like(vectors_ref)

    kinds_column(kinds_ref, edge_ref)
    edge = edge_ref[pl.ds(pl.multiple_of(mol * SLOT, 8), SLOT), :]
    early = mol < pl.num_programs(0) // 2
    total = jnp.zeros((D, WIDE), F32)
    for i, weight_ref in enumerate((query_weight_ref, key_weight_ref, value_weight_ref)):
        low = jnp.where(early, low_0_ref[0, i], low_1_ref[0, i])
        high = jnp.where(early, high_0_ref[0, i], high_1_ref[0, i])
        total = total + dot(weight_ref[:, :HALF], low) + dot(weight_ref[:, HALF:], high)
    grad_first = total.T[:SLOT]
    normed, inv_std = norm_parts(embed(tokens_ref[...], edge, table_ref))
    grad_start = grad_middle_ref[...] + norm_back(grad_first * row_of(gain_ref), normed, inv_std)
    tokens_grad_ref[...] = grad_start.astype(BF16)
    sums = [
        grad_first * normed,
        grad_first,
        jnp.where(edge == 1, 0.0, grad_start),
        jnp.where(edge == 1, grad_start, 0.0),
    ]
    for i, values in enumerate(sums):
        vectors_ref[i : i + 1] += jnp.sum(values, 0, keepdims=True)

    @pl.when(mol == pl.num_programs(0) - 1)
    def scale_sums():
        vectors_ref[...] = vectors_ref[...] * factor


def whole(*shape):
    return pl.BlockSpec(shape, lambda i, *_: (0,) * len(shape))


def rows_of(width):
    return pl.BlockSpec((SLOT, width), lambda i, *_: (i, 0))


def mols_of(*shape):
    return pl.BlockSpec((1,) + shape, lambda i, *_: (i,) + (0,) * len(shape))


def shape_of(*shape, dtype=F32):
    return jax.ShapeDtypeStruct(shape, dtype)


def call(kernel, count, in_specs, out_specs, out_shape, scratch, args, flops, name, aliases=None):
    return pl.pallas_call(
        kernel,
        grid_spec=pltpu.PrefetchScalarGridSpec(
            num_scalar_prefetch=2,
            grid=(count,),
            in_specs=in_specs,
            out_specs=out_specs,
            scratch_shapes=scratch,
        ),
        out_shape=out_shape,
        input_output_aliases=aliases or {},
        compiler_params=pltpu.CompilerParams(
            dimension_semantics=("arbitrary",), vmem_limit_bytes=52 * 2**20
        ),
        cost_estimate=pl.CostEstimate(flops=flops, bytes_accessed=2**20, transcendentals=0),
        name=name,
    )(*args)


def bits_of(mesh_shape):
    narrow = mesh_shape["narrow"].bit_length() - 1
    wide = mesh_shape["wide"].bit_length() - 1
    y = (wide - 1) // 2
    return {
        "c": [0],
        "x": list(range(1, narrow)),
        "y": list(range(narrow, narrow + y)),
        "z": list(range(narrow + y, narrow + wide)),
    }


def swap(values, bit, devices):
    return lax.ppermute(values, AXES, [(i, i ^ (1 << bit)) for i in range(devices)])


def pick(values, *index):
    for i in index:
        values = lax.dynamic_index_in_dim(values, i, 0, keepdims=False)
    return values


def place_kernel(place_ref, own_ref, other_ref, *refs):
    outs = refs[-3:]
    step = pl.program_id(0)
    second = jnp.where(step // 4 == 0, place_ref[2], place_ref[1])
    level = place_ref[3]
    from_other = lax.rem(step // 2, 2) == 1

    def move(source):
        for i in range(2):
            for j in range(2):
                a = lax.bitwise_xor(i, second)
                b = lax.bitwise_xor(j, level)
                for k, out in enumerate(outs):
                    width = out.shape[-1]
                    out[0, 0, 0, a, b] = source[0, 0, i, j, :, k * width : (k + 1) * width]

    @pl.when(jnp.logical_not(from_other))
    def own():
        move(own_ref)

    @pl.when(from_other)
    def other():
        move(other_ref)


def put_in_place(place, own, other, before, part):
    width = own.shape[-1]
    rows = own.shape[-2]

    def source(core):
        def index(step, place):
            half, mid, low = step // 4, lax.rem(step // 2, 2), lax.rem(step, 2)
            if core == 0:
                kept = jnp.where(mid == 0, low, 1)
            else:
                kept = jnp.where(mid == 1, low, 0)
            return (half, kept, 0, 0, 0, 0)

        return pl.BlockSpec((1, 1, 2, 2, rows, width), index)

    def target(step, place):
        half, mid, low = step // 4, lax.rem(step // 2, 2), lax.rem(step, 2)
        first = jnp.where(half == 0, place[1], place[2])
        return (half, lax.bitwise_xor(mid, place[0]), lax.bitwise_xor(low, first), 0, 0, 0, part)

    shape = (2, 2, 2, 2, 2, rows, D)
    aliases = {} if before is None else {3 + i: i for i in range(3)}
    extra = [] if before is None else list(before)
    return pl.pallas_call(
        place_kernel,
        grid_spec=pltpu.PrefetchScalarGridSpec(
            num_scalar_prefetch=1,
            grid=(8,),
            in_specs=[source(0), source(1)] + [ANY] * len(extra),
            out_specs=[pl.BlockSpec((1, 1, 1, 2, 2, rows, width // 3), target)] * 3,
        ),
        out_shape=[shape_of(*shape)] * 3,
        input_output_aliases=aliases,
        compiler_params=pltpu.CompilerParams(vmem_limit_bytes=40 * 2**20),
        name="place",
    )(place, own, other, *extra)


def spread_sum(kept, sent, bits, me, devices):
    shape = (2, 2, 2, 2, kept.shape[1] // 8, kept.shape[2])
    kept = kept.reshape(shape)
    core, x, y, z = (bits[k][0] for k in "cxyz")
    orders = ((x, y), (y, x))
    (got,) = yield [(sent.reshape(shape), core)]
    parts = [[kept[half], got[half]] for half in range(2)]
    for level in range(2):
        sent = [
            (functools.reduce(jnp.add, [pick(t, 1 - me[order[level]]) for t in terms]), order[level])
            for order, terms in zip(orders, parts)
        ]
        got = yield sent
        parts = [
            [pick(t, me[order[level]]) for t in terms] + [g] for order, terms, g in zip(orders, parts, got)
        ]
    sent = jnp.stack([functools.reduce(jnp.add, [pick(t, 1 - me[z]) for t in terms]) for terms in parts])
    (got,) = yield [(sent, z)]
    total = got + jnp.stack([functools.reduce(jnp.add, [pick(t, me[z]) for t in terms]) for terms in parts])
    for bit in bits["x"][1:] + bits["y"][1:] + bits["z"][1:]:
        (got,) = yield [(total, bit)]
        total = total + got
    (across,) = yield [(total, z)]
    held = [jnp.stack([total[half], across[half]]) for half in range(2)]
    for level in (1, 0):
        got = yield [(part, order[level]) for order, part in zip(orders, held)]
        held = [jnp.stack(pair) for pair in zip(held, got)]
    own = jnp.stack(held)
    (other,) = yield [(own, core)]
    yield own, other


class Order:
    def __init__(self):
        self.before = ()

    def after(self, *values):
        if self.before:
            values, unused = lax.optimization_barrier((values, self.before))
        return values

    def add(self, *values):
        self.before = tuple(values)


class Transfer:
    def __init__(self, steps, devices, order):
        self.steps = steps
        self.devices = devices
        self.order = order
        self.send(next(self.steps))

    def send(self, sent):
        self.order.add(*self.order.before, *[v for v, unused in sent])
        self.got = [swap(v, bit, self.devices) for v, bit in sent]

    def go(self):
        sent = self.steps.send(self.order.after(*self.got))
        if isinstance(sent, tuple):
            self.result = sent
        else:
            self.order.before = ()
            self.send(sent)


def small_sum(values, devices):
    bit = 0
    while 1 << bit < devices:
        (got,) = yield [(values, bit)]
        values = values + got
        bit += 1
    yield (values,)


def per_device(
    mesh_shape, tokens, kinds, lengths, query_weight, key_weight, value_weight, output_weight, inner_weight,
    outer_weight, query_bias, value_bias, output_bias, inner_bias, outer_bias, first_gain, first_shift,
    second_gain, second_shift, type_table, cotangent,
):
    count = lengths.shape[0]
    rows = tokens.shape[0]
    devices = mesh_shape["wide"] * mesh_shape["narrow"]
    factor = 1.0 / devices
    bits = bits_of(mesh_shape)
    index = lax.axis_index("wide") * mesh_shape["narrow"] + lax.axis_index("narrow")
    me = [(index >> bit) & 1 for bit in range(devices.bit_length() - 1)]
    place = jnp.stack([me[bits[k][0]] for k in "cxyz"]).astype(jnp.int32)
    unit = 2 * rows * D * D
    attention = 2 * rows * SLOT * D
    vec = pl.BlockSpec((D,), lambda i, *_: (0,))
    weight = whole(D, D)
    edges = pl.BlockSpec((rows,), lambda i, *_: (0,))
    column = pltpu.VMEM((rows, 1), F32)
    scalars = (lengths, place)
    first, query, keys, values, mixed, stat = call(
        attend_kernel, count,
        [rows_of(D), edges, whole(2, D), vec, vec, vec, vec, weight, weight, weight],
        [mols_of(D, WIDE)] + [mols_of(H, 32, WIDE)] * 3 + [mols_of(D, WIDE), mols_of(2, GROUP, WIDE)],
        [shape_of(count, D, WIDE, dtype=BF16)] + [shape_of(count, H, 32, WIDE, dtype=BF16)] * 3
        + [shape_of(count, D, WIDE, dtype=BF16), shape_of(count, 2, GROUP, WIDE)],
        [column, pltpu.VMEM((4, SLOT, WIDE), F32), pltpu.VMEM((D, WIDE), F32)],
        (*scalars, tokens, kinds, type_table, first_gain, first_shift, query_bias, value_bias, query_weight,
         key_weight, value_weight),
        flops=3 * unit + 20 * attention, name="attend",
    )
    mols = 2
    tall = lambda width: pl.BlockSpec((mols * SLOT, width), lambda i, *_: (i, 0))
    several = pl.BlockSpec((mols, D, WIDE), lambda i, *_: (i, 0, 0))
    split_shape = lambda width: shape_of(2, D // 4, width)
    layer_out, grad_middle, grad_mixed, kept, sent, dense_vectors = call(
        functools.partial(dense_kernel, factor), count // mols,
        [tall(D), edges, whole(2, D), several, tall(D), vec, vec, vec, vec, vec, weight, weight, weight],
        [tall(D), tall(D), several, whole(2, D // 4, 3 * D), whole(2, D // 4, 3 * D), whole(8, D)],
        [shape_of(rows, D, dtype=BF16), shape_of(rows, D), shape_of(count, D, WIDE, dtype=BF16),
         split_shape(3 * D), split_shape(3 * D), shape_of(8, D)],
        [column, pltpu.VMEM((D, 3 * D), F32)],
        (*scalars, tokens, kinds, type_table, mixed, cotangent, output_bias, inner_bias, outer_bias, second_gain,
         second_shift, output_weight, inner_weight, outer_weight),
        flops=9 * unit, name="dense",
    )
    order = Order()
    spread = lambda kept, sent: Transfer(spread_sum(kept, sent, bits, me, devices), devices, order)
    dense_sum = spread(kept, sent)
    sums, turned, vectors = [], [], []
    piece = count // 2
    wide = 3 * HALF
    for part in range(2):
        total = None
        for begin in (0, piece):
            heads = pl.BlockSpec((1, GROUP, 32, WIDE), lambda i, *_, part=part, begin=begin: (i + begin, part, 0, 0))
            half = pl.BlockSpec((1, HALF, WIDE), lambda i, *_, part=part, begin=begin: (i + begin, part, 0))
            acc = [] if begin == 0 else [total, bias_grad]
            (grad_in,) = order.after(grad_mixed)
            halves = [whole(2, D // 4, wide)] * 2 if begin else [whole(D, wide)]
            bias_grad, turned_grads, *totals = call(
                functools.partial(back_kernel, begin, begin > 0, factor), piece,
                [pl.BlockSpec((1, D, WIDE), lambda i, *_, begin=begin: (i + begin, 0, 0)), heads, heads, heads, half,
                 half, pl.BlockSpec((1, 1, GROUP, WIDE), lambda i, *_, part=part, begin=begin: (i + begin, part, 0, 0))]
                + [whole(*a.shape) for a in acc],
                [whole(8, wide), mols_of(3, HALF, WIDE)] + halves,
                [shape_of(8, wide), shape_of(piece, 3, HALF, WIDE, dtype=BF16)]
                + ([split_shape(wide)] * 2 if begin else [shape_of(D, wide)]),
                [pltpu.VMEM((HALF, WIDE), F32)] * 2 + [pltpu.VMEM((3, SLOT, WIDE), F32)] * 2
                + [pltpu.VMEM((3, HALF, WIDE), F32), pltpu.VMEM((D, wide), F32)],
                (*scalars, first, query, keys, values, mixed, grad_in, stat, *acc),
                flops=unit + 10 * attention, name=f"back_{part}_{begin}",
            )
            total = totals[0]
            turned.append(turned_grads)
            order.add(bias_grad)
            for transfer in [dense_sum] + sums:
                transfer.go()
        sums.append(spread(*totals))
        vectors.append(bias_grad)
    query_bias_grad, value_bias_grad = (
        jnp.concatenate([v[0, i * HALF : (i + 1) * HALF] for v in vectors]) for i in (0, 2)
    )
    low_sum, high_sum = sums
    low_sum.go()
    high_sum.go()
    (grad_middle,) = order.after(grad_middle)
    pieces = [pl.BlockSpec((1, 3, HALF, WIDE), index) for index in (
        lambda i, *_: (jnp.minimum(i, piece - 1), 0, 0, 0), lambda i, *_: (jnp.maximum(i - piece, 0), 0, 0, 0))]
    tokens_grad, input_vectors = call(
        functools.partial(input_kernel, factor), count,
        [rows_of(D), edges, whole(2, D), vec] + pieces * 2 + [weight, weight, weight, rows_of(D)],
        [rows_of(D), whole(8, D)],
        [shape_of(rows, D, dtype=BF16), shape_of(8, D)],
        [column],
        (*scalars, tokens, kinds, type_table, first_gain, *turned, query_weight, key_weight, value_weight, grad_middle),
        flops=3 * unit, name="input",
    )
    order.add(input_vectors)
    small = jnp.concatenate(
        [input_vectors[:4], query_bias_grad[None], value_bias_grad[None], input_vectors[6:], dense_vectors]
    )
    small_values = Transfer(small_sum(small, devices), devices, order)
    steps = (
        (dense_sum, low_sum, high_sum, small_values, low_sum, high_sum, dense_sum, small_values, high_sum, low_sum)
        + (low_sum, high_sum, dense_sum, small_values, high_sum, dense_sum, small_values, low_sum, high_sum)
        + (small_values, high_sum, low_sum, dense_sum)
    )
    for transfer in steps:
        transfer.go()
    for transfer in (low_sum, high_sum, dense_sum, small_values):
        while not hasattr(transfer, "result"):
            transfer.go()
    placed = put_in_place(place, *low_sum.result, None, 0)
    outer_grad, inner_grad, output_grad = put_in_place(place, *dense_sum.result, None, 0)
    query_grad, key_grad, value_grad = put_in_place(place, *high_sum.result, placed, 1)
    (small,) = small_values.result
    return tuple(
        [layer_out, tokens_grad]
        + [grad.reshape(D, D) for grad in (query_grad, key_grad, value_grad, output_grad, inner_grad, outer_grad)]
        + [small[i] for i in (4, 5, 12, 9, 8, 0, 1, 10, 11)]
        + [small[2:4]]
    )


def solution(mesh):
    split = P(AXES, None)
    return jax.shard_map(
        functools.partial(per_device, dict(mesh.shape)),
        mesh=mesh,
        in_specs=(split, P(AXES), P(AXES)) + (P(),) * 16 + (split,),
        out_specs=(split, split) + (P(),) * 16,
        check_vma=False,
    )
```

```python
import functools
import math

import jax
import jax.numpy as jnp
import numpy as np
from jax import lax
from jax.experimental import pallas as pl
from jax.experimental.pallas import tpu as pltpu
from jax.sharding import PartitionSpec as P

D = 768
H = 32
DH = 24
SLOT = 208
GROUP = 16
HALF = GROUP * DH
WIDE = 256
SCALE = 1.0 / math.sqrt(DH)
LOG_SCALE = math.log2(math.e) / math.sqrt(DH)
LN_2 = math.log(2.0)
AXES = ("wide", "narrow")
NN = (((1,), (0,)), ((), ()))
NT = (((1,), (1,)), ((), ()))
TN = (((0,), (0,)), ((), ()))
F32 = jnp.float32
BF16 = jnp.bfloat16
VMEM = 60 * 2**20
ANY = pl.BlockSpec(memory_space=pl.ANY)


SCHEDULE = "FwDA0Ax1yAOzBACOIABOCBAOCBAOCBOCBOCABOCAaBOoCBbCc"


def dot(left, right, dims=NN):
    return lax.dot_general(left, right, dims, preferred_element_type=F32)


def norm_parts(values):
    average = jnp.mean(values, -1, keepdims=True)
    centered = values - average
    inv_std = lax.rsqrt(jnp.mean(centered * centered, -1, keepdims=True) + 1e-05)
    return centered * inv_std, inv_std


def norm_back(grad_hat, normed, inv_std):
    return (
        grad_hat
        - jnp.mean(grad_hat, -1, keepdims=True)
        - normed * jnp.mean(grad_hat * normed, -1, keepdims=True)
    ) * inv_std


def row_of(ref):
    return ref[...].astype(F32).reshape(1, D)


def kinds_column(kinds_ref, edge_ref):
    @pl.when(pl.program_id(0) == 0)
    def turn():
        kinds = kinds_ref[...].astype(F32).reshape(1, -1)
        edge_ref[...] = jnp.broadcast_to(kinds, (8, kinds.shape[1])).T[:, :1]


def embed(tokens, edge, table_ref):
    table = table_ref[...].astype(F32)
    return tokens.astype(F32) + jnp.where(edge == 1, table[1:2], table[0:1])


def turn(values):
    return jnp.concatenate([values, jnp.zeros((WIDE - SLOT, values.shape[1]), F32)]).T


def with_rows(values, rows):
    index = lax.broadcasted_iota(jnp.int32, (8, WIDE), 0)
    extra = jnp.zeros((8, WIDE), F32)
    for i, row in enumerate(rows):
        extra = jnp.where(index == i, row, extra)
    if values.ndim == 3:
        extra = jnp.broadcast_to(extra, (values.shape[0], 8, WIDE))
    return jnp.concatenate([values, extra], -2).astype(BF16)


def split_row(row):
    high = row.astype(BF16).astype(F32)
    mid = (row - high).astype(BF16).astype(F32)
    return [high, mid, row - high - mid]


def attend_kernel(
    lengths_ref, place_ref, tokens_ref, kinds_ref, table_ref, gain_ref, shift_ref, query_bias_ref, value_bias_ref,
    query_weight_ref, key_weight_ref, value_weight_ref,
    first_ref, query_ref, keys_ref, values_ref, mixed_ref, stat_ref,
    edge_ref, scores_ref, out_ref,
):
    mol = pl.program_id(0)
    kinds_column(kinds_ref, edge_ref)
    edge = edge_ref[pl.ds(pl.multiple_of(mol * SLOT, 8), SLOT), :]
    normed, unused = norm_parts(embed(tokens_ref[...], edge, table_ref))
    first32 = normed * row_of(gain_ref) + row_of(shift_ref)
    first = first32.astype(BF16)
    first_ref[0] = turn(first32).astype(BF16)
    slot = lax.broadcasted_iota(jnp.int32, (1, WIDE), 1)
    bias = jnp.where(slot < lengths_ref[mol], 0.0, -1e30)
    ones = jnp.ones((1, WIDE), F32)
    query = (dot(first, query_weight_ref[...]) + row_of(query_bias_ref)) * LOG_SCALE
    keys = dot(first, key_weight_ref[...])
    values = dot(first, value_weight_ref[...]) + row_of(value_bias_ref)
    query_ref[0] = with_rows(turn(query).reshape(H, DH, WIDE), [ones])
    keys_ref[0] = with_rows(turn(keys).reshape(H, DH, WIDE), [bias, ones, ones, ones])
    values_ref[0] = with_rows(turn(values).reshape(H, DH, WIDE), [ones, ones, ones])
    lag = 3

    def score(h):
        scores_ref[h % (lag + 1)] = dot(keys_ref[0, h, :, :SLOT], query_ref[0, h], TN)

    def mix(h):
        scores = scores_ref[h % (lag + 1)]
        top = jnp.max(scores, axis=0, keepdims=True)
        powered = jnp.exp2(scores - top).astype(BF16)
        out = dot(values_ref[0, h, :, :SLOT], powered)
        total = out[DH : DH + 1]
        out_ref[h * DH : (h + 1) * DH, :] = out[:DH] * (1.0 / total)
        stat_ref[0, h // GROUP, h % GROUP : h % GROUP + 1] = top + jnp.log2(total)

    for h in range(H + lag):
        if h < H:
            score(h)
        if h >= lag:
            mix(h - lag)
    mixed_ref[0] = out_ref[...].astype(BF16)


def gelu_parts(inner):
    root = math.sqrt(2.0 / math.pi)
    square = inner * inner
    bent = jnp.tanh(root * (inner + 0.044715 * inner * square))
    half = 0.5 * (1.0 + bent)
    slope = half + 0.5 * inner * (1.0 - bent * bent) * root * (1.0 + 3 * 0.044715 * square)
    return inner * half, slope


def valid_rows(lengths_ref, first, mols):
    slot = lax.broadcasted_iota(jnp.int32, (SLOT, 1), 0)
    return jnp.concatenate([(slot < lengths_ref[first + i]).astype(F32) for i in range(mols)])


def forward_kernel(
    factor, lengths_ref, place_ref, tokens_ref, kinds_ref, table_ref, mixed_ref, cotangent_ref, output_bias_ref,
    inner_bias_ref, gain_ref, shift_ref, output_weight_ref, inner_weight_ref, outer_weight_ref,
    middle_ref, act_ref, grad_inner_ref, kept_ref, sent_ref,
    edge_ref, total_ref,
):
    step = pl.program_id(0)
    mols = mixed_ref.shape[0]
    rows = mols * SLOT
    kinds_column(kinds_ref, edge_ref)
    edge = edge_ref[pl.ds(pl.multiple_of(step * rows, 8), rows), :]
    valid = valid_rows(lengths_ref, step * mols, mols)
    mixed = jnp.concatenate([dot(mixed_ref[i], output_weight_ref[...], TN)[:SLOT] for i in range(mols)])
    middle = embed(tokens_ref[...], edge, table_ref) + mixed + row_of(output_bias_ref)
    middle_ref[...] = middle
    normed, unused = norm_parts(middle)
    second = (normed * row_of(gain_ref) + row_of(shift_ref)).astype(BF16)
    inner = dot(second, inner_weight_ref[...]) + row_of(inner_bias_ref)
    act32, slope = gelu_parts(inner)
    act = act32.astype(BF16)
    act_ref[...] = act
    grad_low = (cotangent_ref[...].astype(F32) * valid).astype(BF16)
    grad_inner = (dot(grad_low, outer_weight_ref[...], NT) * slope).astype(BF16)
    grad_inner_ref[...] = grad_inner

    @pl.when(step == 0)
    def first():
        total_ref[:, :D] = dot(act, grad_low, TN)
        total_ref[:, D:] = dot(second, grad_inner, TN)

    @pl.when(step > 0)
    def later():
        total_ref[:, :D] += dot(act, grad_low, TN)
        total_ref[:, D:] += dot(second, grad_inner, TN)

    @pl.when(step == pl.num_programs(0) - 1)
    def finish():
        part_by_core(total_ref, kept_ref, sent_ref, place_ref[0], factor)


def backward_kernel(
    factor, lengths_ref, place_ref, middle_ref, act_ref, grad_inner_ref, mixed_ref, cotangent_ref, outer_bias_ref,
    gain_ref, output_weight_ref, inner_weight_ref, outer_weight_ref,
    layer_ref, grad_middle_ref, grad_mixed_ref, kept_ref, sent_ref, vectors_ref,
    total_ref,
):
    step = pl.program_id(0)
    mols = mixed_ref.shape[0]

    @pl.when(step == 0)
    def start_sums():
        total_ref[...] = jnp.zeros_like(total_ref)
        vectors_ref[...] = jnp.zeros_like(vectors_ref)

    valid = valid_rows(lengths_ref, step * mols, mols)
    middle = middle_ref[...]
    normed, inv_std = norm_parts(middle)
    grad_out = cotangent_ref[...].astype(F32) * valid
    grad_inner = grad_inner_ref[...]
    grad_second = dot(grad_inner, inner_weight_ref[...], NT)
    grad_middle = grad_out + norm_back(grad_second * row_of(gain_ref), normed, inv_std)
    grad_middle_ref[...] = grad_middle
    pad = jnp.zeros((WIDE - SLOT, D), F32)
    for i in range(mols):
        grad_attn = jnp.concatenate([grad_middle[i * SLOT : (i + 1) * SLOT], pad]).astype(BF16)
        total_ref[...] += dot(mixed_ref[i], grad_attn)
        grad_mixed_ref[i] = dot(output_weight_ref[...], grad_attn, NT).astype(BF16)
    layer = middle + dot(act_ref[...], outer_weight_ref[...]) + row_of(outer_bias_ref)
    layer_ref[...] = (layer * valid).astype(BF16)
    sums = [
        grad_out,
        grad_inner.astype(F32),
        grad_second * normed,
        grad_second,
        grad_middle.astype(BF16).astype(F32),
    ]
    for i, values in enumerate(sums):
        vectors_ref[i : i + 1] += jnp.sum(values, 0, keepdims=True)

    @pl.when(step == pl.num_programs(0) - 1)
    def finish():
        part_by_core(total_ref, kept_ref, sent_ref, place_ref[0], factor)
        vectors_ref[...] = vectors_ref[...] * factor


def part_by_core(total_ref, kept_ref, sent_ref, core, factor):
    rows = total_ref.shape[0] // 2
    for target, which in ((kept_ref, core), (sent_ref, 1 - core)):
        target[...] = total_ref[pl.ds(pl.multiple_of(which * rows, 8), rows), :] * factor


def back_kernel(
    factor, lengths_ref, place_ref, first_ref, query_ref, keys_ref, values_ref, mixed_ref, grad_ref, stat_ref,
    vectors_ref, turned_grads_ref, kept_ref, sent_ref,
    mixed32_ref, grad32_ref, scores_ref, probs_ref, grads_ref, total_ref,
):
    step = pl.program_id(0)

    @pl.when(step == 0)
    def start_sums():
        grads_ref[...] = jnp.zeros_like(grads_ref)
        total_ref[...] = jnp.zeros_like(total_ref)
        vectors_ref[...] = jnp.zeros_like(vectors_ref)

    mixed32_ref[...] = mixed_ref[0].astype(F32)
    grad32_ref[...] = grad_ref[0].astype(F32)
    lag = 2

    def score(h):
        rows = slice(h * DH, (h + 1) * DH)
        stat = split_row(-stat_ref[0, 0, h : h + 1])
        query = with_rows(query_ref[0, h, :DH].astype(F32), [1.0] + stat)
        scores_ref[h % (lag + 1)] = dot(keys_ref[0, h, :, :SLOT], query, TN)
        grad = grad32_ref[rows]
        shared = split_row(-jnp.sum(grad * mixed32_ref[rows], axis=0, keepdims=True))
        probs_ref[h % (lag + 1)] = dot(values_ref[0, h, :, :SLOT], with_rows(grad, shared), TN)

    def back(h):
        rows = slice(h * DH, (h + 1) * DH)
        probs = jnp.exp2(scores_ref[h % (lag + 1)])
        grad_scores = (probs * probs_ref[h % (lag + 1)]).astype(BF16)
        grad = with_rows(grad32_ref[rows], [])
        grads_ref[0, rows] = dot(keys_ref[0, h, :, :SLOT], grad_scores)[:DH] * SCALE
        grads_ref[1, rows, :SLOT] = dot(query_ref[0, h], grad_scores, NT)[:DH] * LN_2
        grads_ref[2, rows, :SLOT] = dot(grad, probs.astype(BF16), NT)[:DH]

    for h in range(GROUP + lag):
        if h < GROUP:
            score(h)
        if h >= lag:
            back(h - lag)
    ones = jnp.ones((8, WIDE), BF16)
    for i in range(3):
        grads = grads_ref[i].astype(BF16)
        turned_grads_ref[0, i] = grads
        columns = slice(i * HALF, (i + 1) * HALF)
        total_ref[:, columns] += dot(first_ref[0], grads, NT)
        vectors_ref[:, columns] += dot(ones, grads, NT)

    @pl.when(step == pl.num_programs(0) - 1)
    def finish():
        part_by_core(total_ref, kept_ref, sent_ref, place_ref[0], factor)
        vectors_ref[...] = vectors_ref[...] * factor


def input_kernel(
    factor, lengths_ref, place_ref, tokens_ref, kinds_ref, table_ref, gain_ref, low_ref, high_ref, query_weight_ref,
    key_weight_ref, value_weight_ref, grad_middle_ref, dense_ref, low_bias_ref, high_bias_ref,
    tokens_grad_ref, vectors_ref,
    edge_ref,
):
    mol = pl.program_id(0)

    @pl.when(mol == 0)
    def start_sums():
        vectors_ref[...] = jnp.zeros_like(vectors_ref)

    kinds_column(kinds_ref, edge_ref)
    edge = edge_ref[pl.ds(pl.multiple_of(mol * SLOT, 8), SLOT), :]
    total = jnp.zeros((D, WIDE), F32)
    for i, weight_ref in enumerate((query_weight_ref, key_weight_ref, value_weight_ref)):
        total = total + dot(weight_ref[:, :HALF], low_ref[0, i]) + dot(weight_ref[:, HALF:], high_ref[0, i])
    grad_first = total.T[:SLOT]
    normed, inv_std = norm_parts(embed(tokens_ref[...], edge, table_ref))
    grad_start = grad_middle_ref[...] + norm_back(grad_first * row_of(gain_ref), normed, inv_std)
    tokens_grad_ref[...] = grad_start.astype(BF16)
    sums = [
        grad_first * normed,
        grad_first,
        jnp.where(edge == 1, 0.0, grad_start),
        jnp.where(edge == 1, grad_start, 0.0),
    ]
    for i, values in enumerate(sums):
        vectors_ref[i : i + 1] += jnp.sum(values, 0, keepdims=True)

    @pl.when(mol == pl.num_programs(0) - 1)
    def finish():
        vectors_ref[...] = vectors_ref[...] * factor
        for i, begin in ((0, 0), (1, 2 * HALF)):
            vectors_ref[4 + i : 5 + i, :HALF] = low_bias_ref[:1, begin : begin + HALF]
            vectors_ref[4 + i : 5 + i, HALF:] = high_bias_ref[:1, begin : begin + HALF]
        vectors_ref[8:16] = dense_ref[...]


def whole(*shape):
    return pl.BlockSpec(shape, lambda i, *_: (0,) * len(shape))


def rows_of(width):
    return pl.BlockSpec((SLOT, width), lambda i, *_: (i, 0))


def mols_of(*shape):
    return pl.BlockSpec((1,) + shape, lambda i, *_: (i,) + (0,) * len(shape))


def shape_of(*shape, dtype=F32):
    return jax.ShapeDtypeStruct(shape, dtype)


def call(kernel, count, in_specs, out_specs, out_shape, scratch, args, flops, name, aliases=None):
    return pl.pallas_call(
        kernel,
        grid_spec=pltpu.PrefetchScalarGridSpec(
            num_scalar_prefetch=2,
            grid=(count,),
            in_specs=in_specs,
            out_specs=out_specs,
            scratch_shapes=scratch,
        ),
        out_shape=out_shape,
        input_output_aliases=aliases or {},
        compiler_params=pltpu.CompilerParams(
            dimension_semantics=("arbitrary",), vmem_limit_bytes=VMEM
        ),
        cost_estimate=pl.CostEstimate(flops=20 * flops, bytes_accessed=2**20, transcendentals=0),
        name=name,
    )(*args)


def bits_of(mesh_shape):
    narrow = mesh_shape["narrow"].bit_length() - 1
    wide = mesh_shape["wide"].bit_length() - 1
    y = (wide - 1) // 2
    return {
        "c": [0],
        "x": list(range(1, narrow)),
        "y": list(range(narrow, narrow + y)),
        "z": list(range(narrow + y, narrow + wide)),
    }


def swap(values, bit, devices):
    even, odd = bit if isinstance(bit, tuple) else (bit, bit)
    return lax.ppermute(values, AXES, [(i, i ^ (1 << (odd if i & 1 else even))) for i in range(devices)])


def pick(values, *index):
    for i in index:
        values = lax.dynamic_index_in_dim(values, i, 0, keepdims=False)
    return values


def place_kernel(count_in, matrices, part, place_ref, *refs):
    sources = refs[:4]
    outs = refs[4 + count_in : 4 + count_in + matrices]
    stage, in_sems, out_sems = refs[4 + count_in + matrices :]
    width = stage.shape[2] // matrices
    fetches = []
    for k in range(16):
        source = sources[k // 4]
        fetches.append(
            pltpu.make_async_copy(source.at[k // 2 % 2, k % 2], stage.at[k], in_sems.at[k])
        )
        fetches[-1].start()
    stores = []
    for k in range(16):
        core = place_ref[0] if k < 8 else 1 - place_ref[0]
        first, second = (place_ref[1], place_ref[2]) if k < 8 else (place_ref[2], place_ref[1])
        row = [core] + [
            lax.bitwise_xor(k // step % 2, bit) for step, bit in ((4, first), (2, second), (1, place_ref[3]))
        ]
        fetches[k].wait()
        for m in range(matrices):
            stores.append(
                pltpu.make_async_copy(
                    stage.at[k, :, m * width : (m + 1) * width],
                    outs[m].at[*row, :, part * width : (part + 1) * width],
                    out_sems.at[k, m],
                )
            )
            stores[-1].start()
    for store in stores:
        store.wait()


def put_in_place(place, pieces, matrices, before=None, part=0):
    rows, width = pieces[0].shape[-2:]
    extra = [] if before is None else list(before)
    return pl.pallas_call(
        functools.partial(place_kernel, len(extra), matrices, part),
        grid_spec=pltpu.PrefetchScalarGridSpec(
            num_scalar_prefetch=1,
            grid=(1,),
            in_specs=[ANY] * (4 + len(extra)),
            out_specs=[ANY] * matrices,
            scratch_shapes=[
                pltpu.VMEM((16, rows, width), F32),
                pltpu.SemaphoreType.DMA((16,)),
                pltpu.SemaphoreType.DMA((16, matrices)),
            ],
        ),
        out_shape=[shape_of(2, 2, 2, 2, rows, D)] * matrices,
        input_output_aliases={5 + i: i for i in range(len(extra))},
        compiler_params=pltpu.CompilerParams(vmem_limit_bytes=VMEM),
        name="place",
    )(place, *pieces, *extra)


def spread_sum(kept, sent, rider, bits, me, devices):
    rows, width = kept.shape[0] // 8, kept.shape[1]
    core, x, y, z = (bits[k][0] for k in "cxyz")
    (got,) = yield [(sent, core)]
    terms = [v.reshape(2, 2, 2, rows, width) for v in (kept, got)]
    scatter = (((x, y), me[1]), ((y, x), me[2]), (z, me[3]))
    for bit, mine in scatter:
        (got,) = yield [(functools.reduce(jnp.add, [pick(t, 1 - mine) for t in terms]), bit)]
        terms = [pick(t, mine) for t in terms] + [got]
    total = functools.reduce(jnp.add, terms)
    small = rider()

    def with_small(values):
        return values if small is None else jnp.concatenate([values.reshape(-1, width), small])

    def apart(values, shape):
        if small is None:
            return values, None
        count = math.prod(shape[:-1])
        return values[:count].reshape(shape), small + values[count:]

    for bit in bits["x"][1:] + bits["y"][1:] + bits["z"][1:]:
        (got,) = yield [(with_small(total), bit)]
        got, small = apart(got, total.shape)
        total = total + got
    (got,) = yield [(with_small(total), z)]
    got, small = apart(got, total.shape)
    total = jnp.stack([total, got])
    (got,) = yield [(with_small(total), (y, x))]
    got, small = apart(got, total.shape)
    total = jnp.stack([total, got])
    got, other = yield [(with_small(total), (x, y)), (total, core)]
    got, small = apart(got, total.shape)
    (last,) = yield [(with_small(got), core)]
    last, small = apart(last, got.shape)
    yield (total, got, other, last), small


class Order:
    def __init__(self):
        self.before = ()

    def after(self, *values):
        if self.before:
            values, unused = lax.optimization_barrier((values, self.before))
        return values

    def add(self, *values):
        self.before = tuple(values)


class Transfer:
    def __init__(self, name, steps, devices, order):
        self.name = name
        self.level = 0
        self.steps = steps
        self.devices = devices
        self.order = order
        self.result = None
        self.send(next(self.steps))

    def send(self, sent):
        self.order.add(*self.order.before, *[values for values, unused in sent])
        with jax.named_scope(f"{self.name}_{self.level}"):
            self.got = [swap(values, bit, self.devices) for values, bit in sent]
        self.level += 1

    def go(self):
        if self.result is not None:
            return
        sent = self.steps.send(self.order.after(*self.got))
        if isinstance(sent, list):
            self.order.before = ()
            self.send(sent)
        else:
            self.result = sent


def per_device(
    mesh_shape, tokens, kinds, lengths, query_weight, key_weight, value_weight, output_weight, inner_weight,
    outer_weight, query_bias, value_bias, output_bias, inner_bias, outer_bias, first_gain, first_shift,
    second_gain, second_shift, type_table, cotangent,
):
    count = lengths.shape[0]
    rows = tokens.shape[0]
    devices = mesh_shape["wide"] * mesh_shape["narrow"]
    factor = 1.0 / devices
    bits = bits_of(mesh_shape)
    index = lax.axis_index("wide") * mesh_shape["narrow"] + lax.axis_index("narrow")
    at = [(index >> bits[k][0]) & 1 for k in "cxyz"]
    me = [at[0], jnp.where(at[0] == 0, at[1], at[2]), jnp.where(at[0] == 0, at[2], at[1]), at[3]]
    place = jnp.stack(me).astype(jnp.int32)
    unit = 2 * rows * D * D
    attention = 2 * rows * SLOT * D
    vec = pl.BlockSpec((D,), lambda i, *_: (0,))
    weight = whole(D, D)
    edges = pl.BlockSpec((rows,), lambda i, *_: (0,))
    column = pltpu.VMEM((rows, 1), F32)
    scalars = (lengths, place)
    first, query, keys, values, mixed, stat = call(
        attend_kernel, count,
        [rows_of(D), edges, whole(2, D), vec, vec, vec, vec, weight, weight, weight],
        [mols_of(D, WIDE)] + [mols_of(H, 32, WIDE)] * 3 + [mols_of(D, WIDE), mols_of(2, GROUP, WIDE)],
        [shape_of(count, D, WIDE, dtype=BF16)] + [shape_of(count, H, 32, WIDE, dtype=BF16)] * 3
        + [shape_of(count, D, WIDE, dtype=BF16), shape_of(count, 2, GROUP, WIDE)],
        [column, pltpu.VMEM((4, SLOT, WIDE), F32), pltpu.VMEM((D, WIDE), F32)],
        (*scalars, tokens, kinds, type_table, first_gain, first_shift, query_bias, value_bias, query_weight,
         key_weight, value_weight),
        flops=3 * unit + 20 * attention, name="attend",
    )
    mols = 2
    tall = lambda width: pl.BlockSpec((mols * SLOT, width), lambda i, *_: (i, 0))
    several = pl.BlockSpec((mols, D, WIDE), lambda i, *_: (i, 0, 0))
    halves = lambda width: [whole(D // 2, width)] * 2
    half_shapes = lambda width: [shape_of(D // 2, width)] * 2
    wide = 3 * HALF
    order = Order()
    transfers, made, placed = {}, {}, {}

    def begin(name):
        kept, sent = made[name]
        (sent,) = order.after(sent)
        order.before = ()
        rider = (lambda: made["input"][1]) if name == "O" else (lambda: None)
        transfers[name] = Transfer(f"sum_{name}", spread_sum(kept, sent, rider, bits, me, devices), devices, order)

    def spread(name, *parts):
        made[name] = parts

    def dense_forward():
        (mixed_in,) = order.after(mixed)
        middle, act, grad_inner, *parts = call(
            functools.partial(forward_kernel, factor), count // mols,
            [tall(D), edges, whole(2, D), several, tall(D), vec, vec, vec, vec, weight, weight, weight],
            [tall(D), tall(D), tall(D)] + halves(2 * D),
            [shape_of(rows, D), shape_of(rows, D, dtype=BF16), shape_of(rows, D, dtype=BF16)] + half_shapes(2 * D),
            [column, pltpu.VMEM((D, 2 * D), F32)],
            (*scalars, tokens, kinds, type_table, mixed_in, cotangent, output_bias, inner_bias, second_gain,
             second_shift, output_weight, inner_weight, outer_weight),
            flops=5 * unit, name="dense_forward",
        )
        made["forward"] = middle, act, grad_inner
        order.add(act)
        spread("A", *parts)

    def dense_backward():
        middle, act, grad_inner = made["forward"]
        (act,) = order.after(act)
        layer_out, grad_middle, grad_mixed, *parts, dense_vectors = call(
            functools.partial(backward_kernel, factor), count // mols,
            [tall(D), tall(D), tall(D), several, tall(D), vec, vec, weight, weight, weight],
            [tall(D), tall(D), several] + halves(D) + [whole(8, D)],
            [shape_of(rows, D, dtype=BF16), shape_of(rows, D), shape_of(count, D, WIDE, dtype=BF16)] + half_shapes(D)
            + [shape_of(8, D)],
            [pltpu.VMEM((D, D), F32)],
            (*scalars, middle, act, grad_inner, mixed, cotangent, outer_bias, second_gain, output_weight,
             inner_weight, outer_weight),
            flops=4 * unit, name="dense_backward",
        )
        made["backward"] = layer_out, grad_middle, grad_mixed, dense_vectors
        order.add(dense_vectors)
        spread("O", *parts)

    def back(part):
        heads = pl.BlockSpec((1, GROUP, 32, WIDE), lambda i, *_: (i, part, 0, 0))
        half = pl.BlockSpec((1, HALF, WIDE), lambda i, *_: (i, part, 0))
        (grad_in,) = order.after(made["backward"][2])
        bias_grad, turned_grads, *parts = call(
            functools.partial(back_kernel, factor), count,
            [mols_of(D, WIDE), heads, heads, heads, half, half,
             pl.BlockSpec((1, 1, GROUP, WIDE), lambda i, *_: (i, part, 0, 0))],
            [whole(8, wide), mols_of(3, HALF, WIDE)] + halves(wide),
            [shape_of(8, wide), shape_of(count, 3, HALF, WIDE, dtype=BF16)] + half_shapes(wide),
            [pltpu.VMEM((HALF, WIDE), F32)] * 2 + [pltpu.VMEM((3, SLOT, WIDE), F32)] * 2
            + [pltpu.VMEM((3, HALF, WIDE), F32), pltpu.VMEM((D, wide), F32)],
            (*scalars, first, query, keys, values, mixed, grad_in, stat),
            flops=unit + 20 * attention, name=f"back_{part}",
        )
        made[part] = turned_grads, bias_grad
        order.add(bias_grad)
        spread("BC"[part], *parts)

    def to_input():
        layer_out, grad_middle, grad_mixed, dense_vectors = made["backward"]
        (grad_middle,) = order.after(grad_middle)
        made["input"] = call(
            functools.partial(input_kernel, factor), count,
            [rows_of(D), edges, whole(2, D), vec, mols_of(3, HALF, WIDE), mols_of(3, HALF, WIDE), weight, weight,
             weight, rows_of(D), whole(8, D), whole(8, wide), whole(8, wide)],
            [rows_of(D), whole(16, D)],
            [shape_of(rows, D, dtype=BF16), shape_of(16, D)],
            [column],
            (*scalars, tokens, kinds, type_table, first_gain, made[0][0], made[1][0], query_weight, key_weight,
             value_weight, grad_middle, dense_vectors, made[0][1], made[1][1]),
            flops=3 * unit, name="input",
        )
        order.add(made["input"][1])

    def into_place(name):
        while transfers[name].result is None:
            transfers[name].go()
        pieces, unused = transfers[name].result
        pieces = order.after(*pieces)
        if name in "AO":
            placed[name] = put_in_place(place, pieces, 2 if name == "A" else 1)
            order.add(placed[name][0])
        else:
            placed["BC"] = put_in_place(place, pieces, 3, placed.get("BC"), "BC".index(name))
            order.add(placed["BC"][0])

    kernels = {"F": dense_forward, "D": dense_backward, "0": lambda: back(0), "1": lambda: back(1), "I": to_input}
    for step in SCHEDULE:
        if step in kernels:
            kernels[step]()
        elif step in "wxyz":
            begin("AOBC"["wxyz".index(step)])
        elif step in transfers:
            transfers[step].go()
        else:
            into_place(step.upper())
    outer_grad, inner_grad = placed["A"]
    (output_grad,) = placed["O"]
    query_grad, key_grad, value_grad = placed["BC"]
    layer_out = made["backward"][0]
    tokens_grad = made["input"][0]
    unused, small = transfers["O"].result
    return tuple(
        [layer_out, tokens_grad]
        + [grad.reshape(D, D) for grad in (query_grad, key_grad, value_grad, output_grad, inner_grad, outer_grad)]
        + [small[i] for i in (4, 5, 12, 9, 8, 0, 1, 10, 11)]
        + [small[2:4]]
    )


def solution(mesh):
    split = P(AXES, None)
    return jax.shard_map(
        functools.partial(per_device, dict(mesh.shape)),
        mesh=mesh,
        in_specs=(split, P(AXES), P(AXES)) + (P(),) * 16 + (split,),
        out_specs=(split, split) + (P(),) * 16,
        check_vma=False,
    )
```

```python
import functools
import math

import jax
import jax.numpy as jnp
import numpy as np
from jax import lax
from jax.experimental import pallas as pl
from jax.experimental.pallas import tpu as pltpu
from jax.sharding import PartitionSpec as P

D = 768
H = 32
DH = 24
SLOT = 208
GROUP = 16
HALF = GROUP * DH
WIDE = 256
SCALE = 1.0 / math.sqrt(DH)
LOG_SCALE = math.log2(math.e) / math.sqrt(DH)
LN_2 = math.log(2.0)
AXES = ("wide", "narrow")
NN = (((1,), (0,)), ((), ()))
NT = (((1,), (1,)), ((), ()))
TN = (((0,), (0,)), ((), ()))
F32 = jnp.float32
BF16 = jnp.bfloat16
VMEM = 60 * 2**20
HBM = pl.BlockSpec(memory_space=pltpu.HBM)


SCHEDULE = "FwDAx0OA1yOAzBOCAIOBACOBACBOACOBCBACOBOAoaCBBbCqCr"


def dot(left, right, dims=NN):
    return lax.dot_general(left, right, dims, preferred_element_type=F32)


def norm_parts(values):
    average = jnp.mean(values, -1, keepdims=True)
    centered = values - average
    inv_std = lax.rsqrt(jnp.mean(centered * centered, -1, keepdims=True) + 1e-05)
    return centered * inv_std, inv_std


def norm_back(grad_hat, normed, inv_std):
    return (
        grad_hat
        - jnp.mean(grad_hat, -1, keepdims=True)
        - normed * jnp.mean(grad_hat * normed, -1, keepdims=True)
    ) * inv_std


def row_of(ref):
    return ref[...].astype(F32).reshape(1, D)


def kinds_column(kinds_ref, edge_ref):
    @pl.when(pl.program_id(0) == 0)
    def turn():
        kinds = kinds_ref[...].astype(F32).reshape(1, -1)
        edge_ref[...] = jnp.broadcast_to(kinds, (8, kinds.shape[1])).T[:, :1]


def embed(tokens, edge, table_ref):
    table = table_ref[...].astype(F32)
    return tokens.astype(F32) + jnp.where(edge == 1, table[1:2], table[0:1])


def turn(values):
    return jnp.concatenate([values, jnp.zeros((WIDE - SLOT, values.shape[1]), F32)]).T


def with_rows(values, rows):
    index = lax.broadcasted_iota(jnp.int32, (8, WIDE), 0)
    extra = jnp.zeros((8, WIDE), F32)
    for i, row in enumerate(rows):
        extra = jnp.where(index == i, row, extra)
    if values.ndim == 3:
        extra = jnp.broadcast_to(extra, (values.shape[0], 8, WIDE))
    return jnp.concatenate([values, extra], -2).astype(BF16)


def split_row(row):
    high = row.astype(BF16).astype(F32)
    mid = (row - high).astype(BF16).astype(F32)
    return [high, mid, row - high - mid]


def attend_kernel(
    lengths_ref, place_ref, tokens_ref, kinds_ref, table_ref, gain_ref, shift_ref, query_bias_ref, value_bias_ref,
    query_weight_ref, key_weight_ref, value_weight_ref,
    first_ref, query_ref, keys_ref, values_ref, mixed_ref, stat_ref,
    edge_ref, scores_ref, out_ref,
):
    mol = pl.program_id(0)
    kinds_column(kinds_ref, edge_ref)
    edge = edge_ref[pl.ds(pl.multiple_of(mol * SLOT, 8), SLOT), :]
    normed, unused = norm_parts(embed(tokens_ref[...], edge, table_ref))
    first32 = normed * row_of(gain_ref) + row_of(shift_ref)
    first = first32.astype(BF16)
    first_ref[0] = turn(first32).astype(BF16)
    slot = lax.broadcasted_iota(jnp.int32, (1, WIDE), 1)
    bias = jnp.where(slot < lengths_ref[mol], 0.0, -1e30)
    ones = jnp.ones((1, WIDE), F32)
    query = (dot(first, query_weight_ref[...]) + row_of(query_bias_ref)) * LOG_SCALE
    keys = dot(first, key_weight_ref[...])
    values = dot(first, value_weight_ref[...]) + row_of(value_bias_ref)
    query_ref[0] = with_rows(turn(query).reshape(H, DH, WIDE), [ones])
    keys_ref[0] = with_rows(turn(keys).reshape(H, DH, WIDE), [bias, ones, ones, ones])
    values_ref[0] = with_rows(turn(values).reshape(H, DH, WIDE), [ones, ones, ones])
    lag = 7

    def score(h):
        scores_ref[h % (lag + 1)] = dot(keys_ref[0, h, :, :SLOT], query_ref[0, h], TN)

    def mix(h):
        scores = scores_ref[h % (lag + 1)]
        top = jnp.max(scores, axis=0, keepdims=True)
        powered = jnp.exp2(scores - top).astype(BF16)
        out = dot(values_ref[0, h, :, :SLOT], powered)
        total = out[DH : DH + 1]
        out_ref[h * DH : (h + 1) * DH, :] = out[:DH] * (1.0 / total)
        stat_ref[0, h // GROUP, h % GROUP : h % GROUP + 1] = top + jnp.log2(total)

    for h in range(H + lag):
        if h < H:
            score(h)
        if h >= lag:
            mix(h - lag)
    mixed_ref[0] = out_ref[...].astype(BF16)


def gelu_parts(inner):
    root = math.sqrt(2.0 / math.pi)
    bend = root * 0.044715 * inner * inner + root
    half = 0.5 * jnp.tanh(inner * bend) + 0.5
    act = inner * half
    return act, half + act * (1.0 - half) * (6.0 * bend - 4.0 * root)


def valid_rows(lengths_ref, first, mols):
    slot = lax.broadcasted_iota(jnp.int32, (SLOT, 1), 0)
    return jnp.concatenate([(slot < lengths_ref[first + i]).astype(F32) for i in range(mols)])


def forward_kernel(
    factor, lengths_ref, place_ref, tokens_ref, kinds_ref, table_ref, mixed_ref, cotangent_ref, output_bias_ref,
    inner_bias_ref, gain_ref, shift_ref, output_weight_ref, inner_weight_ref, outer_weight_ref,
    middle_ref, act_ref, grad_inner_ref, kept_ref, sent_ref,
    edge_ref, second_ref,
):
    mols = mixed_ref.shape[0]
    kinds_column(kinds_ref, edge_ref)
    edge = edge_ref[...]
    valid = valid_rows(lengths_ref, 0, mols)
    mixed = jnp.concatenate([dot(mixed_ref[i], output_weight_ref[...], TN)[:SLOT] for i in range(mols)])
    middle = embed(tokens_ref[...], edge, table_ref) + mixed + row_of(output_bias_ref)
    middle_ref[...] = middle
    normed, unused = norm_parts(middle)
    second = (normed * row_of(gain_ref) + row_of(shift_ref)).astype(BF16)
    inner = dot(second, inner_weight_ref[...]) + row_of(inner_bias_ref)
    act32, slope = gelu_parts(inner)
    act = act32.astype(BF16)
    act_ref[...] = act
    grad_low = (cotangent_ref[...].astype(F32) * valid).astype(BF16)
    grad_inner = (dot(grad_low, outer_weight_ref[...], NT) * slope).astype(BF16)
    grad_inner_ref[...] = grad_inner

    second_ref[...] = second
    for target, begin in core_halves(place_ref[0], kept_ref, sent_ref):
        target[:, :D] = dot(act_ref[:, pl.ds(begin, D // 2)], grad_low * BF16(factor), TN)
        target[:, D:] = dot(second_ref[:, pl.ds(begin, D // 2)], grad_inner * BF16(factor), TN)


def core_halves(core, kept_ref, sent_ref):
    rows = kept_ref.shape[0]
    return [(ref, pl.multiple_of(which * rows, 128)) for ref, which in ((kept_ref, core), (sent_ref, 1 - core))]


def backward_kernel(
    factor, lengths_ref, place_ref, middle_ref, act_ref, grad_inner_ref, mixed_ref, cotangent_ref, outer_bias_ref,
    gain_ref, output_weight_ref, inner_weight_ref, outer_weight_ref,
    layer_ref, grad_middle_ref, grad_mixed_ref, kept_ref, sent_ref, vectors_ref,
):
    mols = mixed_ref.shape[0]
    valid = valid_rows(lengths_ref, 0, mols)
    middle = middle_ref[...]
    normed, inv_std = norm_parts(middle)
    grad_out = cotangent_ref[...].astype(F32) * valid
    grad_inner = grad_inner_ref[...]
    grad_second = dot(grad_inner, inner_weight_ref[...], NT)
    grad_middle = grad_out + norm_back(grad_second * row_of(gain_ref), normed, inv_std)
    grad_middle_ref[...] = grad_middle
    pad = jnp.zeros((WIDE - SLOT, D), F32)
    grads = [jnp.concatenate([grad_middle[i * SLOT : (i + 1) * SLOT], pad]).astype(BF16) for i in range(mols)]
    for i, grad in enumerate(grads):
        grad_mixed_ref[i] = dot(output_weight_ref[...], grad, NT).astype(BF16)
    for target, begin in core_halves(place_ref[0], kept_ref, sent_ref):
        products = [dot(mixed_ref[i, pl.ds(begin, D // 2), :], grad * BF16(factor)) for i, grad in enumerate(grads)]
        target[...] = functools.reduce(jnp.add, products)
    layer = middle + dot(act_ref[...], outer_weight_ref[...]) + row_of(outer_bias_ref)
    layer_ref[...] = (layer * valid).astype(BF16)
    sums = [
        grad_out,
        grad_inner.astype(F32),
        grad_second * normed,
        grad_second,
        grad_middle.astype(BF16).astype(F32),
    ]
    vectors_ref[...] = jnp.zeros_like(vectors_ref)
    for i, values in enumerate(sums):
        vectors_ref[i : i + 1] = jnp.sum(values, 0, keepdims=True) * factor


def back_kernel(
    factor, lengths_ref, place_ref, first_ref, query_ref, keys_ref, values_ref, mixed_ref, grad_ref, stat_ref,
    vectors_ref, turned_grads_ref, kept_ref, sent_ref,
    mixed32_ref, grad32_ref, scores_ref, probs_ref, grads_ref,
):
    step = pl.program_id(0)

    @pl.when(step == 0)
    def start_sums():
        for ref in (grads_ref, kept_ref, sent_ref, vectors_ref):
            ref[...] = jnp.zeros_like(ref)

    mixed32_ref[...] = mixed_ref[0].astype(F32)
    grad32_ref[...] = grad_ref[0].astype(F32)
    lag = 2

    def score(h):
        rows = slice(h * DH, (h + 1) * DH)
        stat = split_row(-stat_ref[0, 0, h : h + 1])
        query = with_rows(query_ref[0, h, :DH].astype(F32), [1.0] + stat)
        scores_ref[h % (lag + 1)] = dot(keys_ref[0, h, :, :SLOT], query, TN)
        grad = grad32_ref[rows]
        shared = split_row(-jnp.sum(grad * mixed32_ref[rows], axis=0, keepdims=True))
        probs_ref[h % (lag + 1)] = dot(values_ref[0, h, :, :SLOT], with_rows(grad, shared), TN)

    def back(h):
        rows = slice(h * DH, (h + 1) * DH)
        probs = jnp.exp2(scores_ref[h % (lag + 1)])
        grad_scores = (probs * probs_ref[h % (lag + 1)]).astype(BF16)
        grad = with_rows(grad32_ref[rows], [])
        grads_ref[0, rows] = dot(keys_ref[0, h, :, :SLOT], grad_scores)[:DH] * SCALE
        grads_ref[1, rows, :SLOT] = dot(query_ref[0, h], grad_scores, NT)[:DH] * LN_2
        grads_ref[2, rows, :SLOT] = dot(grad, probs.astype(BF16), NT)[:DH]

    for h in range(GROUP + lag):
        if h < GROUP:
            score(h)
        if h >= lag:
            back(h - lag)
    grads = grads_ref[...].astype(BF16)
    turned_grads_ref[0] = grads
    grads = (grads * BF16(factor)).reshape(3 * HALF, WIDE)
    for target, begin in core_halves(place_ref[0], kept_ref, sent_ref):
        target[...] += dot(first_ref[0, pl.ds(begin, D // 2), :], grads, NT)
    vectors_ref[...] += dot(jnp.ones((8, WIDE), BF16), grads, NT)


def input_kernel(
    factor, lengths_ref, place_ref, tokens_ref, kinds_ref, table_ref, gain_ref, low_ref, high_ref, query_weight_ref,
    key_weight_ref, value_weight_ref, grad_middle_ref, dense_ref, low_bias_ref, high_bias_ref,
    tokens_grad_ref, vectors_ref,
    edge_ref,
):
    mol = pl.program_id(0)

    @pl.when(mol == 0)
    def start_sums():
        vectors_ref[...] = jnp.zeros_like(vectors_ref)

    kinds_column(kinds_ref, edge_ref)
    edge = edge_ref[pl.ds(pl.multiple_of(mol * SLOT, 8), SLOT), :]
    total = jnp.zeros((D, WIDE), F32)
    for i, weight_ref in enumerate((query_weight_ref, key_weight_ref, value_weight_ref)):
        total = total + dot(weight_ref[...], jnp.concatenate([low_ref[0, i], high_ref[0, i]]))
    grad_first = total.T[:SLOT]
    normed, inv_std = norm_parts(embed(tokens_ref[...], edge, table_ref))
    grad_start = grad_middle_ref[...] + norm_back(grad_first * row_of(gain_ref), normed, inv_std)
    tokens_grad_ref[...] = grad_start.astype(BF16)
    sums = [
        grad_first * normed,
        grad_first,
        jnp.where(edge == 1, 0.0, grad_start),
        jnp.where(edge == 1, grad_start, 0.0),
    ]
    for i, values in enumerate(sums):
        vectors_ref[i : i + 1] += jnp.sum(values, 0, keepdims=True)

    @pl.when(mol == pl.num_programs(0) - 1)
    def finish():
        vectors_ref[...] = vectors_ref[...] * factor
        for i, begin in ((0, 0), (1, 2 * HALF)):
            vectors_ref[4 + i : 5 + i, :HALF] = low_bias_ref[:1, begin : begin + HALF]
            vectors_ref[4 + i : 5 + i, HALF:] = high_bias_ref[:1, begin : begin + HALF]
        vectors_ref[8:16] = dense_ref[...]


def whole(*shape):
    return pl.BlockSpec(shape, lambda i, *_: (0,) * len(shape))


def rows_of(width):
    return pl.BlockSpec((SLOT, width), lambda i, *_: (i, 0))


def mols_of(*shape):
    return pl.BlockSpec((1,) + shape, lambda i, *_: (i,) + (0,) * len(shape))


def shape_of(*shape, dtype=F32):
    return jax.ShapeDtypeStruct(shape, dtype)


def call(kernel, count, in_specs, out_specs, out_shape, scratch, args, flops, name, vmem=VMEM):
    return pl.pallas_call(
        kernel,
        grid_spec=pltpu.PrefetchScalarGridSpec(
            num_scalar_prefetch=2,
            grid=(count,),
            in_specs=in_specs,
            out_specs=out_specs,
            scratch_shapes=scratch,
        ),
        out_shape=out_shape,
        compiler_params=pltpu.CompilerParams(
            dimension_semantics=("arbitrary",), vmem_limit_bytes=vmem
        ),
        cost_estimate=pl.CostEstimate(flops=20 * flops, bytes_accessed=2**20, transcendentals=0),
        name=name,
    )(*args)


def bits_of(mesh_shape):
    narrow = mesh_shape["narrow"].bit_length() - 1
    wide = mesh_shape["wide"].bit_length() - 1
    y = (wide - 1) // 2
    return {
        "c": [0],
        "x": list(range(1, narrow)),
        "y": list(range(narrow, narrow + y)),
        "z": list(range(narrow + y, narrow + wide)),
    }


def swap(values, bit, devices):
    even, odd = bit if isinstance(bit, tuple) else (bit, bit)
    return lax.ppermute(values, AXES, [(i, i ^ (1 << (odd if i & 1 else even))) for i in range(devices)])


def pick(values, *index):
    for i in index:
        values = lax.dynamic_index_in_dim(values, i, 0, keepdims=False)
    return values


def place_kernel(parts, count_in, place_ref, *refs):
    sources = refs[: len(parts)]
    outs = refs[len(parts) + count_in : -2 - len(parts)]
    stages, (in_sems, out_sems) = refs[-2 - len(parts) : -2], refs[-2:]
    fetches, stores = {}, []
    for n, (source, stage) in enumerate(zip(sources, stages)):
        rows = stage.shape[1]
        for k in range(4):
            fetches[n, k] = pltpu.make_async_copy(source.at[pl.ds(k * rows, rows)], stage.at[k], in_sems.at[n, k])
            fetches[n, k].start()
    for n, (other, low, targets, column) in enumerate(parts):
        core, first, second = place_ref[0], place_ref[1], place_ref[2]
        if other:
            core, first, second = 1 - core, second, first
        width = stages[n].shape[2] // len(targets)
        for k in range(4):
            row = (
                core,
                lax.bitwise_xor(low, first),
                lax.bitwise_xor(k // 2, second),
                lax.bitwise_xor(k % 2, place_ref[3]),
            )
            fetches[n, k].wait()
            for m, target in enumerate(targets):
                stores.append(
                    pltpu.make_async_copy(
                        stages[n].at[k, :, m * width : (m + 1) * width],
                        outs[target].at[*row, :, column : column + width],
                        out_sems.at[n, k, m],
                    )
                )
                stores[-1].start()
    for store in stores:
        store.wait()


def put_in_place(place, pieces, parts, count_out, before=()):
    rows = D // 16
    pieces = [piece.reshape(-1, piece.shape[-1]) for piece in pieces]
    return pl.pallas_call(
        functools.partial(place_kernel, parts, len(before)),
        grid_spec=pltpu.PrefetchScalarGridSpec(
            num_scalar_prefetch=1,
            grid=(1,),
            in_specs=[HBM] * (len(pieces) + len(before)),
            out_specs=[HBM] * count_out,
            scratch_shapes=[pltpu.VMEM((4, rows, piece.shape[1]), F32) for piece in pieces]
            + [pltpu.SemaphoreType.DMA((len(pieces), 4)), pltpu.SemaphoreType.DMA((len(pieces), 4, 3))],
        ),
        out_shape=[shape_of(2, 2, 2, 2, rows, D)] * count_out,
        input_output_aliases={1 + len(pieces) + i: i for i in range(len(before))},
        compiler_params=pltpu.CompilerParams(vmem_limit_bytes=VMEM),
        cost_estimate=pl.CostEstimate(flops=10**10, bytes_accessed=2**20, transcendentals=0),
        name="place",
    )(place, *pieces, *before)


def spread_sum(kept, sent, rider, own, bits, me, devices):
    rows, width = kept.shape[0] // 8, kept.shape[1]
    core, x, y, z = (bits[k][0] for k in "cxyz")
    (got,) = yield [(sent, core)]
    terms = [v.reshape(2, 2, 2, rows, width) for v in (kept, got)]
    scatter = (((x, y), me[1]), ((y, x), me[2]), (z, me[3]))
    for bit, mine in scatter:
        (got,) = yield [(functools.reduce(jnp.add, [pick(t, 1 - mine) for t in terms]), bit)]
        terms = [pick(t, mine) for t in terms] + [got]
    total = functools.reduce(jnp.add, terms)
    small = rider()

    def with_small(values):
        return values if small is None else jnp.concatenate([values.reshape(-1, width), small])

    def apart(values, shape):
        if small is None:
            return values, None
        count = math.prod(shape[:-1])
        return values[:count].reshape(shape), small + values[count:]

    for bit in bits["x"][1:] + bits["y"][1:] + bits["z"][1:]:
        (got,) = yield [(with_small(total), bit)]
        got, small = apart(got, total.shape)
        total = total + got
    (got,) = yield [(with_small(total), z)]
    got, small = apart(got, total.shape)
    total = jnp.stack([total, got])
    (got,) = yield [(with_small(total), (y, x))]
    got, small = apart(got, total.shape)
    total = jnp.stack([total, got])
    got, other = yield [(with_small(total), (x, y)), (total, core)]
    got, small = apart(got, total.shape)
    own.extend((total, got))
    (last,) = yield [(with_small(got), core)]
    if small is not None:
        small = small + last[-small.shape[0] :]
    yield (other, last), small


class Order:
    def __init__(self):
        self.before = ()

    def after(self, *values):
        if self.before:
            values, unused = lax.optimization_barrier((values, self.before))
        return values

    def add(self, *values):
        self.before = tuple(values)


class Transfer:
    def __init__(self, name, steps, own, devices, order):
        self.name = name
        self.own = own
        self.level = 0
        self.steps = steps
        self.devices = devices
        self.order = order
        self.result = None
        self.send(next(self.steps))

    def send(self, sent):
        self.order.add(*self.order.before, *[values for values, unused in sent])
        with jax.named_scope(f"{self.name}_{self.level}"):
            self.got = [swap(values, bit, self.devices) for values, bit in sent]
        self.level += 1

    def go(self):
        if self.result is not None:
            return
        sent = self.steps.send(self.order.after(*self.got))
        if isinstance(sent, list):
            self.order.before = ()
            self.send(sent)
        else:
            self.result = sent


def per_device(
    mesh_shape, tokens, kinds, lengths, query_weight, key_weight, value_weight, output_weight, inner_weight,
    outer_weight, query_bias, value_bias, output_bias, inner_bias, outer_bias, first_gain, first_shift,
    second_gain, second_shift, type_table, cotangent,
):
    count = lengths.shape[0]
    rows = tokens.shape[0]
    devices = mesh_shape["wide"] * mesh_shape["narrow"]
    factor = 1.0 / devices
    bits = bits_of(mesh_shape)
    index = lax.axis_index("wide") * mesh_shape["narrow"] + lax.axis_index("narrow")
    at = [(index >> bits[k][0]) & 1 for k in "cxyz"]
    me = [at[0], jnp.where(at[0] == 0, at[1], at[2]), jnp.where(at[0] == 0, at[2], at[1]), at[3]]
    place = jnp.stack(me).astype(jnp.int32)
    unit = 2 * rows * D * D
    attention = 2 * rows * SLOT * D
    vec = pl.BlockSpec((D,), lambda i, *_: (0,))
    weight = whole(D, D)
    edges = pl.BlockSpec((rows,), lambda i, *_: (0,))
    column = pltpu.VMEM((rows, 1), F32)
    scalars = (lengths, place)
    first, query, keys, values, mixed, stat = call(
        attend_kernel, count,
        [rows_of(D), edges, whole(2, D), vec, vec, vec, vec, weight, weight, weight],
        [mols_of(D, WIDE)] + [mols_of(H, 32, WIDE)] * 3 + [mols_of(D, WIDE), mols_of(2, GROUP, WIDE)],
        [shape_of(count, D, WIDE, dtype=BF16)] + [shape_of(count, H, 32, WIDE, dtype=BF16)] * 3
        + [shape_of(count, D, WIDE, dtype=BF16), shape_of(count, 2, GROUP, WIDE)],
        [column, pltpu.VMEM((8, SLOT, WIDE), F32), pltpu.VMEM((D, WIDE), F32)],
        (*scalars, tokens, kinds, type_table, first_gain, first_shift, query_bias, value_bias, query_weight,
         key_weight, value_weight),
        flops=3 * unit + 20 * attention, name="attend",
    )
    mols = count
    tall = lambda width: pl.BlockSpec((mols * SLOT, width), lambda i, *_: (i, 0))
    several = pl.BlockSpec((mols, D, WIDE), lambda i, *_: (i, 0, 0))
    halves = lambda width: [whole(D // 2, width)] * 2
    half_shapes = lambda width: [shape_of(D // 2, width)] * 2
    wide = 3 * HALF
    order = Order()
    transfers, made, placed = {}, {}, {}

    def begin(name):
        kept, sent = made[name]
        (sent,) = order.after(sent)
        order.before = ()
        rider = (lambda: made["input"][1]) if name == "O" else (lambda: None)
        own = []
        steps = spread_sum(kept, sent, rider, own, bits, me, devices)
        transfers[name] = Transfer(f"sum_{name}", steps, own, devices, order)

    def spread(name, *parts):
        made[name] = parts

    def dense_forward():
        (mixed_in,) = order.after(mixed)
        middle, act, grad_inner, *parts = call(
            functools.partial(forward_kernel, factor), count // mols,
            [tall(D), edges, whole(2, D), several, tall(D), vec, vec, vec, vec, weight, weight, weight],
            [tall(D), tall(D), tall(D)] + halves(2 * D),
            [shape_of(rows, D), shape_of(rows, D, dtype=BF16), shape_of(rows, D, dtype=BF16)] + half_shapes(2 * D),
            [column, pltpu.VMEM((rows, D), BF16)],
            (*scalars, tokens, kinds, type_table, mixed_in, cotangent, output_bias, inner_bias, second_gain,
             second_shift, output_weight, inner_weight, outer_weight),
            flops=5 * unit, name="dense_forward",
        )
        made["forward"] = middle, act, grad_inner
        order.add(act)
        spread("A", *parts)

    def dense_backward():
        middle, act, grad_inner = made["forward"]
        (act,) = order.after(act)
        layer_out, grad_middle, grad_mixed, *parts, dense_vectors = call(
            functools.partial(backward_kernel, factor), count // mols,
            [tall(D), tall(D), tall(D), several, tall(D), vec, vec, weight, weight, weight],
            [tall(D), tall(D), several] + halves(D) + [whole(8, D)],
            [shape_of(rows, D, dtype=BF16), shape_of(rows, D), shape_of(count, D, WIDE, dtype=BF16)] + half_shapes(D)
            + [shape_of(8, D)],
            [],
            (*scalars, middle, act, grad_inner, mixed, cotangent, outer_bias, second_gain, output_weight,
             inner_weight, outer_weight),
            flops=4 * unit, name="dense_backward",
        )
        made["backward"] = layer_out, grad_middle, grad_mixed, dense_vectors
        order.add(dense_vectors)
        spread("O", *parts)

    def back(part):
        heads = pl.BlockSpec((1, GROUP, 32, WIDE), lambda i, *_: (i, part, 0, 0))
        half = pl.BlockSpec((1, HALF, WIDE), lambda i, *_: (i, part, 0))
        (grad_in,) = order.after(made["backward"][2])
        bias_grad, turned_grads, *parts = call(
            functools.partial(back_kernel, factor), count,
            [mols_of(D, WIDE), heads, heads, heads, half, half,
             pl.BlockSpec((1, 1, GROUP, WIDE), lambda i, *_: (i, part, 0, 0))],
            [whole(8, wide), mols_of(3, HALF, WIDE)] + halves(wide),
            [shape_of(8, wide), shape_of(count, 3, HALF, WIDE, dtype=BF16)] + half_shapes(wide),
            [pltpu.VMEM((HALF, WIDE), F32)] * 2 + [pltpu.VMEM((3, SLOT, WIDE), F32)] * 2
            + [pltpu.VMEM((3, HALF, WIDE), F32)],
            (*scalars, first, query, keys, values, mixed, grad_in, stat),
            flops=unit + 20 * attention, name=f"back_{part}",
        )
        made[part] = turned_grads, bias_grad
        order.add(bias_grad)
        spread("BC"[part], *parts)

    def to_input():
        layer_out, grad_middle, grad_mixed, dense_vectors = made["backward"]
        (grad_middle,) = order.after(grad_middle)
        made["input"] = call(
            functools.partial(input_kernel, factor), count,
            [rows_of(D), edges, whole(2, D), vec, mols_of(3, HALF, WIDE), mols_of(3, HALF, WIDE), weight, weight,
             weight, rows_of(D), whole(8, D), whole(8, wide), whole(8, wide)],
            [rows_of(D), whole(16, D)],
            [shape_of(rows, D, dtype=BF16), shape_of(16, D)],
            [column],
            (*scalars, tokens, kinds, type_table, first_gain, made[0][0], made[1][0], query_weight, key_weight,
             value_weight, grad_middle, dense_vectors, made[0][1], made[1][1]),
            flops=3 * unit, name="input",
        )
        order.add(made["input"][1])

    def own_parts(name, targets, column=0):
        while not transfers[name].own:
            transfers[name].go()
        return [(piece, (0, low, targets, column)) for low, piece in enumerate(transfers[name].own)]

    def other_parts(name, targets, column=0):
        while transfers[name].result is None:
            transfers[name].go()
        return [(piece, (1, low, targets, column)) for low, piece in enumerate(transfers[name].result[0])]

    def into_place(step):
        before, three = (), (0, 1, 2)
        if step == "a":
            found = other_parts("A", (0, 1)) + own_parts("A", (0, 1))
        elif step == "o":
            found = other_parts("O", (0,)) + own_parts("O", (0,))
        elif step == "b":
            found = other_parts("B", three) + own_parts("B", three)
        elif step == "q":
            found, before = own_parts("C", three, HALF), placed["b"]
        else:
            found, before = other_parts("C", three, HALF), placed["q"]
        pieces, parts = zip(*found)
        placed[step] = put_in_place(
            place, order.after(*pieces), parts, {"a": 2, "o": 1}.get(step, 3), before
        )
        order.add(placed[step][0])

    def finish_vectors():
        if "vectors" not in made:
            small = transfers["O"].result[1]
            made["vectors"] = [small[i] for i in (4, 5, 12, 9, 8, 0, 1, 10, 11)] + [small[2:4]]
            order.add(*order.before, *made["vectors"])

    kernels = {"F": dense_forward, "D": dense_backward, "0": lambda: back(0), "1": lambda: back(1), "I": to_input}
    for step in SCHEDULE:
        if step in kernels:
            kernels[step]()
        elif step in "wxyz":
            begin("AOBC"["wxyz".index(step)])
        elif step in transfers:
            transfers[step].go()
            if step == "O" and transfers[step].result is not None:
                finish_vectors()
        else:
            into_place(step)
    outer_grad, inner_grad = placed["a"]
    (output_grad,) = placed["o"]
    query_grad, key_grad, value_grad = placed["r"]
    layer_out = made["backward"][0]
    tokens_grad = made["input"][0]
    finish_vectors()
    return tuple(
        [layer_out, tokens_grad]
        + [grad.reshape(D, D) for grad in (query_grad, key_grad, value_grad, output_grad, inner_grad, outer_grad)]
        + made["vectors"]
    )


def solution(mesh):
    split = P(AXES, None)
    return jax.shard_map(
        functools.partial(per_device, dict(mesh.shape)),
        mesh=mesh,
        in_specs=(split, P(AXES), P(AXES)) + (P(),) * 16 + (split,),
        out_specs=(split, split) + (P(),) * 16,
        check_vma=False,
    )
```

```python
import functools
import math

import jax
import jax.numpy as jnp
import numpy as np
from jax import lax
from jax.experimental import pallas as pl
from jax.experimental.pallas import tpu as pltpu
from jax.sharding import PartitionSpec as P

D = 768
H = 32
DH = 24
SLOT = 208
GROUP = 16
HALF = GROUP * DH
WIDE = 256
SCALE = 1.0 / math.sqrt(DH)
LOG_SCALE = math.log2(math.e) / math.sqrt(DH)
LN_2 = math.log(2.0)
AXES = ("wide", "narrow")
NN = (((1,), (0,)), ((), ()))
NT = (((1,), (1,)), ((), ()))
TN = (((0,), (0,)), ((), ()))
F32 = jnp.float32
BF16 = jnp.bfloat16
VMEM = 60 * 2**20
HBM = pl.BlockSpec(memory_space=pltpu.HBM)


SCHEDULE = "FwDAx0OA1yOAzBOCAIOBACOBACBOACOBCBACOBOAoaCBBbCqCr"


def dot(left, right, dims=NN):
    return lax.dot_general(left, right, dims, preferred_element_type=F32)


def norm_parts(values):
    average = jnp.mean(values, -1, keepdims=True)
    centered = values - average
    inv_std = lax.rsqrt(jnp.mean(centered * centered, -1, keepdims=True) + 1e-05)
    return centered * inv_std, inv_std


def norm_back(grad_hat, normed, inv_std):
    return (
        grad_hat
        - jnp.mean(grad_hat, -1, keepdims=True)
        - normed * jnp.mean(grad_hat * normed, -1, keepdims=True)
    ) * inv_std


def row_of(ref):
    return ref[...].astype(F32).reshape(1, D)


def kinds_column(kinds_ref, edge_ref):
    @pl.when(pl.program_id(0) == 0)
    def turn():
        kinds = kinds_ref[...].astype(F32).reshape(1, -1)
        edge_ref[...] = jnp.broadcast_to(kinds, (8, kinds.shape[1])).T[:, :1]


def embed(tokens, edge, table_ref):
    table = table_ref[...].astype(F32)
    return tokens.astype(F32) + jnp.where(edge == 1, table[1:2], table[0:1])


def turn(values):
    return jnp.concatenate([values, jnp.zeros((WIDE - SLOT, values.shape[1]), F32)]).T


def with_rows(values, rows):
    index = lax.broadcasted_iota(jnp.int32, (8, WIDE), 0)
    extra = jnp.zeros((8, WIDE), F32)
    for i, row in enumerate(rows):
        extra = jnp.where(index == i, row, extra)
    if values.ndim == 3:
        extra = jnp.broadcast_to(extra, (values.shape[0], 8, WIDE))
    return jnp.concatenate([values, extra], -2).astype(BF16)


def split_row(row):
    high = row.astype(BF16).astype(F32)
    mid = (row - high).astype(BF16).astype(F32)
    return [high, mid, row - high - mid]


def attend_kernel(
    factor, lengths_ref, place_ref, tokens_ref, kinds_ref, table_ref, gain_ref, shift_ref, query_bias_ref,
    value_bias_ref, query_weight_ref, key_weight_ref, value_weight_ref, output_bias_ref, inner_bias_ref,
    second_gain_ref, second_shift_ref, *refs,
):
    later_hbm, refs = refs[:5], refs[5:]
    first_ref, query_ref, keys_ref, values_ref, mixed_ref, stat_ref, *outputs = refs[:11]
    edge_ref, scores_ref, out_ref, mixed_all_ref, second_ref, *later, sems = refs[11:]
    mol = pl.program_id(0)
    copies = [pltpu.make_async_copy(*pair, sems.at[k]) for k, pair in enumerate(zip(later_hbm, later))]

    @pl.when(mol == 0)
    def fetch():
        for copy in copies:
            copy.start()

    kinds_column(kinds_ref, edge_ref)

    @pl.when(mol < pl.num_programs(0) - 1)
    def attend():
        attend_molecule(
            mol, lengths_ref, tokens_ref, edge_ref, table_ref, gain_ref, shift_ref, query_bias_ref, value_bias_ref,
            query_weight_ref, key_weight_ref, value_weight_ref, first_ref, query_ref, keys_ref, values_ref, mixed_ref,
            stat_ref, scores_ref, out_ref,
        )
        mixed_all_ref[mol] = mixed_ref[0]

    @pl.when(mol == pl.num_programs(0) - 1)
    def forward():
        for copy in copies:
            copy.wait()
        feed_forward(
            factor, lengths_ref, place_ref, edge_ref, table_ref, mixed_all_ref, *later, output_bias_ref,
            inner_bias_ref, second_gain_ref, second_shift_ref, *outputs, second_ref,
        )


def attend_molecule(
    mol, lengths_ref, tokens_ref, edge_ref, table_ref, gain_ref, shift_ref, query_bias_ref, value_bias_ref,
    query_weight_ref, key_weight_ref, value_weight_ref, first_ref, query_ref, keys_ref, values_ref, mixed_ref,
    stat_ref, scores_ref, out_ref,
):
    edge = edge_ref[pl.ds(pl.multiple_of(mol * SLOT, 8), SLOT), :]
    normed, unused = norm_parts(embed(tokens_ref[...], edge, table_ref))
    first32 = normed * row_of(gain_ref) + row_of(shift_ref)
    first = first32.astype(BF16)
    first_ref[0] = turn(first32).astype(BF16)
    slot = lax.broadcasted_iota(jnp.int32, (1, WIDE), 1)
    bias = jnp.where(slot < lengths_ref[mol], 0.0, -1e30)
    ones = jnp.ones((1, WIDE), F32)
    query = (dot(first, query_weight_ref[...]) + row_of(query_bias_ref)) * LOG_SCALE
    keys = dot(first, key_weight_ref[...])
    values = dot(first, value_weight_ref[...]) + row_of(value_bias_ref)
    query_ref[0] = with_rows(turn(query).reshape(H, DH, WIDE), [ones])
    keys_ref[0] = with_rows(turn(keys).reshape(H, DH, WIDE), [bias, ones, ones, ones])
    values_ref[0] = with_rows(turn(values).reshape(H, DH, WIDE), [ones, ones, ones])
    lag = 7

    def score(h):
        scores_ref[h % (lag + 1)] = dot(keys_ref[0, h, :, :SLOT], query_ref[0, h], TN)

    def mix(h):
        scores = scores_ref[h % (lag + 1)]
        top = jnp.max(scores, axis=0, keepdims=True)
        powered = jnp.exp2(scores - top).astype(BF16)
        out = dot(values_ref[0, h, :, :SLOT], powered)
        total = out[DH : DH + 1]
        out_ref[h * DH : (h + 1) * DH, :] = out[:DH] * (1.0 / total)
        stat_ref[0, h // GROUP, h % GROUP : h % GROUP + 1] = top + jnp.log2(total)

    for h in range(H + lag):
        if h < H:
            score(h)
        if h >= lag:
            mix(h - lag)
    mixed_ref[0] = out_ref[...].astype(BF16)


def gelu_parts(inner):
    root = math.sqrt(2.0 / math.pi)
    bend = root * 0.044715 * inner * inner + root
    half = 0.5 * jnp.tanh(inner * bend) + 0.5
    act = inner * half
    return act, half + act * (1.0 - half) * (6.0 * bend - 4.0 * root)


def valid_rows(lengths_ref, first, mols):
    slot = lax.broadcasted_iota(jnp.int32, (SLOT, 1), 0)
    return jnp.concatenate([(slot < lengths_ref[first + i]).astype(F32) for i in range(mols)])


def feed_forward(
    factor, lengths_ref, place_ref, edge_ref, table_ref, mixed_ref, tokens_ref, cotangent_ref, output_weight_ref,
    inner_weight_ref, outer_weight_ref, output_bias_ref, inner_bias_ref, gain_ref, shift_ref,
    middle_ref, act_ref, grad_inner_ref, kept_ref, sent_ref, second_ref,
):
    mols = mixed_ref.shape[0]
    edge = edge_ref[...]
    valid = valid_rows(lengths_ref, 0, mols)
    mixed = jnp.concatenate([dot(mixed_ref[i], output_weight_ref[...], TN)[:SLOT] for i in range(mols)])
    middle = embed(tokens_ref[...], edge, table_ref) + mixed + row_of(output_bias_ref)
    middle_ref[...] = middle
    normed, unused = norm_parts(middle)
    second = (normed * row_of(gain_ref) + row_of(shift_ref)).astype(BF16)
    inner = dot(second, inner_weight_ref[...]) + row_of(inner_bias_ref)
    act32, slope = gelu_parts(inner)
    act = act32.astype(BF16)
    act_ref[...] = act
    grad_low = (cotangent_ref[...].astype(F32) * valid).astype(BF16)
    grad_inner = (dot(grad_low, outer_weight_ref[...], NT) * slope).astype(BF16)
    grad_inner_ref[...] = grad_inner

    second_ref[...] = second
    for target, begin in core_halves(place_ref[0], kept_ref, sent_ref):
        target[:, :D] = dot(act_ref[:, pl.ds(begin, D // 2)], grad_low * BF16(factor), TN)
        target[:, D:] = dot(second_ref[:, pl.ds(begin, D // 2)], grad_inner * BF16(factor), TN)


def core_halves(core, kept_ref, sent_ref):
    rows = kept_ref.shape[0]
    return [(ref, pl.multiple_of(which * rows, 128)) for ref, which in ((kept_ref, core), (sent_ref, 1 - core))]


def backward_kernel(
    factor, lengths_ref, place_ref, middle_ref, act_ref, grad_inner_ref, mixed_ref, cotangent_ref, outer_bias_ref,
    gain_ref, output_weight_ref, inner_weight_ref, outer_weight_ref,
    layer_ref, grad_middle_ref, grad_mixed_ref, kept_ref, sent_ref, vectors_ref,
):
    mols = mixed_ref.shape[0]
    valid = valid_rows(lengths_ref, 0, mols)
    middle = middle_ref[...]
    normed, inv_std = norm_parts(middle)
    grad_out = cotangent_ref[...].astype(F32) * valid
    grad_inner = grad_inner_ref[...]
    grad_second = dot(grad_inner, inner_weight_ref[...], NT)
    grad_middle = grad_out + norm_back(grad_second * row_of(gain_ref), normed, inv_std)
    grad_middle_ref[...] = grad_middle
    pad = jnp.zeros((WIDE - SLOT, D), F32)
    grads = [jnp.concatenate([grad_middle[i * SLOT : (i + 1) * SLOT], pad]).astype(BF16) for i in range(mols)]
    for i, grad in enumerate(grads):
        grad_mixed_ref[i] = dot(output_weight_ref[...], grad, NT).astype(BF16)
    for target, begin in core_halves(place_ref[0], kept_ref, sent_ref):
        products = [dot(mixed_ref[i, pl.ds(begin, D // 2), :], grad * BF16(factor)) for i, grad in enumerate(grads)]
        target[...] = functools.reduce(jnp.add, products)
    layer = middle + dot(act_ref[...], outer_weight_ref[...]) + row_of(outer_bias_ref)
    layer_ref[...] = (layer * valid).astype(BF16)
    sums = [
        grad_out,
        grad_inner.astype(F32),
        grad_second * normed,
        grad_second,
        grad_middle.astype(BF16).astype(F32),
    ]
    vectors_ref[...] = jnp.zeros_like(vectors_ref)
    for i, values in enumerate(sums):
        vectors_ref[i : i + 1] = jnp.sum(values, 0, keepdims=True) * factor


def back_kernel(
    factor, lengths_ref, place_ref, first_ref, query_ref, keys_ref, values_ref, mixed_ref, grad_ref, stat_ref,
    vectors_ref, turned_grads_ref, kept_ref, sent_ref,
    mixed32_ref, grad32_ref, scores_ref, probs_ref, grads_ref,
):
    step = pl.program_id(0)

    @pl.when(step == 0)
    def start_sums():
        for ref in (grads_ref, kept_ref, sent_ref, vectors_ref):
            ref[...] = jnp.zeros_like(ref)

    mixed32_ref[...] = mixed_ref[0].astype(F32)
    grad32_ref[...] = grad_ref[0].astype(F32)
    lag = 2

    def score(h):
        rows = slice(h * DH, (h + 1) * DH)
        stat = split_row(-stat_ref[0, 0, h : h + 1])
        query = with_rows(query_ref[0, h, :DH].astype(F32), [1.0] + stat)
        scores_ref[h % (lag + 1)] = dot(keys_ref[0, h, :, :SLOT], query, TN)
        grad = grad32_ref[rows]
        shared = split_row(-jnp.sum(grad * mixed32_ref[rows], axis=0, keepdims=True))
        probs_ref[h % (lag + 1)] = dot(values_ref[0, h, :, :SLOT], with_rows(grad, shared), TN)

    def back(h):
        rows = slice(h * DH, (h + 1) * DH)
        probs = jnp.exp2(scores_ref[h % (lag + 1)])
        grad_scores = (probs * probs_ref[h % (lag + 1)]).astype(BF16)
        grad = with_rows(grad32_ref[rows], [])
        grads_ref[0, rows] = dot(keys_ref[0, h, :, :SLOT], grad_scores)[:DH] * SCALE
        grads_ref[1, rows, :SLOT] = dot(query_ref[0, h], grad_scores, NT)[:DH] * LN_2
        grads_ref[2, rows, :SLOT] = dot(grad, probs.astype(BF16), NT)[:DH]

    for h in range(GROUP + lag):
        if h < GROUP:
            score(h)
        if h >= lag:
            back(h - lag)
    grads = grads_ref[...].astype(BF16)
    turned_grads_ref[0] = grads
    grads = (grads * BF16(factor)).reshape(3 * HALF, WIDE)
    for target, begin in core_halves(place_ref[0], kept_ref, sent_ref):
        target[...] += dot(first_ref[0, pl.ds(begin, D // 2), :], grads, NT)
    vectors_ref[...] += dot(jnp.ones((8, WIDE), BF16), grads, NT)


def input_kernel(
    factor, lengths_ref, place_ref, tokens_ref, kinds_ref, table_ref, gain_ref, low_ref, high_ref, query_weight_ref,
    key_weight_ref, value_weight_ref, grad_middle_ref, dense_ref, low_bias_ref, high_bias_ref,
    tokens_grad_ref, vectors_ref,
    edge_ref,
):
    mol = pl.program_id(0)

    @pl.when(mol == 0)
    def start_sums():
        vectors_ref[...] = jnp.zeros_like(vectors_ref)

    kinds_column(kinds_ref, edge_ref)
    edge = edge_ref[pl.ds(pl.multiple_of(mol * SLOT, 8), SLOT), :]
    total = jnp.zeros((D, WIDE), F32)
    for i, weight_ref in enumerate((query_weight_ref, key_weight_ref, value_weight_ref)):
        total = total + dot(weight_ref[...], jnp.concatenate([low_ref[0, i], high_ref[0, i]]))
    grad_first = total.T[:SLOT]
    normed, inv_std = norm_parts(embed(tokens_ref[...], edge, table_ref))
    grad_start = grad_middle_ref[...] + norm_back(grad_first * row_of(gain_ref), normed, inv_std)
    tokens_grad_ref[...] = grad_start.astype(BF16)
    sums = [
        grad_first * normed,
        grad_first,
        jnp.where(edge == 1, 0.0, grad_start),
        jnp.where(edge == 1, grad_start, 0.0),
    ]
    for i, values in enumerate(sums):
        vectors_ref[i : i + 1] += jnp.sum(values, 0, keepdims=True)

    @pl.when(mol == pl.num_programs(0) - 1)
    def finish():
        vectors_ref[...] = vectors_ref[...] * factor
        for i, begin in ((0, 0), (1, 2 * HALF)):
            vectors_ref[4 + i : 5 + i, :HALF] = low_bias_ref[:1, begin : begin + HALF]
            vectors_ref[4 + i : 5 + i, HALF:] = high_bias_ref[:1, begin : begin + HALF]
        vectors_ref[8:16] = dense_ref[...]


def whole(*shape):
    return pl.BlockSpec(shape, lambda i, *_: (0,) * len(shape))


def rows_of(width):
    return pl.BlockSpec((SLOT, width), lambda i, *_: (i, 0))


def mols_of(*shape):
    return pl.BlockSpec((1,) + shape, lambda i, *_: (i,) + (0,) * len(shape))


def shape_of(*shape, dtype=F32):
    return jax.ShapeDtypeStruct(shape, dtype)


def call(kernel, count, in_specs, out_specs, out_shape, scratch, args, flops, name, vmem=VMEM):
    return pl.pallas_call(
        kernel,
        grid_spec=pltpu.PrefetchScalarGridSpec(
            num_scalar_prefetch=2,
            grid=(count,),
            in_specs=in_specs,
            out_specs=out_specs,
            scratch_shapes=scratch,
        ),
        out_shape=out_shape,
        compiler_params=pltpu.CompilerParams(
            dimension_semantics=("arbitrary",), vmem_limit_bytes=vmem
        ),
        cost_estimate=pl.CostEstimate(flops=20 * flops, bytes_accessed=2**20, transcendentals=0),
        name=name,
    )(*args)


def bits_of(mesh_shape):
    narrow = mesh_shape["narrow"].bit_length() - 1
    wide = mesh_shape["wide"].bit_length() - 1
    y = (wide - 1) // 2
    return {
        "c": [0],
        "x": list(range(1, narrow)),
        "y": list(range(narrow, narrow + y)),
        "z": list(range(narrow + y, narrow + wide)),
    }


def swap(values, bit, devices):
    even, odd = bit if isinstance(bit, tuple) else (bit, bit)
    return lax.ppermute(values, AXES, [(i, i ^ (1 << (odd if i & 1 else even))) for i in range(devices)])


def pick(values, *index):
    for i in index:
        values = lax.dynamic_index_in_dim(values, i, 0, keepdims=False)
    return values


def place_kernel(parts, count_in, place_ref, *refs):
    sources = refs[: len(parts)]
    outs, sems = refs[len(parts) + count_in : -1], refs[-1]
    stores = []
    for n, (other, low, targets, column) in enumerate(parts):
        core, first, second = place_ref[0], place_ref[1], place_ref[2]
        if other:
            core, first, second = 1 - core, second, first
        rows = D // 16
        width = sources[n].shape[1] // len(targets)
        for k in range(4):
            row = (
                core,
                lax.bitwise_xor(low, first),
                lax.bitwise_xor(k // 2, second),
                lax.bitwise_xor(k % 2, place_ref[3]),
            )
            for m, target in enumerate(targets):
                stores.append(
                    pltpu.make_async_copy(
                        sources[n].at[k * rows : (k + 1) * rows, m * width : (m + 1) * width],
                        outs[target].at[*row, :, column : column + width],
                        sems.at[n, k, m],
                    )
                )
                stores[-1].start()
    for store in stores:
        store.wait()


def put_in_place(place, pieces, parts, count_out, before=()):
    rows = D // 16
    pieces = [piece.reshape(-1, piece.shape[-1]) for piece in pieces]
    return pl.pallas_call(
        functools.partial(place_kernel, parts, len(before)),
        grid_spec=pltpu.PrefetchScalarGridSpec(
            num_scalar_prefetch=1,
            grid=(1,),
            in_specs=[whole(*piece.shape) for piece in pieces] + [HBM] * len(before),
            out_specs=[HBM] * count_out,
            scratch_shapes=[pltpu.SemaphoreType.DMA((len(pieces), 4, 3))],
        ),
        out_shape=[shape_of(2, 2, 2, 2, rows, D)] * count_out,
        input_output_aliases={1 + len(pieces) + i: i for i in range(len(before))},
        compiler_params=pltpu.CompilerParams(vmem_limit_bytes=20 * 2**20),
        cost_estimate=pl.CostEstimate(flops=10**10, bytes_accessed=2**20, transcendentals=0),
        name="place",
    )(place, *pieces, *before)


def spread_sum(kept, sent, rider, own, bits, me, devices):
    rows, width = kept.shape[0] // 8, kept.shape[1]
    core, x, y, z = (bits[k][0] for k in "cxyz")
    (got,) = yield [(sent, core)]
    terms = [v.reshape(2, 2, 2, rows, width) for v in (kept, got)]
    scatter = (((x, y), me[1]), ((y, x), me[2]), (z, me[3]))
    for bit, mine in scatter:
        (got,) = yield [(functools.reduce(jnp.add, [pick(t, 1 - mine) for t in terms]), bit)]
        terms = [pick(t, mine) for t in terms] + [got]
    total = functools.reduce(jnp.add, terms)
    small = rider()

    def with_small(values):
        return values if small is None else jnp.concatenate([values.reshape(-1, width), small])

    def apart(values, shape):
        if small is None:
            return values, None
        count = math.prod(shape[:-1])
        return values[:count].reshape(shape), small + values[count:]

    for bit in bits["x"][1:] + bits["y"][1:] + bits["z"][1:]:
        (got,) = yield [(with_small(total), bit)]
        got, small = apart(got, total.shape)
        total = total + got
    (got,) = yield [(with_small(total), z)]
    got, small = apart(got, total.shape)
    total = jnp.stack([total, got])
    (got,) = yield [(with_small(total), (y, x))]
    got, small = apart(got, total.shape)
    total = jnp.stack([total, got])
    got, other = yield [(with_small(total), (x, y)), (total, core)]
    got, small = apart(got, total.shape)
    own.extend((total, got))
    (last,) = yield [(with_small(got), core)]
    if small is not None:
        small = small + last[-small.shape[0] :]
    yield (other, last), small


class Order:
    def __init__(self):
        self.before = ()

    def after(self, *values):
        if self.before:
            values, unused = lax.optimization_barrier((values, self.before))
        return values

    def add(self, *values):
        self.before = tuple(values)


class Transfer:
    def __init__(self, name, steps, own, devices, order):
        self.name = name
        self.own = own
        self.level = 0
        self.steps = steps
        self.devices = devices
        self.order = order
        self.result = None
        self.send(next(self.steps))

    def send(self, sent):
        self.order.add(*self.order.before, *[values for values, unused in sent])
        with jax.named_scope(f"{self.name}_{self.level}"):
            self.got = [swap(values, bit, self.devices) for values, bit in sent]
        self.level += 1

    def go(self):
        if self.result is not None:
            return
        sent = self.steps.send(self.order.after(*self.got))
        if isinstance(sent, list):
            self.order.before = ()
            self.send(sent)
        else:
            self.result = sent


def per_device(
    mesh_shape, tokens, kinds, lengths, query_weight, key_weight, value_weight, output_weight, inner_weight,
    outer_weight, query_bias, value_bias, output_bias, inner_bias, outer_bias, first_gain, first_shift,
    second_gain, second_shift, type_table, cotangent,
):
    count = lengths.shape[0]
    rows = tokens.shape[0]
    devices = mesh_shape["wide"] * mesh_shape["narrow"]
    factor = 1.0 / devices
    bits = bits_of(mesh_shape)
    index = lax.axis_index("wide") * mesh_shape["narrow"] + lax.axis_index("narrow")
    at = [(index >> bits[k][0]) & 1 for k in "cxyz"]
    me = [at[0], jnp.where(at[0] == 0, at[1], at[2]), jnp.where(at[0] == 0, at[2], at[1]), at[3]]
    place = jnp.stack(me).astype(jnp.int32)
    unit = 2 * rows * D * D
    attention = 2 * rows * SLOT * D
    vec = pl.BlockSpec((D,), lambda i, *_: (0,))
    weight = whole(D, D)
    edges = pl.BlockSpec((rows,), lambda i, *_: (0,))
    column = pltpu.VMEM((rows, 1), F32)
    scalars = (lengths, place)
    once = pl.Buffered(1)
    single = lambda *shape: pl.BlockSpec(shape, lambda i, *_: (0,) * len(shape), pipeline_mode=once)
    now = lambda *shape: pl.BlockSpec((1,) + shape, lambda i, *_: (jnp.minimum(i, count - 1),) + (0,) * len(shape))
    low = pltpu.VMEM((rows, D), BF16)
    room = pltpu.VMEM((D, D), BF16)
    first, query, keys, values, mixed, stat, middle, act, grad_inner, *dense_parts = call(
        functools.partial(attend_kernel, factor), count + 1,
        [pl.BlockSpec((SLOT, D), lambda i, *_: (jnp.minimum(i, count - 1), 0)), edges, whole(2, D), vec, vec, vec, vec,
         single(D, D), single(D, D), single(D, D), vec, vec, vec, vec] + [HBM] * 5,
        [now(D, WIDE)] + [now(H, 32, WIDE)] * 3 + [now(D, WIDE), now(2, GROUP, WIDE)] + [single(rows, D)] * 3
        + [single(D // 2, 2 * D)] * 2,
        [shape_of(count, D, WIDE, dtype=BF16)] + [shape_of(count, H, 32, WIDE, dtype=BF16)] * 3
        + [shape_of(count, D, WIDE, dtype=BF16), shape_of(count, 2, GROUP, WIDE), shape_of(rows, D),
           shape_of(rows, D, dtype=BF16), shape_of(rows, D, dtype=BF16)] + [shape_of(D // 2, 2 * D)] * 2,
        [column, pltpu.VMEM((8, SLOT, WIDE), F32), pltpu.VMEM((D, WIDE), F32), pltpu.VMEM((count, D, WIDE), BF16), low,
         low, low, room, room, room, pltpu.SemaphoreType.DMA((5,))],
        (*scalars, tokens, kinds, type_table, first_gain, first_shift, query_bias, value_bias, query_weight,
         key_weight, value_weight, output_bias, inner_bias, second_gain, second_shift, tokens, cotangent,
         output_weight, inner_weight, outer_weight),
        flops=8 * unit + 20 * attention, name="attend",
    )
    mols = count
    tall = lambda width: pl.BlockSpec((mols * SLOT, width), lambda i, *_: (i, 0))
    several = pl.BlockSpec((mols, D, WIDE), lambda i, *_: (i, 0, 0))
    halves = lambda width: [whole(D // 2, width)] * 2
    half_shapes = lambda width: [shape_of(D // 2, width)] * 2
    wide = 3 * HALF
    order = Order()
    transfers, made, placed = {}, {}, {}

    def begin(name):
        kept, sent = made[name]
        (sent,) = order.after(sent)
        order.before = ()
        rider = (lambda: made["input"][1]) if name == "O" else (lambda: None)
        own = []
        steps = spread_sum(kept, sent, rider, own, bits, me, devices)
        transfers[name] = Transfer(f"sum_{name}", steps, own, devices, order)

    def spread(name, *parts):
        made[name] = parts

    def dense_forward():
        order.add(act)
        spread("A", *dense_parts)

    def dense_backward():
        (act_in,) = order.after(act)
        layer_out, grad_middle, grad_mixed, *parts, dense_vectors = call(
            functools.partial(backward_kernel, factor), count // mols,
            [tall(D), tall(D), tall(D), several, tall(D), vec, vec, weight, weight, weight],
            [tall(D), tall(D), several] + halves(D) + [whole(8, D)],
            [shape_of(rows, D, dtype=BF16), shape_of(rows, D), shape_of(count, D, WIDE, dtype=BF16)] + half_shapes(D)
            + [shape_of(8, D)],
            [],
            (*scalars, middle, act_in, grad_inner, mixed, cotangent, outer_bias, second_gain, output_weight,
             inner_weight, outer_weight),
            flops=4 * unit, name="dense_backward",
        )
        made["backward"] = layer_out, grad_middle, grad_mixed, dense_vectors
        order.add(dense_vectors)
        spread("O", *parts)

    def back(part):
        heads = pl.BlockSpec((1, GROUP, 32, WIDE), lambda i, *_: (i, part, 0, 0))
        half = pl.BlockSpec((1, HALF, WIDE), lambda i, *_: (i, part, 0))
        (grad_in,) = order.after(made["backward"][2])
        bias_grad, turned_grads, *parts = call(
            functools.partial(back_kernel, factor), count,
            [mols_of(D, WIDE), heads, heads, heads, half, half,
             pl.BlockSpec((1, 1, GROUP, WIDE), lambda i, *_: (i, part, 0, 0))],
            [whole(8, wide), mols_of(3, HALF, WIDE)] + halves(wide),
            [shape_of(8, wide), shape_of(count, 3, HALF, WIDE, dtype=BF16)] + half_shapes(wide),
            [pltpu.VMEM((HALF, WIDE), F32)] * 2 + [pltpu.VMEM((3, SLOT, WIDE), F32)] * 2
            + [pltpu.VMEM((3, HALF, WIDE), F32)],
            (*scalars, first, query, keys, values, mixed, grad_in, stat),
            flops=unit + 20 * attention, name=f"back_{part}",
        )
        made[part] = turned_grads, bias_grad
        order.add(bias_grad)
        spread("BC"[part], *parts)

    def to_input():
        layer_out, grad_middle, grad_mixed, dense_vectors = made["backward"]
        (grad_middle,) = order.after(grad_middle)
        made["input"] = call(
            functools.partial(input_kernel, factor), count,
            [rows_of(D), edges, whole(2, D), vec, mols_of(3, HALF, WIDE), mols_of(3, HALF, WIDE), weight, weight,
             weight, rows_of(D), whole(8, D), whole(8, wide), whole(8, wide)],
            [rows_of(D), whole(16, D)],
            [shape_of(rows, D, dtype=BF16), shape_of(16, D)],
            [column],
            (*scalars, tokens, kinds, type_table, first_gain, made[0][0], made[1][0], query_weight, key_weight,
             value_weight, grad_middle, dense_vectors, made[0][1], made[1][1]),
            flops=3 * unit, name="input",
        )
        order.add(made["input"][1])

    def own_parts(name, targets, column=0):
        while not transfers[name].own:
            transfers[name].go()
        return [(piece, (0, low, targets, column)) for low, piece in enumerate(transfers[name].own)]

    def other_parts(name, targets, column=0):
        while transfers[name].result is None:
            transfers[name].go()
        return [(piece, (1, low, targets, column)) for low, piece in enumerate(transfers[name].result[0])]

    def into_place(step):
        before, three = (), (0, 1, 2)
        if step == "a":
            found = other_parts("A", (0, 1)) + own_parts("A", (0, 1))
        elif step == "o":
            found = other_parts("O", (0,)) + own_parts("O", (0,))
        elif step == "b":
            found = other_parts("B", three) + own_parts("B", three)
        elif step == "q":
            found, before = own_parts("C", three, HALF), placed["b"]
        else:
            found, before = other_parts("C", three, HALF), placed["q"]
        pieces, parts = zip(*found)
        placed[step] = put_in_place(
            place, order.after(*pieces), parts, {"a": 2, "o": 1}.get(step, 3), before
        )
        order.add(placed[step][0])

    def finish_vectors():
        if "vectors" not in made:
            small = transfers["O"].result[1]
            made["vectors"] = [small[i] for i in (4, 5, 12, 9, 8, 0, 1, 10, 11)] + [small[2:4]]
            order.add(*order.before, *made["vectors"])

    kernels = {"F": dense_forward, "D": dense_backward, "0": lambda: back(0), "1": lambda: back(1), "I": to_input}
    for step in SCHEDULE:
        if step in kernels:
            kernels[step]()
        elif step in "wxyz":
            begin("AOBC"["wxyz".index(step)])
        elif step in transfers:
            transfers[step].go()
            if step == "O" and transfers[step].result is not None:
                finish_vectors()
        else:
            into_place(step)
    outer_grad, inner_grad = placed["a"]
    (output_grad,) = placed["o"]
    query_grad, key_grad, value_grad = placed["r"]
    layer_out = made["backward"][0]
    tokens_grad = made["input"][0]
    finish_vectors()
    return tuple(
        [layer_out, tokens_grad]
        + [grad.reshape(D, D) for grad in (query_grad, key_grad, value_grad, output_grad, inner_grad, outer_grad)]
        + made["vectors"]
    )


def solution(mesh):
    split = P(AXES, None)
    return jax.shard_map(
        functools.partial(per_device, dict(mesh.shape)),
        mesh=mesh,
        in_specs=(split, P(AXES), P(AXES)) + (P(),) * 16 + (split,),
        out_specs=(split, split) + (P(),) * 16,
        check_vma=False,
    )
```

```python
import functools
import math

import jax
import jax.numpy as jnp
import numpy as np
from jax import lax
from jax.experimental import pallas as pl
from jax.experimental.pallas import tpu as pltpu
from jax.sharding import PartitionSpec as P

D = 768
H = 32
DH = 24
SLOT = 208
GROUP = 16
HALF = GROUP * DH
WIDE = 256
SCALE = 1.0 / math.sqrt(DH)
LOG_SCALE = math.log2(math.e) / math.sqrt(DH)
LN_2 = math.log(2.0)
AXES = ("wide", "narrow")
NN = (((1,), (0,)), ((), ()))
NT = (((1,), (1,)), ((), ()))
TN = (((0,), (0,)), ((), ()))
F32 = jnp.float32
BF16 = jnp.bfloat16
VMEM = 60 * 2**20
HBM = pl.BlockSpec(memory_space=pltpu.HBM)


SCHEDULE = "FwDAx0OA1yOAzBOCAIOBACOBACBOACOBCBACOBOAoaCBBbCqCr"


def dot(left, right, dims=NN):
    return lax.dot_general(left, right, dims, preferred_element_type=F32)


def norm_parts(values):
    average = jnp.mean(values, -1, keepdims=True)
    centered = values - average
    inv_std = lax.rsqrt(jnp.mean(centered * centered, -1, keepdims=True) + 1e-05)
    return centered * inv_std, inv_std


def norm_back(grad_hat, normed, inv_std):
    return (
        grad_hat
        - jnp.mean(grad_hat, -1, keepdims=True)
        - normed * jnp.mean(grad_hat * normed, -1, keepdims=True)
    ) * inv_std


def row_of(ref):
    return ref[...].astype(F32).reshape(1, D)


def kinds_column(kinds_ref, edge_ref):
    @pl.when(pl.program_id(0) == 0)
    def turn():
        kinds = kinds_ref[...].astype(F32).reshape(1, -1)
        edge_ref[...] = jnp.broadcast_to(kinds, (8, kinds.shape[1])).T[:, :1]


def embed(tokens, edge, table_ref):
    table = table_ref[...].astype(F32)
    return tokens.astype(F32) + jnp.where(edge == 1, table[1:2], table[0:1])


def turn(values):
    return jnp.concatenate([values, jnp.zeros((WIDE - SLOT, values.shape[1]), F32)]).T


def with_rows(values, rows):
    index = lax.broadcasted_iota(jnp.int32, (8, WIDE), 0)
    extra = jnp.zeros((8, WIDE), F32)
    for i, row in enumerate(rows):
        extra = jnp.where(index == i, row, extra)
    if values.ndim == 3:
        extra = jnp.broadcast_to(extra, (values.shape[0], 8, WIDE))
    return jnp.concatenate([values, extra], -2).astype(BF16)


def split_row(row):
    high = row.astype(BF16).astype(F32)
    mid = (row - high).astype(BF16).astype(F32)
    return [high, mid, row - high - mid]


def attend_kernel(
    factor, lengths_ref, place_ref, tokens_ref, kinds_ref, table_ref, gain_ref, shift_ref, query_bias_ref,
    value_bias_ref, query_weight_ref, key_weight_ref, value_weight_ref, output_bias_ref, inner_bias_ref,
    second_gain_ref, second_shift_ref, *refs,
):
    later_hbm, refs = refs[:5], refs[5:]
    first_ref, query_ref, keys_ref, values_ref, mixed_ref, stat_ref, *outputs = refs[:11]
    edge_ref, scores_ref, out_ref, mixed_all_ref, second_ref, *later, sems = refs[11:]
    mol = pl.program_id(0)
    copies = [pltpu.make_async_copy(*pair, sems.at[k]) for k, pair in enumerate(zip(later_hbm, later))]

    @pl.when(mol == 0)
    def fetch():
        for copy in copies:
            copy.start()

    kinds_column(kinds_ref, edge_ref)

    @pl.when(mol < pl.num_programs(0) - 1)
    def attend():
        attend_molecule(
            mol, lengths_ref, tokens_ref, edge_ref, table_ref, gain_ref, shift_ref, query_bias_ref, value_bias_ref,
            query_weight_ref, key_weight_ref, value_weight_ref, first_ref, query_ref, keys_ref, values_ref, mixed_ref,
            stat_ref, scores_ref, out_ref,
        )
        mixed_all_ref[mol] = mixed_ref[0]

    @pl.when(mol == pl.num_programs(0) - 1)
    def forward():
        for copy in copies:
            copy.wait()
        feed_forward(
            factor, lengths_ref, place_ref, edge_ref, table_ref, mixed_all_ref, *later, output_bias_ref,
            inner_bias_ref, second_gain_ref, second_shift_ref, *outputs, second_ref,
        )


def attend_molecule(
    mol, lengths_ref, tokens_ref, edge_ref, table_ref, gain_ref, shift_ref, query_bias_ref, value_bias_ref,
    query_weight_ref, key_weight_ref, value_weight_ref, first_ref, query_ref, keys_ref, values_ref, mixed_ref,
    stat_ref, scores_ref, out_ref,
):
    edge = edge_ref[pl.ds(pl.multiple_of(mol * SLOT, 8), SLOT), :]
    normed, unused = norm_parts(embed(tokens_ref[...], edge, table_ref))
    first32 = normed * row_of(gain_ref) + row_of(shift_ref)
    first = first32.astype(BF16)
    first_ref[0] = turn(first32).astype(BF16)
    slot = lax.broadcasted_iota(jnp.int32, (1, WIDE), 1)
    bias = jnp.where(slot < lengths_ref[mol], 0.0, -1e30)
    ones = jnp.ones((1, WIDE), F32)
    query = (dot(first, query_weight_ref[...]) + row_of(query_bias_ref)) * LOG_SCALE
    keys = dot(first, key_weight_ref[...])
    values = dot(first, value_weight_ref[...]) + row_of(value_bias_ref)
    query_ref[0] = with_rows(turn(query).reshape(H, DH, WIDE), [ones])
    keys_ref[0] = with_rows(turn(keys).reshape(H, DH, WIDE), [bias, ones, ones, ones])
    values_ref[0] = with_rows(turn(values).reshape(H, DH, WIDE), [ones, ones, ones])
    lag = 7

    def score(h):
        scores_ref[h % (lag + 1)] = dot(keys_ref[0, h, :, :SLOT], query_ref[0, h], TN)

    def mix(h):
        scores = scores_ref[h % (lag + 1)]
        top = jnp.max(scores, axis=0, keepdims=True)
        powered = jnp.exp2(scores - top).astype(BF16)
        out = dot(values_ref[0, h, :, :SLOT], powered)
        total = out[DH : DH + 1]
        out_ref[h * DH : (h + 1) * DH, :] = out[:DH] * (1.0 / total)
        stat_ref[0, h // GROUP, h % GROUP : h % GROUP + 1] = top + jnp.log2(total)

    for h in range(H + lag):
        if h < H:
            score(h)
        if h >= lag:
            mix(h - lag)
    mixed_ref[0] = out_ref[...].astype(BF16)


def gelu_parts(inner):
    root = math.sqrt(2.0 / math.pi)
    bend = root * 0.044715 * inner * inner + root
    half = 0.5 * jnp.tanh(inner * bend) + 0.5
    act = inner * half
    return act, half + act * (1.0 - half) * (6.0 * bend - 4.0 * root)


def valid_rows(lengths_ref, first, mols):
    slot = lax.broadcasted_iota(jnp.int32, (SLOT, 1), 0)
    return jnp.concatenate([(slot < lengths_ref[first + i]).astype(F32) for i in range(mols)])


def feed_forward(
    factor, lengths_ref, place_ref, edge_ref, table_ref, mixed_ref, tokens_ref, cotangent_ref, output_weight_ref,
    inner_weight_ref, outer_weight_ref, output_bias_ref, inner_bias_ref, gain_ref, shift_ref,
    middle_ref, act_ref, grad_inner_ref, kept_ref, sent_ref, second_ref,
):
    mols = mixed_ref.shape[0]
    edge = edge_ref[...]
    valid = valid_rows(lengths_ref, 0, mols)
    mixed = jnp.concatenate([dot(mixed_ref[i], output_weight_ref[...], TN)[:SLOT] for i in range(mols)])
    middle = embed(tokens_ref[...], edge, table_ref) + mixed + row_of(output_bias_ref)
    middle_ref[...] = middle
    normed, unused = norm_parts(middle)
    second = (normed * row_of(gain_ref) + row_of(shift_ref)).astype(BF16)
    inner = dot(second, inner_weight_ref[...]) + row_of(inner_bias_ref)
    act32, slope = gelu_parts(inner)
    act = act32.astype(BF16)
    act_ref[...] = act
    grad_low = (cotangent_ref[...].astype(F32) * valid).astype(BF16)
    grad_inner = (dot(grad_low, outer_weight_ref[...], NT) * slope).astype(BF16)
    grad_inner_ref[...] = grad_inner

    second_ref[...] = second
    for target, begin in core_halves(place_ref[0], kept_ref, sent_ref):
        target[:, :D] = dot(act_ref[:, pl.ds(begin, D // 2)], grad_low * BF16(factor), TN)
        target[:, D:] = dot(second_ref[:, pl.ds(begin, D // 2)], grad_inner * BF16(factor), TN)


def core_halves(core, kept_ref, sent_ref):
    rows = kept_ref.shape[0]
    return [(ref, pl.multiple_of(which * rows, 128)) for ref, which in ((kept_ref, core), (sent_ref, 1 - core))]


def backward_kernel(
    factor, lengths_ref, place_ref, middle_ref, act_ref, grad_inner_ref, mixed_ref, cotangent_ref, outer_bias_ref,
    gain_ref, output_weight_ref, inner_weight_ref, outer_weight_ref,
    layer_ref, grad_middle_ref, grad_mixed_ref, kept_ref, sent_ref, vectors_ref,
):
    mols = mixed_ref.shape[0]
    valid = valid_rows(lengths_ref, 0, mols)
    middle = middle_ref[...]
    normed, inv_std = norm_parts(middle)
    grad_out = cotangent_ref[...].astype(F32) * valid
    grad_inner = grad_inner_ref[...]
    grad_second = dot(grad_inner, inner_weight_ref[...], NT)
    grad_middle = grad_out + norm_back(grad_second * row_of(gain_ref), normed, inv_std)
    grad_middle_ref[...] = grad_middle
    pad = jnp.zeros((WIDE - SLOT, D), F32)
    grads = [jnp.concatenate([grad_middle[i * SLOT : (i + 1) * SLOT], pad]).astype(BF16) for i in range(mols)]
    for i, grad in enumerate(grads):
        grad_mixed_ref[i] = dot(output_weight_ref[...], grad, NT).astype(BF16)
    for target, begin in core_halves(place_ref[0], kept_ref, sent_ref):
        products = [dot(mixed_ref[i, pl.ds(begin, D // 2), :], grad * BF16(factor)) for i, grad in enumerate(grads)]
        target[...] = functools.reduce(jnp.add, products)
    layer = middle + dot(act_ref[...], outer_weight_ref[...]) + row_of(outer_bias_ref)
    layer_ref[...] = (layer * valid).astype(BF16)
    sums = [
        grad_out,
        grad_inner.astype(F32),
        grad_second * normed,
        grad_second,
        grad_middle.astype(BF16).astype(F32),
    ]
    vectors_ref[...] = jnp.zeros_like(vectors_ref)
    for i, values in enumerate(sums):
        vectors_ref[i : i + 1] = jnp.sum(values, 0, keepdims=True) * factor


def back_kernel(
    factor, lengths_ref, place_ref, first_ref, query_ref, keys_ref, values_ref, mixed_ref, grad_ref, stat_ref,
    vectors_ref, turned_grads_ref, kept_ref, sent_ref,
    mixed32_ref, grad32_ref, scores_ref, probs_ref, grads_ref,
):
    step = pl.program_id(0)

    @pl.when(step == 0)
    def start_sums():
        for ref in (grads_ref, kept_ref, sent_ref, vectors_ref):
            ref[...] = jnp.zeros_like(ref)

    mixed32_ref[...] = mixed_ref[0].astype(F32)
    grad32_ref[...] = grad_ref[0].astype(F32)
    lag = 2

    def score(h):
        rows = slice(h * DH, (h + 1) * DH)
        stat = split_row(-stat_ref[0, 0, h : h + 1])
        query = with_rows(query_ref[0, h, :DH].astype(F32), [1.0] + stat)
        scores_ref[h % (lag + 1)] = dot(keys_ref[0, h, :, :SLOT], query, TN)
        grad = grad32_ref[rows]
        shared = split_row(-jnp.sum(grad * mixed32_ref[rows], axis=0, keepdims=True))
        probs_ref[h % (lag + 1)] = dot(values_ref[0, h, :, :SLOT], with_rows(grad, shared), TN)

    def back(h):
        rows = slice(h * DH, (h + 1) * DH)
        probs = jnp.exp2(scores_ref[h % (lag + 1)])
        grad_scores = (probs * probs_ref[h % (lag + 1)]).astype(BF16)
        grad = with_rows(grad32_ref[rows], [])
        grads_ref[0, rows] = dot(keys_ref[0, h, :, :SLOT], grad_scores)[:DH] * SCALE
        grads_ref[1, rows, :SLOT] = dot(query_ref[0, h], grad_scores, NT)[:DH] * LN_2
        grads_ref[2, rows, :SLOT] = dot(grad, probs.astype(BF16), NT)[:DH]

    for h in range(GROUP + lag):
        if h < GROUP:
            score(h)
        if h >= lag:
            back(h - lag)
    grads = grads_ref[...].astype(BF16)
    turned_grads_ref[0] = grads
    grads = (grads * BF16(factor)).reshape(3 * HALF, WIDE)
    for target, begin in core_halves(place_ref[0], kept_ref, sent_ref):
        target[...] += dot(first_ref[0, pl.ds(begin, D // 2), :], grads, NT)
    vectors_ref[...] += dot(jnp.ones((8, WIDE), BF16), grads, NT)


def input_kernel(
    factor, lengths_ref, place_ref, tokens_ref, kinds_ref, table_ref, gain_ref, low_ref, high_ref, query_weight_ref,
    key_weight_ref, value_weight_ref, grad_middle_ref, dense_ref, low_bias_ref, high_bias_ref,
    tokens_grad_ref, vectors_ref,
    edge_ref,
):
    mol = pl.program_id(0)

    @pl.when(mol == 0)
    def start_sums():
        vectors_ref[...] = jnp.zeros_like(vectors_ref)

    kinds_column(kinds_ref, edge_ref)
    edge = edge_ref[pl.ds(pl.multiple_of(mol * SLOT, 8), SLOT), :]
    total = jnp.zeros((D, WIDE), F32)
    for i, weight_ref in enumerate((query_weight_ref, key_weight_ref, value_weight_ref)):
        total = total + dot(weight_ref[...], jnp.concatenate([low_ref[0, i], high_ref[0, i]]))
    grad_first = total.T[:SLOT]
    normed, inv_std = norm_parts(embed(tokens_ref[...], edge, table_ref))
    grad_start = grad_middle_ref[...] + norm_back(grad_first * row_of(gain_ref), normed, inv_std)
    tokens_grad_ref[...] = grad_start.astype(BF16)
    sums = [
        grad_first * normed,
        grad_first,
        jnp.where(edge == 1, 0.0, grad_start),
        jnp.where(edge == 1, grad_start, 0.0),
    ]
    for i, values in enumerate(sums):
        vectors_ref[i : i + 1] += jnp.sum(values, 0, keepdims=True)

    @pl.when(mol == pl.num_programs(0) - 1)
    def finish():
        vectors_ref[...] = vectors_ref[...] * factor
        for i, begin in ((0, 0), (1, 2 * HALF)):
            vectors_ref[4 + i : 5 + i, :HALF] = low_bias_ref[:1, begin : begin + HALF]
            vectors_ref[4 + i : 5 + i, HALF:] = high_bias_ref[:1, begin : begin + HALF]
        vectors_ref[8:16] = dense_ref[...]


def whole(*shape):
    return pl.BlockSpec(shape, lambda i, *_: (0,) * len(shape))


def rows_of(width):
    return pl.BlockSpec((SLOT, width), lambda i, *_: (i, 0))


def mols_of(*shape):
    return pl.BlockSpec((1,) + shape, lambda i, *_: (i,) + (0,) * len(shape))


def shape_of(*shape, dtype=F32):
    return jax.ShapeDtypeStruct(shape, dtype)


def call(kernel, count, in_specs, out_specs, out_shape, scratch, args, flops, name, vmem=VMEM):
    return pl.pallas_call(
        kernel,
        grid_spec=pltpu.PrefetchScalarGridSpec(
            num_scalar_prefetch=2,
            grid=(count,),
            in_specs=in_specs,
            out_specs=out_specs,
            scratch_shapes=scratch,
        ),
        out_shape=out_shape,
        compiler_params=pltpu.CompilerParams(
            dimension_semantics=("arbitrary",), vmem_limit_bytes=vmem
        ),
        cost_estimate=pl.CostEstimate(flops=20 * flops, bytes_accessed=2**20, transcendentals=0),
        name=name,
    )(*args)


def bits_of(mesh_shape):
    narrow = mesh_shape["narrow"].bit_length() - 1
    wide = mesh_shape["wide"].bit_length() - 1
    y = (wide - 1) // 2
    return {
        "c": [0],
        "x": list(range(1, narrow)),
        "y": list(range(narrow, narrow + y)),
        "z": list(range(narrow + y, narrow + wide)),
    }


def swap(values, bit, devices):
    even, odd = bit if isinstance(bit, tuple) else (bit, bit)
    return lax.ppermute(values, AXES, [(i, i ^ (1 << (odd if i & 1 else even))) for i in range(devices)])


def pick(values, *index):
    for i in index:
        values = lax.dynamic_index_in_dim(values, i, 0, keepdims=False)
    return values


def place_kernel(parts, count_in, place_ref, *refs):
    sources = refs[: len(parts)]
    outs, sems = refs[len(parts) + count_in : -1], refs[-1]
    stores = []
    for n, (other, low, targets, column) in enumerate(parts):
        core, first, second = place_ref[0], place_ref[1], place_ref[2]
        if other:
            core, first, second = 1 - core, second, first
        rows = D // 16
        width = sources[n].shape[1] // len(targets)
        for k in range(4):
            row = (
                core,
                lax.bitwise_xor(low, first),
                lax.bitwise_xor(k // 2, second),
                lax.bitwise_xor(k % 2, place_ref[3]),
            )
            for m, target in enumerate(targets):
                stores.append(
                    pltpu.make_async_copy(
                        sources[n].at[k * rows : (k + 1) * rows, m * width : (m + 1) * width],
                        outs[target].at[*row, :, column : column + width],
                        sems.at[n, k, m],
                    )
                )
                stores[-1].start()
    for store in stores:
        store.wait()


def put_in_place(place, pieces, parts, count_out, before=()):
    rows = D // 16
    pieces = [piece.reshape(-1, piece.shape[-1]) for piece in pieces]
    return pl.pallas_call(
        functools.partial(place_kernel, parts, len(before)),
        grid_spec=pltpu.PrefetchScalarGridSpec(
            num_scalar_prefetch=1,
            grid=(1,),
            in_specs=[whole(*piece.shape) for piece in pieces] + [HBM] * len(before),
            out_specs=[HBM] * count_out,
            scratch_shapes=[pltpu.SemaphoreType.DMA((len(pieces), 4, 3))],
        ),
        out_shape=[shape_of(2, 2, 2, 2, rows, D)] * count_out,
        input_output_aliases={1 + len(pieces) + i: i for i in range(len(before))},
        compiler_params=pltpu.CompilerParams(vmem_limit_bytes=20 * 2**20),
        cost_estimate=pl.CostEstimate(flops=10**10, bytes_accessed=2**20, transcendentals=0),
        name="place",
    )(place, *pieces, *before)


def spread_sum(kept, sent, rider, own, bits, me, devices):
    rows, width = kept.shape[0] // 8, kept.shape[1]
    core, x, y, z = (bits[k][0] for k in "cxyz")
    (got,) = yield [(sent, core)]
    terms = [v.reshape(2, 2, 2, rows, width) for v in (kept, got)]
    scatter = (((x, y), me[1]), ((y, x), me[2]), (z, me[3]))
    for bit, mine in scatter:
        (got,) = yield [(functools.reduce(jnp.add, [pick(t, 1 - mine) for t in terms]), bit)]
        terms = [pick(t, mine) for t in terms] + [got]
    total = functools.reduce(jnp.add, terms)
    small = rider()

    def with_small(values):
        return values if small is None else jnp.concatenate([values.reshape(-1, width), small])

    def apart(values, shape):
        if small is None:
            return values, None
        count = math.prod(shape[:-1])
        return values[:count].reshape(shape), small + values[count:]

    for bit in bits["x"][1:] + bits["y"][1:] + bits["z"][1:]:
        (got,) = yield [(with_small(total), bit)]
        got, small = apart(got, total.shape)
        total = total + got
    (got,) = yield [(with_small(total), z)]
    got, small = apart(got, total.shape)
    total = jnp.stack([total, got])
    (got,) = yield [(with_small(total), (y, x))]
    got, small = apart(got, total.shape)
    total = jnp.stack([total, got])
    got, other = yield [(with_small(total), (x, y)), (total, core)]
    got, small = apart(got, total.shape)
    own.extend((total, got))
    (last,) = yield [(with_small(got), core)]
    if small is not None:
        small = small + last[-small.shape[0] :]
    yield (other, last), small


class Order:
    def __init__(self):
        self.before = ()

    def after(self, *values):
        if self.before:
            values, unused = lax.optimization_barrier((values, self.before))
        return values

    def add(self, *values):
        self.before = tuple(values)


class Transfer:
    def __init__(self, name, steps, own, devices, order):
        self.name = name
        self.own = own
        self.level = 0
        self.steps = steps
        self.devices = devices
        self.order = order
        self.result = None
        self.send(next(self.steps))

    def send(self, sent):
        self.order.add(*self.order.before, *[values for values, unused in sent])
        with jax.named_scope(f"{self.name}_{self.level}"):
            self.got = [swap(values, bit, self.devices) for values, bit in sent]
        self.level += 1

    def go(self):
        if self.result is not None:
            return
        sent = self.steps.send(self.order.after(*self.got))
        if isinstance(sent, list):
            self.order.before = ()
            self.send(sent)
        else:
            self.result = sent


def per_device(
    mesh_shape, tokens, kinds, lengths, query_weight, key_weight, value_weight, output_weight, inner_weight,
    outer_weight, query_bias, value_bias, output_bias, inner_bias, outer_bias, first_gain, first_shift,
    second_gain, second_shift, type_table, cotangent,
):
    count = lengths.shape[0]
    rows = tokens.shape[0]
    devices = mesh_shape["wide"] * mesh_shape["narrow"]
    factor = 1.0 / devices
    bits = bits_of(mesh_shape)
    index = lax.axis_index("wide") * mesh_shape["narrow"] + lax.axis_index("narrow")
    at = [(index >> bits[k][0]) & 1 for k in "cxyz"]
    me = [at[0], jnp.where(at[0] == 0, at[1], at[2]), jnp.where(at[0] == 0, at[2], at[1]), at[3]]
    place = jnp.stack(me).astype(jnp.int32)
    unit = 2 * rows * D * D
    attention = 2 * rows * SLOT * D
    vec = pl.BlockSpec((D,), lambda i, *_: (0,))
    weight = whole(D, D)
    edges = pl.BlockSpec((rows,), lambda i, *_: (0,))
    column = pltpu.VMEM((rows, 1), F32)
    scalars = (lengths, place)
    once = pl.Buffered(1)
    single = lambda *shape: pl.BlockSpec(shape, lambda i, *_: (0,) * len(shape), pipeline_mode=once)
    now = lambda *shape: pl.BlockSpec((1,) + shape, lambda i, *_: (jnp.minimum(i, count - 1),) + (0,) * len(shape))
    low = pltpu.VMEM((rows, D), BF16)
    room = pltpu.VMEM((D, D), BF16)
    first, query, keys, values, mixed, stat, middle, act, grad_inner, *dense_parts = call(
        functools.partial(attend_kernel, factor), count + 1,
        [pl.BlockSpec((SLOT, D), lambda i, *_: (jnp.minimum(i, count - 1), 0)), edges, whole(2, D), vec, vec, vec, vec,
         single(D, D), single(D, D), single(D, D), vec, vec, vec, vec] + [HBM] * 5,
        [now(D, WIDE)] + [now(H, 32, WIDE)] * 3 + [now(D, WIDE), now(2, GROUP, WIDE)] + [single(rows, D)] * 3
        + [single(D // 2, 2 * D)] * 2,
        [shape_of(count, D, WIDE, dtype=BF16)] + [shape_of(count, H, 32, WIDE, dtype=BF16)] * 3
        + [shape_of(count, D, WIDE, dtype=BF16), shape_of(count, 2, GROUP, WIDE), shape_of(rows, D),
           shape_of(rows, D, dtype=BF16), shape_of(rows, D, dtype=BF16)] + [shape_of(D // 2, 2 * D)] * 2,
        [column, pltpu.VMEM((8, SLOT, WIDE), F32), pltpu.VMEM((D, WIDE), F32), pltpu.VMEM((count, D, WIDE), BF16), low,
         low, low, room, room, room, pltpu.SemaphoreType.DMA((5,))],
        (*scalars, tokens, kinds, type_table, first_gain, first_shift, query_bias, value_bias, query_weight,
         key_weight, value_weight, output_bias, inner_bias, second_gain, second_shift, tokens, cotangent,
         output_weight, inner_weight, outer_weight),
        flops=8 * unit + 20 * attention, name="attend",
    )
    mols = count
    tall = lambda width: pl.BlockSpec((mols * SLOT, width), lambda i, *_: (i, 0))
    several = pl.BlockSpec((mols, D, WIDE), lambda i, *_: (i, 0, 0))
    halves = lambda width: [whole(D // 2, width)] * 2
    half_shapes = lambda width: [shape_of(D // 2, width)] * 2
    wide = 3 * HALF
    order = Order()
    transfers, made, placed = {}, {}, {}

    def begin(name):
        kept, sent = made[name]
        (sent,) = order.after(sent)
        order.before = ()
        rider = (lambda: made["input"][1]) if name == "O" else (lambda: None)
        own = []
        steps = spread_sum(kept, sent, rider, own, bits, me, devices)
        transfers[name] = Transfer(f"sum_{name}", steps, own, devices, order)

    def spread(name, *parts):
        made[name] = parts

    def dense_forward():
        order.add(act)
        spread("A", *dense_parts)

    def dense_backward():
        (act_in,) = order.after(act)
        layer_out, grad_middle, grad_mixed, *parts, dense_vectors = call(
            functools.partial(backward_kernel, factor), count // mols,
            [tall(D), tall(D), tall(D), several, tall(D), vec, vec, weight, weight, weight],
            [tall(D), tall(D), several] + halves(D) + [whole(8, D)],
            [shape_of(rows, D, dtype=BF16), shape_of(rows, D), shape_of(count, D, WIDE, dtype=BF16)] + half_shapes(D)
            + [shape_of(8, D)],
            [],
            (*scalars, middle, act_in, grad_inner, mixed, cotangent, outer_bias, second_gain, output_weight,
             inner_weight, outer_weight),
            flops=4 * unit, name="dense_backward",
        )
        made["backward"] = layer_out, grad_middle, grad_mixed, dense_vectors
        order.add(dense_vectors)
        spread("O", *parts)

    def back(part):
        heads = pl.BlockSpec((1, GROUP, 32, WIDE), lambda i, *_: (i, part, 0, 0))
        half = pl.BlockSpec((1, HALF, WIDE), lambda i, *_: (i, part, 0))
        (grad_in,) = order.after(made["backward"][2])
        bias_grad, turned_grads, *parts = call(
            functools.partial(back_kernel, factor), count,
            [mols_of(D, WIDE), heads, heads, heads, half, half,
             pl.BlockSpec((1, 1, GROUP, WIDE), lambda i, *_: (i, part, 0, 0))],
            [whole(8, wide), mols_of(3, HALF, WIDE)] + halves(wide),
            [shape_of(8, wide), shape_of(count, 3, HALF, WIDE, dtype=BF16)] + half_shapes(wide),
            [pltpu.VMEM((HALF, WIDE), F32)] * 2 + [pltpu.VMEM((3, SLOT, WIDE), F32)] * 2
            + [pltpu.VMEM((3, HALF, WIDE), F32)],
            (*scalars, first, query, keys, values, mixed, grad_in, stat),
            flops=unit + 20 * attention, name=f"back_{part}",
        )
        made[part] = turned_grads, bias_grad
        order.add(bias_grad)
        spread("BC"[part], *parts)

    def to_input():
        layer_out, grad_middle, grad_mixed, dense_vectors = made["backward"]
        (grad_middle,) = order.after(grad_middle)
        made["input"] = call(
            functools.partial(input_kernel, factor), count,
            [rows_of(D), edges, whole(2, D), vec, mols_of(3, HALF, WIDE), mols_of(3, HALF, WIDE), weight, weight,
             weight, rows_of(D), whole(8, D), whole(8, wide), whole(8, wide)],
            [rows_of(D), whole(16, D)],
            [shape_of(rows, D, dtype=BF16), shape_of(16, D)],
            [column],
            (*scalars, tokens, kinds, type_table, first_gain, made[0][0], made[1][0], query_weight, key_weight,
             value_weight, grad_middle, dense_vectors, made[0][1], made[1][1]),
            flops=3 * unit, name="input", vmem=40 * 2**20,
        )
        order.add(made["input"][1])

    def own_parts(name, targets, column=0):
        while not transfers[name].own:
            transfers[name].go()
        return [(piece, (0, low, targets, column)) for low, piece in enumerate(transfers[name].own)]

    def other_parts(name, targets, column=0):
        while transfers[name].result is None:
            transfers[name].go()
        return [(piece, (1, low, targets, column)) for low, piece in enumerate(transfers[name].result[0])]

    def into_place(step):
        before, three = (), (0, 1, 2)
        if step == "a":
            found = other_parts("A", (0, 1)) + own_parts("A", (0, 1))
        elif step == "o":
            found = other_parts("O", (0,)) + own_parts("O", (0,))
        elif step == "b":
            found = other_parts("B", three) + own_parts("B", three)
        elif step == "q":
            found, before = own_parts("C", three, HALF), placed["b"]
        else:
            found, before = other_parts("C", three, HALF), placed["q"]
        pieces, parts = zip(*found)
        placed[step] = put_in_place(
            place, order.after(*pieces), parts, {"a": 2, "o": 1}.get(step, 3), before
        )
        order.add(placed[step][0])

    def finish_vectors():
        if "vectors" not in made:
            small = transfers["O"].result[1]
            made["vectors"] = [small[i] for i in (4, 5, 12, 9, 8, 0, 1, 10, 11)] + [small[2:4]]
            order.add(*order.before, *made["vectors"])

    kernels = {"F": dense_forward, "D": dense_backward, "0": lambda: back(0), "1": lambda: back(1), "I": to_input}
    for step in SCHEDULE:
        if step in kernels:
            kernels[step]()
        elif step in "wxyz":
            begin("AOBC"["wxyz".index(step)])
        elif step in transfers:
            transfers[step].go()
            if step == "O" and transfers[step].result is not None:
                finish_vectors()
        else:
            into_place(step)
    outer_grad, inner_grad = placed["a"]
    (output_grad,) = placed["o"]
    query_grad, key_grad, value_grad = placed["r"]
    layer_out = made["backward"][0]
    tokens_grad = made["input"][0]
    finish_vectors()
    return tuple(
        [layer_out, tokens_grad]
        + [grad.reshape(D, D) for grad in (query_grad, key_grad, value_grad, output_grad, inner_grad, outer_grad)]
        + made["vectors"]
    )


def solution(mesh):
    split = P(AXES, None)
    return jax.shard_map(
        functools.partial(per_device, dict(mesh.shape)),
        mesh=mesh,
        in_specs=(split, P(AXES), P(AXES)) + (P(),) * 16 + (split,),
        out_specs=(split, split) + (P(),) * 16,
        check_vma=False,
    )
```

```python
import functools
import math

import jax
import jax.numpy as jnp
import numpy as np
from jax import lax
from jax.experimental import pallas as pl
from jax.experimental.pallas import tpu as pltpu
from jax.sharding import PartitionSpec as P

D = 768
H = 32
DH = 24
SLOT = 208
GROUP = 16
HALF = GROUP * DH
WIDE = 256
SCALE = 1.0 / math.sqrt(DH)
LOG_SCALE = math.log2(math.e) / math.sqrt(DH)
LN_2 = math.log(2.0)
AXES = ("wide", "narrow")
NN = (((1,), (0,)), ((), ()))
NT = (((1,), (1,)), ((), ()))
TN = (((0,), (0,)), ((), ()))
F32 = jnp.float32
BF16 = jnp.bfloat16
VMEM = 60 * 2**20
HBM = pl.BlockSpec(memory_space=pltpu.HBM)


SCHEDULE = "FwDAx0OA1yOAzBOCAIOBACOBACBOACOBCBACOBOAoaCBBbCqCr"


def dot(left, right, dims=NN):
    return lax.dot_general(left, right, dims, preferred_element_type=F32)


def norm_parts(values):
    average = jnp.mean(values, -1, keepdims=True)
    centered = values - average
    inv_std = lax.rsqrt(jnp.mean(centered * centered, -1, keepdims=True) + 1e-05)
    return centered * inv_std, inv_std


def norm_back(grad_hat, normed, inv_std):
    return (
        grad_hat
        - jnp.mean(grad_hat, -1, keepdims=True)
        - normed * jnp.mean(grad_hat * normed, -1, keepdims=True)
    ) * inv_std


def row_of(ref):
    return ref[...].astype(F32).reshape(1, D)


def kinds_column(kinds_ref, edge_ref):
    @pl.when(pl.program_id(0) == 0)
    def turn():
        kinds = kinds_ref[...].astype(F32).reshape(1, -1)
        edge_ref[...] = jnp.broadcast_to(kinds, (8, kinds.shape[1])).T[:, :1]


def embed(tokens, edge, table_ref):
    table = table_ref[...].astype(F32)
    return tokens.astype(F32) + jnp.where(edge == 1, table[1:2], table[0:1])


def turn(values):
    return jnp.concatenate([values, jnp.zeros((WIDE - SLOT, values.shape[1]), F32)]).T


def with_rows(values, rows):
    index = lax.broadcasted_iota(jnp.int32, (8, WIDE), 0)
    extra = jnp.zeros((8, WIDE), F32)
    for i, row in enumerate(rows):
        extra = jnp.where(index == i, row, extra)
    if values.ndim == 3:
        extra = jnp.broadcast_to(extra, (values.shape[0], 8, WIDE))
    return jnp.concatenate([values, extra], -2).astype(BF16)


def split_row(row):
    high = row.astype(BF16).astype(F32)
    mid = (row - high).astype(BF16).astype(F32)
    return [high, mid, row - high - mid]


def attend_kernel(
    factor, lengths_ref, place_ref, tokens_ref, kinds_ref, table_ref, gain_ref, shift_ref, query_bias_ref,
    value_bias_ref, query_weight_ref, key_weight_ref, value_weight_ref, output_bias_ref, inner_bias_ref,
    second_gain_ref, second_shift_ref, *refs,
):
    later_hbm, refs = refs[:5], refs[5:]
    first_ref, query_ref, keys_ref, values_ref, mixed_ref, stat_ref, *outputs = refs[:11]
    edge_ref, scores_ref, out_ref, mixed_all_ref, second_ref, *later, sems = refs[11:]
    mol = pl.program_id(0)
    copies = [pltpu.make_async_copy(*pair, sems.at[k]) for k, pair in enumerate(zip(later_hbm, later))]

    @pl.when(mol == 0)
    def fetch():
        for copy in copies:
            copy.start()

    kinds_column(kinds_ref, edge_ref)

    @pl.when(mol < pl.num_programs(0) - 1)
    def attend():
        attend_molecule(
            mol, lengths_ref, tokens_ref, edge_ref, table_ref, gain_ref, shift_ref, query_bias_ref, value_bias_ref,
            query_weight_ref, key_weight_ref, value_weight_ref, first_ref, query_ref, keys_ref, values_ref, mixed_ref,
            stat_ref, scores_ref, out_ref,
        )
        mixed_all_ref[mol] = mixed_ref[0]

    @pl.when(mol == pl.num_programs(0) - 1)
    def forward():
        for copy in copies:
            copy.wait()
        feed_forward(
            factor, lengths_ref, place_ref, edge_ref, table_ref, mixed_all_ref, *later, output_bias_ref,
            inner_bias_ref, second_gain_ref, second_shift_ref, *outputs, second_ref,
        )


def attend_molecule(
    mol, lengths_ref, tokens_ref, edge_ref, table_ref, gain_ref, shift_ref, query_bias_ref, value_bias_ref,
    query_weight_ref, key_weight_ref, value_weight_ref, first_ref, query_ref, keys_ref, values_ref, mixed_ref,
    stat_ref, scores_ref, out_ref,
):
    edge = edge_ref[pl.ds(pl.multiple_of(mol * SLOT, 8), SLOT), :]
    normed, unused = norm_parts(embed(tokens_ref[...], edge, table_ref))
    first32 = normed * row_of(gain_ref) + row_of(shift_ref)
    first = first32.astype(BF16)
    first_ref[0] = turn(first32).astype(BF16)
    slot = lax.broadcasted_iota(jnp.int32, (1, WIDE), 1)
    bias = jnp.where(slot < lengths_ref[mol], 0.0, -1e30)
    ones = jnp.ones((1, WIDE), F32)
    query = (dot(first, query_weight_ref[...]) + row_of(query_bias_ref)) * LOG_SCALE
    keys = dot(first, key_weight_ref[...])
    values = dot(first, value_weight_ref[...]) + row_of(value_bias_ref)
    query_ref[0] = with_rows(turn(query).reshape(H, DH, WIDE), [ones])
    keys_ref[0] = with_rows(turn(keys).reshape(H, DH, WIDE), [bias, ones, ones, ones])
    values_ref[0] = with_rows(turn(values).reshape(H, DH, WIDE), [ones, ones, ones])
    lag = 7

    def score(h):
        scores_ref[h % (lag + 1)] = dot(keys_ref[0, h, :, :SLOT], query_ref[0, h], TN)

    def mix(h):
        scores = scores_ref[h % (lag + 1)]
        top = jnp.max(scores, axis=0, keepdims=True)
        powered = jnp.exp2(scores - top).astype(BF16)
        out = dot(values_ref[0, h, :, :SLOT], powered)
        total = out[DH : DH + 1]
        out_ref[h * DH : (h + 1) * DH, :] = out[:DH] * (1.0 / total)
        stat_ref[0, h // GROUP, h % GROUP : h % GROUP + 1] = top + jnp.log2(total)

    for h in range(H + lag):
        if h < H:
            score(h)
        if h >= lag:
            mix(h - lag)
    mixed_ref[0] = out_ref[...].astype(BF16)


def gelu_parts(inner):
    root = math.sqrt(2.0 / math.pi)
    bend = root * 0.044715 * inner * inner + root
    half = 0.5 * jnp.tanh(inner * bend) + 0.5
    act = inner * half
    return act, half + act * (1.0 - half) * (6.0 * bend - 4.0 * root)


def valid_rows(lengths_ref, first, mols):
    slot = lax.broadcasted_iota(jnp.int32, (SLOT, 1), 0)
    return jnp.concatenate([(slot < lengths_ref[first + i]).astype(F32) for i in range(mols)])


def feed_forward(
    factor, lengths_ref, place_ref, edge_ref, table_ref, mixed_ref, tokens_ref, cotangent_ref, output_weight_ref,
    inner_weight_ref, outer_weight_ref, output_bias_ref, inner_bias_ref, gain_ref, shift_ref,
    middle_ref, act_ref, grad_inner_ref, kept_ref, sent_ref, second_ref,
):
    mols = mixed_ref.shape[0]
    edge = edge_ref[...]
    valid = valid_rows(lengths_ref, 0, mols)
    mixed = jnp.concatenate([dot(mixed_ref[i], output_weight_ref[...], TN)[:SLOT] for i in range(mols)])
    middle = embed(tokens_ref[...], edge, table_ref) + mixed + row_of(output_bias_ref)
    middle_ref[...] = middle
    normed, unused = norm_parts(middle)
    second = (normed * row_of(gain_ref) + row_of(shift_ref)).astype(BF16)
    inner = dot(second, inner_weight_ref[...]) + row_of(inner_bias_ref)
    act32, slope = gelu_parts(inner)
    act = act32.astype(BF16)
    act_ref[...] = act
    grad_low = (cotangent_ref[...].astype(F32) * valid).astype(BF16)
    grad_inner = (dot(grad_low, outer_weight_ref[...], NT) * slope).astype(BF16)
    grad_inner_ref[...] = grad_inner

    second_ref[...] = second
    for target, begin in core_halves(place_ref[0], kept_ref, sent_ref):
        target[:, :D] = dot(act_ref[:, pl.ds(begin, D // 2)], grad_low * BF16(factor), TN)
        target[:, D:] = dot(second_ref[:, pl.ds(begin, D // 2)], grad_inner * BF16(factor), TN)


def core_halves(core, kept_ref, sent_ref):
    rows = kept_ref.shape[0]
    return [(ref, pl.multiple_of(which * rows, 128)) for ref, which in ((kept_ref, core), (sent_ref, 1 - core))]


def backward_kernel(
    factor, lengths_ref, place_ref, middle_ref, act_ref, grad_inner_ref, mixed_ref, cotangent_ref, outer_bias_ref,
    gain_ref, output_weight_ref, inner_weight_ref, outer_weight_ref,
    layer_ref, grad_middle_ref, grad_mixed_ref, kept_ref, sent_ref, vectors_ref,
):
    mols = mixed_ref.shape[0]
    valid = valid_rows(lengths_ref, 0, mols)
    middle = middle_ref[...]
    normed, inv_std = norm_parts(middle)
    grad_out = cotangent_ref[...].astype(F32) * valid
    grad_inner = grad_inner_ref[...]
    grad_second = dot(grad_inner, inner_weight_ref[...], NT)
    grad_middle = grad_out + norm_back(grad_second * row_of(gain_ref), normed, inv_std)
    grad_middle_ref[...] = grad_middle
    pad = jnp.zeros((WIDE - SLOT, D), F32)
    grads = [jnp.concatenate([grad_middle[i * SLOT : (i + 1) * SLOT], pad]).astype(BF16) for i in range(mols)]
    for i, grad in enumerate(grads):
        grad_mixed_ref[i] = dot(output_weight_ref[...], grad, NT).astype(BF16)
    for target, begin in core_halves(place_ref[0], kept_ref, sent_ref):
        products = [dot(mixed_ref[i, pl.ds(begin, D // 2), :], grad * BF16(factor)) for i, grad in enumerate(grads)]
        target[...] = functools.reduce(jnp.add, products)
    layer = middle + dot(act_ref[...], outer_weight_ref[...]) + row_of(outer_bias_ref)
    layer_ref[...] = (layer * valid).astype(BF16)
    sums = [
        grad_out,
        grad_inner.astype(F32),
        grad_second * normed,
        grad_second,
        grad_middle.astype(BF16).astype(F32),
    ]
    vectors_ref[...] = jnp.zeros_like(vectors_ref)
    for i, values in enumerate(sums):
        vectors_ref[i : i + 1] = jnp.sum(values, 0, keepdims=True) * factor


def back_kernel(
    factor, lengths_ref, place_ref, first_ref, query_ref, keys_ref, values_ref, mixed_ref, grad_ref, stat_ref,
    vectors_ref, turned_grads_ref, kept_ref, sent_ref,
    mixed32_ref, grad32_ref, scores_ref, probs_ref, grads_ref,
):
    step = pl.program_id(0)

    @pl.when(step == 0)
    def start_sums():
        for ref in (grads_ref, kept_ref, sent_ref, vectors_ref):
            ref[...] = jnp.zeros_like(ref)

    mixed32_ref[...] = mixed_ref[0].astype(F32)
    grad32_ref[...] = grad_ref[0].astype(F32)
    lag = 2

    def score(h):
        rows = slice(h * DH, (h + 1) * DH)
        stat = split_row(-stat_ref[0, 0, h : h + 1])
        query = with_rows(query_ref[0, h].astype(F32)[:DH], [1.0] + stat)
        scores_ref[h % (lag + 1)] = dot(keys_ref[0, h, :, :SLOT], query, TN)
        grad = grad32_ref[rows]
        shared = split_row(-jnp.sum(grad * mixed32_ref[rows], axis=0, keepdims=True))
        probs_ref[h % (lag + 1)] = dot(values_ref[0, h, :, :SLOT], with_rows(grad, shared), TN)

    def back(h):
        rows = slice(h * DH, (h + 1) * DH)
        probs = jnp.exp2(scores_ref[h % (lag + 1)])
        grad_scores = (probs * probs_ref[h % (lag + 1)]).astype(BF16)
        grad = with_rows(grad32_ref[rows], [])
        grads_ref[0, rows] = dot(keys_ref[0, h, :, :SLOT], grad_scores)[:DH] * SCALE
        grads_ref[1, rows, :SLOT] = dot(query_ref[0, h], grad_scores, NT)[:DH] * LN_2
        grads_ref[2, rows, :SLOT] = dot(grad, probs.astype(BF16), NT)[:DH]

    for h in range(GROUP + lag):
        if h < GROUP:
            score(h)
        if h >= lag:
            back(h - lag)
    grads = grads_ref[...].astype(BF16)
    turned_grads_ref[0] = grads
    grads = (grads * BF16(factor)).reshape(3 * HALF, WIDE)
    for target, begin in core_halves(place_ref[0], kept_ref, sent_ref):
        target[...] += dot(first_ref[0, pl.ds(begin, D // 2), :], grads, NT)
    vectors_ref[...] += dot(jnp.ones((8, WIDE), BF16), grads, NT)


def input_kernel(
    factor, lengths_ref, place_ref, tokens_ref, kinds_ref, table_ref, gain_ref, low_ref, high_ref, query_weight_ref,
    key_weight_ref, value_weight_ref, grad_middle_ref, dense_ref, low_bias_ref, high_bias_ref,
    tokens_grad_ref, vectors_ref,
    edge_ref,
):
    mol = pl.program_id(0)

    @pl.when(mol == 0)
    def start_sums():
        vectors_ref[...] = jnp.zeros_like(vectors_ref)

    kinds_column(kinds_ref, edge_ref)
    edge = edge_ref[pl.ds(pl.multiple_of(mol * SLOT, 8), SLOT), :]
    total = jnp.zeros((D, WIDE), F32)
    for i, weight_ref in enumerate((query_weight_ref, key_weight_ref, value_weight_ref)):
        total = total + dot(weight_ref[...], jnp.concatenate([low_ref[0, i], high_ref[0, i]]))
    grad_first = total.T[:SLOT]
    normed, inv_std = norm_parts(embed(tokens_ref[...], edge, table_ref))
    grad_start = grad_middle_ref[...] + norm_back(grad_first * row_of(gain_ref), normed, inv_std)
    tokens_grad_ref[...] = grad_start.astype(BF16)
    sums = [
        grad_first * normed,
        grad_first,
        jnp.where(edge == 1, 0.0, grad_start),
        jnp.where(edge == 1, grad_start, 0.0),
    ]
    for i, values in enumerate(sums):
        vectors_ref[i : i + 1] += jnp.sum(values, 0, keepdims=True)

    @pl.when(mol == pl.num_programs(0) - 1)
    def finish():
        vectors_ref[...] = vectors_ref[...] * factor
        for i, begin in ((0, 0), (1, 2 * HALF)):
            vectors_ref[4 + i : 5 + i, :HALF] = low_bias_ref[:1, begin : begin + HALF]
            vectors_ref[4 + i : 5 + i, HALF:] = high_bias_ref[:1, begin : begin + HALF]
        vectors_ref[8:16] = dense_ref[...]


def whole(*shape):
    return pl.BlockSpec(shape, lambda i, *_: (0,) * len(shape))


def rows_of(width):
    return pl.BlockSpec((SLOT, width), lambda i, *_: (i, 0))


def mols_of(*shape):
    return pl.BlockSpec((1,) + shape, lambda i, *_: (i,) + (0,) * len(shape))


def shape_of(*shape, dtype=F32):
    return jax.ShapeDtypeStruct(shape, dtype)


def call(kernel, count, in_specs, out_specs, out_shape, scratch, args, flops, name, vmem=VMEM):
    return pl.pallas_call(
        kernel,
        grid_spec=pltpu.PrefetchScalarGridSpec(
            num_scalar_prefetch=2,
            grid=(count,),
            in_specs=in_specs,
            out_specs=out_specs,
            scratch_shapes=scratch,
        ),
        out_shape=out_shape,
        compiler_params=pltpu.CompilerParams(
            dimension_semantics=("arbitrary",), vmem_limit_bytes=vmem
        ),
        cost_estimate=pl.CostEstimate(flops=20 * flops, bytes_accessed=2**20, transcendentals=0),
        name=name,
    )(*args)


def bits_of(mesh_shape):
    narrow = mesh_shape["narrow"].bit_length() - 1
    wide = mesh_shape["wide"].bit_length() - 1
    y = (wide - 1) // 2
    return {
        "c": [0],
        "x": list(range(1, narrow)),
        "y": list(range(narrow, narrow + y)),
        "z": list(range(narrow + y, narrow + wide)),
    }


def swap(values, bit, devices):
    even, odd = bit if isinstance(bit, tuple) else (bit, bit)
    return lax.ppermute(values, AXES, [(i, i ^ (1 << (odd if i & 1 else even))) for i in range(devices)])


def pick(values, *index):
    for i in index:
        values = lax.dynamic_index_in_dim(values, i, 0, keepdims=False)
    return values


def place_kernel(parts, count_in, place_ref, *refs):
    sources = refs[: len(parts)]
    outs, sems = refs[len(parts) + count_in : -1], refs[-1]
    stores = []
    for n, (other, low, targets, column) in enumerate(parts):
        core, first, second = place_ref[0], place_ref[1], place_ref[2]
        if other:
            core, first, second = 1 - core, second, first
        rows = D // 16
        width = sources[n].shape[1] // len(targets)
        for k in range(4):
            row = (
                core,
                lax.bitwise_xor(low, first),
                lax.bitwise_xor(k // 2, second),
                lax.bitwise_xor(k % 2, place_ref[3]),
            )
            for m, target in enumerate(targets):
                stores.append(
                    pltpu.make_async_copy(
                        sources[n].at[k * rows : (k + 1) * rows, m * width : (m + 1) * width],
                        outs[target].at[*row, :, column : column + width],
                        sems.at[n, k, m],
                    )
                )
                stores[-1].start()
    for store in stores:
        store.wait()


def put_in_place(place, pieces, parts, count_out, before=()):
    rows = D // 16
    pieces = [piece.reshape(-1, piece.shape[-1]) for piece in pieces]
    return pl.pallas_call(
        functools.partial(place_kernel, parts, len(before)),
        grid_spec=pltpu.PrefetchScalarGridSpec(
            num_scalar_prefetch=1,
            grid=(1,),
            in_specs=[whole(*piece.shape) for piece in pieces] + [HBM] * len(before),
            out_specs=[HBM] * count_out,
            scratch_shapes=[pltpu.SemaphoreType.DMA((len(pieces), 4, 3))],
        ),
        out_shape=[shape_of(2, 2, 2, 2, rows, D)] * count_out,
        input_output_aliases={1 + len(pieces) + i: i for i in range(len(before))},
        compiler_params=pltpu.CompilerParams(vmem_limit_bytes=20 * 2**20),
        cost_estimate=pl.CostEstimate(flops=10**10, bytes_accessed=2**20, transcendentals=0),
        name="place",
    )(place, *pieces, *before)


def spread_sum(kept, sent, rider, own, bits, me, devices):
    rows, width = kept.shape[0] // 8, kept.shape[1]
    core, x, y, z = (bits[k][0] for k in "cxyz")
    (got,) = yield [(sent, core)]
    terms = [v.reshape(2, 2, 2, rows, width) for v in (kept, got)]
    scatter = (((x, y), me[1]), ((y, x), me[2]), (z, me[3]))
    for bit, mine in scatter:
        (got,) = yield [(functools.reduce(jnp.add, [pick(t, 1 - mine) for t in terms]), bit)]
        terms = [pick(t, mine) for t in terms] + [got]
    total = functools.reduce(jnp.add, terms)
    small = rider()

    def with_small(values):
        return values if small is None else jnp.concatenate([values.reshape(-1, width), small])

    def apart(values, shape):
        if small is None:
            return values, None
        count = math.prod(shape[:-1])
        return values[:count].reshape(shape), small + values[count:]

    for bit in bits["x"][1:] + bits["y"][1:] + bits["z"][1:]:
        (got,) = yield [(with_small(total), bit)]
        got, small = apart(got, total.shape)
        total = total + got
    (got,) = yield [(with_small(total), z)]
    got, small = apart(got, total.shape)
    total = jnp.stack([total, got])
    (got,) = yield [(with_small(total), (y, x))]
    got, small = apart(got, total.shape)
    total = jnp.stack([total, got])
    got, other = yield [(with_small(total), (x, y)), (total, core)]
    got, small = apart(got, total.shape)
    own.extend((total, got))
    (last,) = yield [(with_small(got), core)]
    if small is not None:
        small = small + last[-small.shape[0] :]
    yield (other, last), small


class Order:
    def __init__(self):
        self.before = ()

    def after(self, *values):
        if self.before:
            values, unused = lax.optimization_barrier((values, self.before))
        return values

    def add(self, *values):
        self.before = tuple(values)


class Transfer:
    def __init__(self, name, steps, own, devices, order):
        self.name = name
        self.own = own
        self.level = 0
        self.steps = steps
        self.devices = devices
        self.order = order
        self.result = None
        self.send(next(self.steps))

    def send(self, sent):
        self.order.add(*self.order.before, *[values for values, unused in sent])
        with jax.named_scope(f"{self.name}_{self.level}"):
            self.got = [swap(values, bit, self.devices) for values, bit in sent]
        self.level += 1

    def go(self):
        if self.result is not None:
            return
        sent = self.steps.send(self.order.after(*self.got))
        if isinstance(sent, list):
            self.order.before = ()
            self.send(sent)
        else:
            self.result = sent


def per_device(
    mesh_shape, tokens, kinds, lengths, query_weight, key_weight, value_weight, output_weight, inner_weight,
    outer_weight, query_bias, value_bias, output_bias, inner_bias, outer_bias, first_gain, first_shift,
    second_gain, second_shift, type_table, cotangent,
):
    count = lengths.shape[0]
    rows = tokens.shape[0]
    devices = mesh_shape["wide"] * mesh_shape["narrow"]
    factor = 1.0 / devices
    bits = bits_of(mesh_shape)
    index = lax.axis_index("wide") * mesh_shape["narrow"] + lax.axis_index("narrow")
    at = [(index >> bits[k][0]) & 1 for k in "cxyz"]
    me = [at[0], jnp.where(at[0] == 0, at[1], at[2]), jnp.where(at[0] == 0, at[2], at[1]), at[3]]
    place = jnp.stack(me).astype(jnp.int32)
    unit = 2 * rows * D * D
    attention = 2 * rows * SLOT * D
    vec = pl.BlockSpec((D,), lambda i, *_: (0,))
    weight = whole(D, D)
    edges = pl.BlockSpec((rows,), lambda i, *_: (0,))
    column = pltpu.VMEM((rows, 1), F32)
    scalars = (lengths, place)
    once = pl.Buffered(1)
    single = lambda *shape: pl.BlockSpec(shape, lambda i, *_: (0,) * len(shape), pipeline_mode=once)
    now = lambda *shape: pl.BlockSpec((1,) + shape, lambda i, *_: (jnp.minimum(i, count - 1),) + (0,) * len(shape))
    low = pltpu.VMEM((rows, D), BF16)
    room = pltpu.VMEM((D, D), BF16)
    first, query, keys, values, mixed, stat, middle, act, grad_inner, *dense_parts = call(
        functools.partial(attend_kernel, factor), count + 1,
        [pl.BlockSpec((SLOT, D), lambda i, *_: (jnp.minimum(i, count - 1), 0)), edges, whole(2, D), vec, vec, vec, vec,
         single(D, D), single(D, D), single(D, D), vec, vec, vec, vec] + [HBM] * 5,
        [now(D, WIDE)] + [now(H, 32, WIDE)] * 3 + [now(D, WIDE), now(2, GROUP, WIDE)] + [single(rows, D)] * 3
        + [single(D // 2, 2 * D)] * 2,
        [shape_of(count, D, WIDE, dtype=BF16)] + [shape_of(count, H, 32, WIDE, dtype=BF16)] * 3
        + [shape_of(count, D, WIDE, dtype=BF16), shape_of(count, 2, GROUP, WIDE), shape_of(rows, D),
           shape_of(rows, D, dtype=BF16), shape_of(rows, D, dtype=BF16)] + [shape_of(D // 2, 2 * D)] * 2,
        [column, pltpu.VMEM((8, SLOT, WIDE), F32), pltpu.VMEM((D, WIDE), F32), pltpu.VMEM((count, D, WIDE), BF16), low,
         low, low, room, room, room, pltpu.SemaphoreType.DMA((5,))],
        (*scalars, tokens, kinds, type_table, first_gain, first_shift, query_bias, value_bias, query_weight,
         key_weight, value_weight, output_bias, inner_bias, second_gain, second_shift, tokens, cotangent,
         output_weight, inner_weight, outer_weight),
        flops=8 * unit + 20 * attention, name="attend",
    )
    mols = count
    tall = lambda width: pl.BlockSpec((mols * SLOT, width), lambda i, *_: (i, 0))
    several = pl.BlockSpec((mols, D, WIDE), lambda i, *_: (i, 0, 0))
    halves = lambda width: [whole(D // 2, width)] * 2
    half_shapes = lambda width: [shape_of(D // 2, width)] * 2
    wide = 3 * HALF
    order = Order()
    transfers, made, placed = {}, {}, {}

    def begin(name):
        kept, sent = made[name]
        (sent,) = order.after(sent)
        order.before = ()
        rider = (lambda: made["input"][1]) if name == "O" else (lambda: None)
        own = []
        steps = spread_sum(kept, sent, rider, own, bits, me, devices)
        transfers[name] = Transfer(f"sum_{name}", steps, own, devices, order)

    def spread(name, *parts):
        made[name] = parts

    def dense_forward():
        order.add(act)
        spread("A", *dense_parts)

    def dense_backward():
        (act_in,) = order.after(act)
        layer_out, grad_middle, grad_mixed, *parts, dense_vectors = call(
            functools.partial(backward_kernel, factor), count // mols,
            [tall(D), tall(D), tall(D), several, tall(D), vec, vec, weight, weight, weight],
            [tall(D), tall(D), several] + halves(D) + [whole(8, D)],
            [shape_of(rows, D, dtype=BF16), shape_of(rows, D), shape_of(count, D, WIDE, dtype=BF16)] + half_shapes(D)
            + [shape_of(8, D)],
            [],
            (*scalars, middle, act_in, grad_inner, mixed, cotangent, outer_bias, second_gain, output_weight,
             inner_weight, outer_weight),
            flops=4 * unit, name="dense_backward",
        )
        made["backward"] = layer_out, grad_middle, grad_mixed, dense_vectors
        order.add(dense_vectors)
        spread("O", *parts)

    def back(part):
        heads = pl.BlockSpec((1, GROUP, 32, WIDE), lambda i, *_: (i, part, 0, 0))
        half = pl.BlockSpec((1, HALF, WIDE), lambda i, *_: (i, part, 0))
        (grad_in,) = order.after(made["backward"][2])
        bias_grad, turned_grads, *parts = call(
            functools.partial(back_kernel, factor), count,
            [mols_of(D, WIDE), heads, heads, heads, half, half,
             pl.BlockSpec((1, 1, GROUP, WIDE), lambda i, *_: (i, part, 0, 0))],
            [whole(8, wide), mols_of(3, HALF, WIDE)] + halves(wide),
            [shape_of(8, wide), shape_of(count, 3, HALF, WIDE, dtype=BF16)] + half_shapes(wide),
            [pltpu.VMEM((HALF, WIDE), F32)] * 2 + [pltpu.VMEM((3, SLOT, WIDE), F32)] * 2
            + [pltpu.VMEM((3, HALF, WIDE), F32)],
            (*scalars, first, query, keys, values, mixed, grad_in, stat),
            flops=unit + 20 * attention, name=f"back_{part}",
        )
        made[part] = turned_grads, bias_grad
        order.add(bias_grad)
        spread("BC"[part], *parts)

    def to_input():
        layer_out, grad_middle, grad_mixed, dense_vectors = made["backward"]
        (grad_middle,) = order.after(grad_middle)
        made["input"] = call(
            functools.partial(input_kernel, factor), count,
            [rows_of(D), edges, whole(2, D), vec, mols_of(3, HALF, WIDE), mols_of(3, HALF, WIDE), weight, weight,
             weight, rows_of(D), whole(8, D), whole(8, wide), whole(8, wide)],
            [rows_of(D), whole(16, D)],
            [shape_of(rows, D, dtype=BF16), shape_of(16, D)],
            [column],
            (*scalars, tokens, kinds, type_table, first_gain, made[0][0], made[1][0], query_weight, key_weight,
             value_weight, grad_middle, dense_vectors, made[0][1], made[1][1]),
            flops=3 * unit, name="input", vmem=40 * 2**20,
        )
        order.add(made["input"][1])

    def own_parts(name, targets, column=0):
        while not transfers[name].own:
            transfers[name].go()
        return [(piece, (0, low, targets, column)) for low, piece in enumerate(transfers[name].own)]

    def other_parts(name, targets, column=0):
        while transfers[name].result is None:
            transfers[name].go()
        return [(piece, (1, low, targets, column)) for low, piece in enumerate(transfers[name].result[0])]

    def into_place(step):
        before, three = (), (0, 1, 2)
        if step == "a":
            found = other_parts("A", (0, 1)) + own_parts("A", (0, 1))
        elif step == "o":
            found = other_parts("O", (0,)) + own_parts("O", (0,))
        elif step == "b":
            found = other_parts("B", three) + own_parts("B", three)
        elif step == "q":
            found, before = own_parts("C", three, HALF), placed["b"]
        else:
            found, before = other_parts("C", three, HALF), placed["q"]
        pieces, parts = zip(*found)
        placed[step] = put_in_place(
            place, order.after(*pieces), parts, {"a": 2, "o": 1}.get(step, 3), before
        )
        order.add(placed[step][0])

    def finish_vectors():
        if "vectors" not in made:
            small = transfers["O"].result[1]
            made["vectors"] = [small[i] for i in (4, 5, 12, 9, 8, 0, 1, 10, 11)] + [small[2:4]]
            order.add(*order.before, *made["vectors"])

    kernels = {"F": dense_forward, "D": dense_backward, "0": lambda: back(0), "1": lambda: back(1), "I": to_input}
    for step in SCHEDULE:
        if step in kernels:
            kernels[step]()
        elif step in "wxyz":
            begin("AOBC"["wxyz".index(step)])
        elif step in transfers:
            transfers[step].go()
            if step == "O" and transfers[step].result is not None:
                finish_vectors()
        else:
            into_place(step)
    outer_grad, inner_grad = placed["a"]
    (output_grad,) = placed["o"]
    query_grad, key_grad, value_grad = placed["r"]
    layer_out = made["backward"][0]
    tokens_grad = made["input"][0]
    finish_vectors()
    return tuple(
        [layer_out, tokens_grad]
        + [grad.reshape(D, D) for grad in (query_grad, key_grad, value_grad, output_grad, inner_grad, outer_grad)]
        + made["vectors"]
    )


def solution(mesh):
    split = P(AXES, None)
    return jax.shard_map(
        functools.partial(per_device, dict(mesh.shape)),
        mesh=mesh,
        in_specs=(split, P(AXES), P(AXES)) + (P(),) * 16 + (split,),
        out_specs=(split, split) + (P(),) * 16,
        check_vma=False,
    )
```

```python
import functools
import math

import jax
import jax.numpy as jnp
import numpy as np
from jax import lax
from jax.experimental import pallas as pl
from jax.experimental.pallas import tpu as pltpu
from jax.sharding import PartitionSpec as P

D = 768
H = 32
DH = 24
SLOT = 208
GROUP = 16
HALF = GROUP * DH
WIDE = 256
SCALE = 1.0 / math.sqrt(DH)
LOG_SCALE = math.log2(math.e) / math.sqrt(DH)
LN_2 = math.log(2.0)
AXES = ("wide", "narrow")
NN = (((1,), (0,)), ((), ()))
NT = (((1,), (1,)), ((), ()))
TN = (((0,), (0,)), ((), ()))
F32 = jnp.float32
BF16 = jnp.bfloat16
VMEM = 60 * 2**20
HBM = pl.BlockSpec(memory_space=pltpu.HBM)


SCHEDULE = "FwDAx0OA1yOAzBOCAIOBACOBACBOACOBCBACOBOAoaCBBbCqCr"


def dot(left, right, dims=NN):
    return lax.dot_general(left, right, dims, preferred_element_type=F32)


def norm_parts(values):
    average = jnp.mean(values, -1, keepdims=True)
    centered = values - average
    inv_std = lax.rsqrt(jnp.mean(centered * centered, -1, keepdims=True) + 1e-05)
    return centered * inv_std, inv_std


def norm_back(grad_hat, normed, inv_std):
    return (
        grad_hat
        - jnp.mean(grad_hat, -1, keepdims=True)
        - normed * jnp.mean(grad_hat * normed, -1, keepdims=True)
    ) * inv_std


def row_of(ref):
    return ref[...].astype(F32).reshape(1, D)


def kinds_column(kinds_ref, edge_ref):
    @pl.when(pl.program_id(0) == 0)
    def turn():
        kinds = kinds_ref[...].astype(F32).reshape(1, -1)
        edge_ref[...] = jnp.broadcast_to(kinds, (8, kinds.shape[1])).T[:, :1]


def embed(tokens, edge, table_ref):
    table = table_ref[...].astype(F32)
    return tokens.astype(F32) + jnp.where(edge == 1, table[1:2], table[0:1])


def turn(values):
    return jnp.concatenate([values, jnp.zeros((WIDE - SLOT, values.shape[1]), F32)]).T


def with_rows(values, rows):
    index = lax.broadcasted_iota(jnp.int32, (8, WIDE), 0)
    extra = jnp.zeros((8, WIDE), F32)
    for i, row in enumerate(rows):
        extra = jnp.where(index == i, row, extra)
    if values.ndim == 3:
        extra = jnp.broadcast_to(extra, (values.shape[0], 8, WIDE))
    return jnp.concatenate([values, extra], -2).astype(BF16)


def split_row(row):
    high = row.astype(BF16).astype(F32)
    mid = (row - high).astype(BF16).astype(F32)
    return [high, mid, row - high - mid]


def attend_kernel(
    factor, lengths_ref, tokens_ref, kinds_ref, table_ref, gain_ref, shift_ref, query_bias_ref,
    value_bias_ref, query_weight_ref, key_weight_ref, value_weight_ref, output_bias_ref, inner_bias_ref,
    second_gain_ref, second_shift_ref, *refs,
):
    later_hbm, refs = refs[:5], refs[5:]
    first_ref, query_ref, keys_ref, values_ref, mixed_ref, stat_ref, *outputs = refs[:11]
    edge_ref, scores_ref, out_ref, mixed_all_ref, second_ref, *later, sems = refs[11:]
    mol = pl.program_id(0)
    copies = [pltpu.make_async_copy(*pair, sems.at[k]) for k, pair in enumerate(zip(later_hbm, later))]

    @pl.when(mol == 0)
    def fetch():
        for copy in copies:
            copy.start()

    kinds_column(kinds_ref, edge_ref)

    @pl.when(mol < pl.num_programs(0) - 1)
    def attend():
        attend_molecule(
            mol, lengths_ref, tokens_ref, edge_ref, table_ref, gain_ref, shift_ref, query_bias_ref, value_bias_ref,
            query_weight_ref, key_weight_ref, value_weight_ref, first_ref, query_ref, keys_ref, values_ref, mixed_ref,
            stat_ref, scores_ref, out_ref,
        )
        mixed_all_ref[mol] = mixed_ref[0]

    @pl.when(mol == pl.num_programs(0) - 1)
    def forward():
        for copy in copies:
            copy.wait()
        feed_forward(
            factor, lengths_ref, edge_ref, table_ref, mixed_all_ref, *later, output_bias_ref,
            inner_bias_ref, second_gain_ref, second_shift_ref, *outputs, second_ref,
        )


def attend_molecule(
    mol, lengths_ref, tokens_ref, edge_ref, table_ref, gain_ref, shift_ref, query_bias_ref, value_bias_ref,
    query_weight_ref, key_weight_ref, value_weight_ref, first_ref, query_ref, keys_ref, values_ref, mixed_ref,
    stat_ref, scores_ref, out_ref,
):
    edge = edge_ref[pl.ds(pl.multiple_of(mol * SLOT, 8), SLOT), :]
    normed, unused = norm_parts(embed(tokens_ref[...], edge, table_ref))
    first32 = normed * row_of(gain_ref) + row_of(shift_ref)
    first = first32.astype(BF16)
    first_ref[0] = turn(first32).astype(BF16)
    slot = lax.broadcasted_iota(jnp.int32, (1, WIDE), 1)
    bias = jnp.where(slot < lengths_ref[mol], 0.0, -1e30)
    ones = jnp.ones((1, WIDE), F32)
    query = (dot(first, query_weight_ref[...]) + row_of(query_bias_ref)) * LOG_SCALE
    keys = dot(first, key_weight_ref[...])
    values = dot(first, value_weight_ref[...]) + row_of(value_bias_ref)
    query_ref[0] = with_rows(turn(query).reshape(H, DH, WIDE), [ones])
    keys_ref[0] = with_rows(turn(keys).reshape(H, DH, WIDE), [bias, ones, ones, ones])
    values_ref[0] = with_rows(turn(values).reshape(H, DH, WIDE), [ones, ones, ones])
    lag = 7

    def score(h):
        scores_ref[h % (lag + 1)] = dot(keys_ref[0, h, :, :SLOT], query_ref[0, h], TN)

    def mix(h):
        scores = scores_ref[h % (lag + 1)]
        top = jnp.max(scores, axis=0, keepdims=True)
        powered = jnp.exp2(scores - top).astype(BF16)
        out = dot(values_ref[0, h, :, :SLOT], powered)
        total = out[DH : DH + 1]
        out_ref[h * DH : (h + 1) * DH, :] = out[:DH] * (1.0 / total)
        stat_ref[0, h // GROUP, h % GROUP : h % GROUP + 1] = top + jnp.log2(total)

    for h in range(H + lag):
        if h < H:
            score(h)
        if h >= lag:
            mix(h - lag)
    mixed_ref[0] = out_ref[...].astype(BF16)


def gelu_parts(inner):
    root = math.sqrt(2.0 / math.pi)
    bend = root * 0.044715 * inner * inner + root
    half = 0.5 * jnp.tanh(inner * bend) + 0.5
    act = inner * half
    return act, half + act * (1.0 - half) * (6.0 * bend - 4.0 * root)


def valid_rows(lengths_ref, first, mols):
    slot = lax.broadcasted_iota(jnp.int32, (SLOT, 1), 0)
    return jnp.concatenate([(slot < lengths_ref[first + i]).astype(F32) for i in range(mols)])


def feed_forward(
    factor, lengths_ref, edge_ref, table_ref, mixed_ref, tokens_ref, cotangent_ref, output_weight_ref,
    inner_weight_ref, outer_weight_ref, output_bias_ref, inner_bias_ref, gain_ref, shift_ref,
    middle_ref, act_ref, grad_inner_ref, kept_ref, sent_ref, second_ref,
):
    mols = mixed_ref.shape[0]
    edge = edge_ref[...]
    valid = valid_rows(lengths_ref, 0, mols)
    mixed = jnp.concatenate([dot(mixed_ref[i], output_weight_ref[...], TN)[:SLOT] for i in range(mols)])
    middle = embed(tokens_ref[...], edge, table_ref) + mixed + row_of(output_bias_ref)
    middle_ref[...] = middle
    normed, unused = norm_parts(middle)
    second = (normed * row_of(gain_ref) + row_of(shift_ref)).astype(BF16)
    inner = dot(second, inner_weight_ref[...]) + row_of(inner_bias_ref)
    act32, slope = gelu_parts(inner)
    act = act32.astype(BF16)
    act_ref[...] = act
    grad_low = (cotangent_ref[...].astype(F32) * valid).astype(BF16)
    grad_inner = (dot(grad_low, outer_weight_ref[...], NT) * slope).astype(BF16)
    grad_inner_ref[...] = grad_inner

    second_ref[...] = second
    for target, begin in core_halves(kept_ref, sent_ref):
        target[:, :D] = dot(act_ref[:, pl.ds(begin, D // 2)], grad_low * BF16(factor), TN)
        target[:, D:] = dot(second_ref[:, pl.ds(begin, D // 2)], grad_inner * BF16(factor), TN)


def core_halves(kept_ref, sent_ref):
    rows = kept_ref.shape[0]
    core = lax.rem(lax.axis_index("narrow"), 2)
    return [(ref, pl.multiple_of(which * rows, 128)) for ref, which in ((kept_ref, core), (sent_ref, 1 - core))]


def backward_kernel(
    factor, lengths_ref, middle_ref, act_ref, grad_inner_ref, mixed_ref, cotangent_ref, outer_bias_ref,
    gain_ref, output_weight_ref, inner_weight_ref, outer_weight_ref,
    layer_ref, grad_middle_ref, grad_mixed_ref, kept_ref, sent_ref, vectors_ref,
):
    mols = mixed_ref.shape[0]
    valid = valid_rows(lengths_ref, 0, mols)
    middle = middle_ref[...]
    normed, inv_std = norm_parts(middle)
    grad_out = cotangent_ref[...].astype(F32) * valid
    grad_inner = grad_inner_ref[...]
    grad_second = dot(grad_inner, inner_weight_ref[...], NT)
    grad_middle = grad_out + norm_back(grad_second * row_of(gain_ref), normed, inv_std)
    grad_middle_ref[...] = grad_middle
    pad = jnp.zeros((WIDE - SLOT, D), F32)
    grads = [jnp.concatenate([grad_middle[i * SLOT : (i + 1) * SLOT], pad]).astype(BF16) for i in range(mols)]
    for i, grad in enumerate(grads):
        grad_mixed_ref[i] = dot(output_weight_ref[...], grad, NT).astype(BF16)
    for target, begin in core_halves(kept_ref, sent_ref):
        products = [dot(mixed_ref[i, pl.ds(begin, D // 2), :], grad * BF16(factor)) for i, grad in enumerate(grads)]
        target[...] = functools.reduce(jnp.add, products)
    layer = middle + dot(act_ref[...], outer_weight_ref[...]) + row_of(outer_bias_ref)
    layer_ref[...] = (layer * valid).astype(BF16)
    sums = [
        grad_out,
        grad_inner.astype(F32),
        grad_second * normed,
        grad_second,
        grad_middle.astype(BF16).astype(F32),
    ]
    vectors_ref[...] = jnp.zeros_like(vectors_ref)
    for i, values in enumerate(sums):
        vectors_ref[i : i + 1] = jnp.sum(values, 0, keepdims=True) * factor


def back_kernel(
    factor, lengths_ref, first_ref, query_ref, keys_ref, values_ref, mixed_ref, grad_ref, stat_ref,
    vectors_ref, turned_grads_ref, kept_ref, sent_ref,
    mixed32_ref, grad32_ref, scores_ref, probs_ref, grads_ref,
):
    step = pl.program_id(0)

    @pl.when(step == 0)
    def start_sums():
        for ref in (grads_ref, kept_ref, sent_ref, vectors_ref):
            ref[...] = jnp.zeros_like(ref)

    mixed32_ref[...] = mixed_ref[0].astype(F32)
    grad32_ref[...] = grad_ref[0].astype(F32)
    lag = 2

    def score(h):
        rows = slice(h * DH, (h + 1) * DH)
        stat = split_row(-stat_ref[0, 0, h : h + 1])
        query = with_rows(query_ref[0, h].astype(F32)[:DH], [1.0] + stat)
        scores_ref[h % (lag + 1)] = dot(keys_ref[0, h, :, :SLOT], query, TN)
        grad = grad32_ref[rows]
        shared = split_row(-jnp.sum(grad * mixed32_ref[rows], axis=0, keepdims=True))
        probs_ref[h % (lag + 1)] = dot(values_ref[0, h, :, :SLOT], with_rows(grad, shared), TN)

    def back(h):
        rows = slice(h * DH, (h + 1) * DH)
        probs = jnp.exp2(scores_ref[h % (lag + 1)])
        grad_scores = (probs * probs_ref[h % (lag + 1)]).astype(BF16)
        grad = with_rows(grad32_ref[rows], [])
        grads_ref[0, rows] = dot(keys_ref[0, h, :, :SLOT], grad_scores)[:DH] * SCALE
        grads_ref[1, rows, :SLOT] = dot(query_ref[0, h], grad_scores, NT)[:DH] * LN_2
        grads_ref[2, rows, :SLOT] = dot(grad, probs.astype(BF16), NT)[:DH]

    for h in range(GROUP + lag):
        if h < GROUP:
            score(h)
        if h >= lag:
            back(h - lag)
    grads = grads_ref[...].astype(BF16)
    turned_grads_ref[0] = grads
    grads = (grads * BF16(factor)).reshape(3 * HALF, WIDE)
    for target, begin in core_halves(kept_ref, sent_ref):
        target[...] += dot(first_ref[0, pl.ds(begin, D // 2), :], grads, NT)
    vectors_ref[...] += dot(jnp.ones((8, WIDE), BF16), grads, NT)


def input_kernel(
    factor, lengths_ref, tokens_ref, kinds_ref, table_ref, gain_ref, low_ref, high_ref, query_weight_ref,
    key_weight_ref, value_weight_ref, grad_middle_ref, dense_ref, low_bias_ref, high_bias_ref,
    tokens_grad_ref, vectors_ref,
    edge_ref,
):
    mol = pl.program_id(0)

    @pl.when(mol == 0)
    def start_sums():
        vectors_ref[...] = jnp.zeros_like(vectors_ref)

    kinds_column(kinds_ref, edge_ref)
    edge = edge_ref[pl.ds(pl.multiple_of(mol * SLOT, 8), SLOT), :]
    total = jnp.zeros((D, WIDE), F32)
    for i, weight_ref in enumerate((query_weight_ref, key_weight_ref, value_weight_ref)):
        total = total + dot(weight_ref[...], jnp.concatenate([low_ref[0, i], high_ref[0, i]]))
    grad_first = total.T[:SLOT]
    normed, inv_std = norm_parts(embed(tokens_ref[...], edge, table_ref))
    grad_start = grad_middle_ref[...] + norm_back(grad_first * row_of(gain_ref), normed, inv_std)
    tokens_grad_ref[...] = grad_start.astype(BF16)
    sums = [
        grad_first * normed,
        grad_first,
        jnp.where(edge == 1, 0.0, grad_start),
        jnp.where(edge == 1, grad_start, 0.0),
    ]
    for i, values in enumerate(sums):
        vectors_ref[i : i + 1] += jnp.sum(values, 0, keepdims=True)

    @pl.when(mol == pl.num_programs(0) - 1)
    def finish():
        vectors_ref[...] = vectors_ref[...] * factor
        for i, begin in ((0, 0), (1, 2 * HALF)):
            vectors_ref[4 + i : 5 + i, :HALF] = low_bias_ref[:1, begin : begin + HALF]
            vectors_ref[4 + i : 5 + i, HALF:] = high_bias_ref[:1, begin : begin + HALF]
        vectors_ref[8:16] = dense_ref[...]


def whole(*shape):
    return pl.BlockSpec(shape, lambda i, *_: (0,) * len(shape))


def rows_of(width):
    return pl.BlockSpec((SLOT, width), lambda i, *_: (i, 0))


def mols_of(*shape):
    return pl.BlockSpec((1,) + shape, lambda i, *_: (i,) + (0,) * len(shape))


def shape_of(*shape, dtype=F32):
    return jax.ShapeDtypeStruct(shape, dtype)


def call(kernel, count, in_specs, out_specs, out_shape, scratch, args, flops, name, vmem=VMEM):
    return pl.pallas_call(
        kernel,
        grid_spec=pltpu.PrefetchScalarGridSpec(
            num_scalar_prefetch=1,
            grid=(count,),
            in_specs=in_specs,
            out_specs=out_specs,
            scratch_shapes=scratch,
        ),
        out_shape=out_shape,
        compiler_params=pltpu.CompilerParams(
            dimension_semantics=("arbitrary",), vmem_limit_bytes=vmem
        ),
        cost_estimate=pl.CostEstimate(flops=20 * flops, bytes_accessed=2**20, transcendentals=0),
        name=name,
    )(*args)


def bits_of(mesh_shape):
    narrow = mesh_shape["narrow"].bit_length() - 1
    wide = mesh_shape["wide"].bit_length() - 1
    y = (wide - 1) // 2
    return {
        "c": [0],
        "x": list(range(1, narrow)),
        "y": list(range(narrow, narrow + y)),
        "z": list(range(narrow + y, narrow + wide)),
    }


def swap(values, bit, devices):
    even, odd = bit if isinstance(bit, tuple) else (bit, bit)
    return lax.ppermute(values, AXES, [(i, i ^ (1 << (odd if i & 1 else even))) for i in range(devices)])


def pick(values, *index):
    for i in index:
        values = lax.dynamic_index_in_dim(values, i, 0, keepdims=False)
    return values


def place_kernel(parts, count_in, place_ref, *refs):
    sources = refs[: len(parts)]
    outs, sems = refs[len(parts) + count_in : -1], refs[-1]
    stores = []
    for n, (other, low, targets, column) in enumerate(parts):
        core, first, second = place_ref[0], place_ref[1], place_ref[2]
        if other:
            core, first, second = 1 - core, second, first
        rows = D // 16
        width = sources[n].shape[1] // len(targets)
        for k in range(4):
            row = (
                core,
                lax.bitwise_xor(low, first),
                lax.bitwise_xor(k // 2, second),
                lax.bitwise_xor(k % 2, place_ref[3]),
            )
            for m, target in enumerate(targets):
                stores.append(
                    pltpu.make_async_copy(
                        sources[n].at[k * rows : (k + 1) * rows, m * width : (m + 1) * width],
                        outs[target].at[*row, :, column : column + width],
                        sems.at[n, k, m],
                    )
                )
                stores[-1].start()
    for store in stores:
        store.wait()


def put_in_place(place, pieces, parts, count_out, before=()):
    rows = D // 16
    pieces = [piece.reshape(-1, piece.shape[-1]) for piece in pieces]
    return pl.pallas_call(
        functools.partial(place_kernel, parts, len(before)),
        grid_spec=pltpu.PrefetchScalarGridSpec(
            num_scalar_prefetch=1,
            grid=(1,),
            in_specs=[whole(*piece.shape) for piece in pieces] + [HBM] * len(before),
            out_specs=[HBM] * count_out,
            scratch_shapes=[pltpu.SemaphoreType.DMA((len(pieces), 4, 3))],
        ),
        out_shape=[shape_of(2, 2, 2, 2, rows, D)] * count_out,
        input_output_aliases={1 + len(pieces) + i: i for i in range(len(before))},
        compiler_params=pltpu.CompilerParams(vmem_limit_bytes=20 * 2**20),
        cost_estimate=pl.CostEstimate(flops=10**10, bytes_accessed=2**20, transcendentals=0),
        name="place",
    )(place, *pieces, *before)


def spread_sum(kept, sent, rider, own, bits, me, devices):
    rows, width = kept.shape[0] // 8, kept.shape[1]
    core, x, y, z = (bits[k][0] for k in "cxyz")
    (got,) = yield [(sent, core)]
    terms = [v.reshape(2, 2, 2, rows, width) for v in (kept, got)]
    scatter = (((x, y), me[1]), ((y, x), me[2]), (z, me[3]))
    for bit, mine in scatter:
        (got,) = yield [(functools.reduce(jnp.add, [pick(t, 1 - mine) for t in terms]), bit)]
        terms = [pick(t, mine) for t in terms] + [got]
    total = functools.reduce(jnp.add, terms)
    small = rider()

    def with_small(values):
        return values if small is None else jnp.concatenate([values.reshape(-1, width), small])

    def apart(values, shape):
        if small is None:
            return values, None
        count = math.prod(shape[:-1])
        return values[:count].reshape(shape), small + values[count:]

    for bit in bits["x"][1:] + bits["y"][1:] + bits["z"][1:]:
        (got,) = yield [(with_small(total), bit)]
        got, small = apart(got, total.shape)
        total = total + got
    (got,) = yield [(with_small(total), z)]
    got, small = apart(got, total.shape)
    total = jnp.stack([total, got])
    (got,) = yield [(with_small(total), (y, x))]
    got, small = apart(got, total.shape)
    total = jnp.stack([total, got])
    got, other = yield [(with_small(total), (x, y)), (total, core)]
    got, small = apart(got, total.shape)
    own.extend((total, got))
    (last,) = yield [(with_small(got), core)]
    if small is not None:
        small = small + last[-small.shape[0] :]
    yield (other, last), small


class Order:
    def __init__(self):
        self.before = ()

    def after(self, *values):
        if self.before:
            values, unused = lax.optimization_barrier((values, self.before))
        return values

    def add(self, *values):
        self.before = tuple(values)


class Transfer:
    def __init__(self, name, steps, own, devices, order):
        self.name = name
        self.own = own
        self.level = 0
        self.steps = steps
        self.devices = devices
        self.order = order
        self.result = None
        self.send(next(self.steps))

    def send(self, sent):
        self.order.add(*self.order.before, *[values for values, unused in sent])
        with jax.named_scope(f"{self.name}_{self.level}"):
            self.got = [swap(values, bit, self.devices) for values, bit in sent]
        self.level += 1

    def go(self):
        if self.result is not None:
            return
        sent = self.steps.send(self.order.after(*self.got))
        if isinstance(sent, list):
            self.order.before = ()
            self.send(sent)
        else:
            self.result = sent


def per_device(
    mesh_shape, tokens, kinds, lengths, query_weight, key_weight, value_weight, output_weight, inner_weight,
    outer_weight, query_bias, value_bias, output_bias, inner_bias, outer_bias, first_gain, first_shift,
    second_gain, second_shift, type_table, cotangent,
):
    count = lengths.shape[0]
    rows = tokens.shape[0]
    devices = mesh_shape["wide"] * mesh_shape["narrow"]
    factor = 1.0 / devices
    bits = bits_of(mesh_shape)
    index = lax.axis_index("wide") * mesh_shape["narrow"] + lax.axis_index("narrow")
    at = [(index >> bits[k][0]) & 1 for k in "cxyz"]
    me = [at[0], jnp.where(at[0] == 0, at[1], at[2]), jnp.where(at[0] == 0, at[2], at[1]), at[3]]
    place = jnp.stack(me).astype(jnp.int32)
    unit = 2 * rows * D * D
    attention = 2 * rows * SLOT * D
    vec = pl.BlockSpec((D,), lambda i, *_: (0,))
    weight = whole(D, D)
    edges = pl.BlockSpec((rows,), lambda i, *_: (0,))
    column = pltpu.VMEM((rows, 1), F32)
    scalars = (lengths,)
    once = pl.Buffered(1)
    single = lambda *shape: pl.BlockSpec(shape, lambda i, *_: (0,) * len(shape), pipeline_mode=once)
    now = lambda *shape: pl.BlockSpec((1,) + shape, lambda i, *_: (jnp.minimum(i, count - 1),) + (0,) * len(shape))
    low = pltpu.VMEM((rows, D), BF16)
    room = pltpu.VMEM((D, D), BF16)
    first, query, keys, values, mixed, stat, middle, act, grad_inner, *dense_parts = call(
        functools.partial(attend_kernel, factor), count + 1,
        [pl.BlockSpec((SLOT, D), lambda i, *_: (jnp.minimum(i, count - 1), 0)), edges, whole(2, D), vec, vec, vec, vec,
         single(D, D), single(D, D), single(D, D), vec, vec, vec, vec] + [HBM] * 5,
        [now(D, WIDE)] + [now(H, 32, WIDE)] * 3 + [now(D, WIDE), now(2, GROUP, WIDE)] + [single(rows, D)] * 3
        + [single(D // 2, 2 * D)] * 2,
        [shape_of(count, D, WIDE, dtype=BF16)] + [shape_of(count, H, 32, WIDE, dtype=BF16)] * 3
        + [shape_of(count, D, WIDE, dtype=BF16), shape_of(count, 2, GROUP, WIDE), shape_of(rows, D),
           shape_of(rows, D, dtype=BF16), shape_of(rows, D, dtype=BF16)] + [shape_of(D // 2, 2 * D)] * 2,
        [column, pltpu.VMEM((8, SLOT, WIDE), F32), pltpu.VMEM((D, WIDE), F32), pltpu.VMEM((count, D, WIDE), BF16), low,
         low, low, room, room, room, pltpu.SemaphoreType.DMA((5,))],
        (*scalars, tokens, kinds, type_table, first_gain, first_shift, query_bias, value_bias, query_weight,
         key_weight, value_weight, output_bias, inner_bias, second_gain, second_shift, tokens, cotangent,
         output_weight, inner_weight, outer_weight),
        flops=8 * unit + 20 * attention, name="attend",
    )
    mols = count
    tall = lambda width: pl.BlockSpec((mols * SLOT, width), lambda i, *_: (i, 0))
    several = pl.BlockSpec((mols, D, WIDE), lambda i, *_: (i, 0, 0))
    halves = lambda width: [whole(D // 2, width)] * 2
    half_shapes = lambda width: [shape_of(D // 2, width)] * 2
    wide = 3 * HALF
    order = Order()
    transfers, made, placed = {}, {}, {}

    def begin(name):
        kept, sent = made[name]
        (sent,) = order.after(sent)
        order.before = ()
        rider = (lambda: made["input"][1]) if name == "O" else (lambda: None)
        own = []
        steps = spread_sum(kept, sent, rider, own, bits, me, devices)
        transfers[name] = Transfer(f"sum_{name}", steps, own, devices, order)

    def spread(name, *parts):
        made[name] = parts

    def dense_forward():
        order.add(act)
        spread("A", *dense_parts)

    def dense_backward():
        (act_in,) = order.after(act)
        layer_out, grad_middle, grad_mixed, *parts, dense_vectors = call(
            functools.partial(backward_kernel, factor), count // mols,
            [tall(D), tall(D), tall(D), several, tall(D), vec, vec, weight, weight, weight],
            [tall(D), tall(D), several] + halves(D) + [whole(8, D)],
            [shape_of(rows, D, dtype=BF16), shape_of(rows, D), shape_of(count, D, WIDE, dtype=BF16)] + half_shapes(D)
            + [shape_of(8, D)],
            [],
            (*scalars, middle, act_in, grad_inner, mixed, cotangent, outer_bias, second_gain, output_weight,
             inner_weight, outer_weight),
            flops=4 * unit, name="dense_backward",
        )
        made["backward"] = layer_out, grad_middle, grad_mixed, dense_vectors
        order.add(dense_vectors)
        spread("O", *parts)

    def back(part):
        heads = pl.BlockSpec((1, GROUP, 32, WIDE), lambda i, *_: (i, part, 0, 0))
        half = pl.BlockSpec((1, HALF, WIDE), lambda i, *_: (i, part, 0))
        (grad_in,) = order.after(made["backward"][2])
        bias_grad, turned_grads, *parts = call(
            functools.partial(back_kernel, factor), count,
            [mols_of(D, WIDE), heads, heads, heads, half, half,
             pl.BlockSpec((1, 1, GROUP, WIDE), lambda i, *_: (i, part, 0, 0))],
            [whole(8, wide), mols_of(3, HALF, WIDE)] + halves(wide),
            [shape_of(8, wide), shape_of(count, 3, HALF, WIDE, dtype=BF16)] + half_shapes(wide),
            [pltpu.VMEM((HALF, WIDE), F32)] * 2 + [pltpu.VMEM((3, SLOT, WIDE), F32)] * 2
            + [pltpu.VMEM((3, HALF, WIDE), F32)],
            (*scalars, first, query, keys, values, mixed, grad_in, stat),
            flops=unit + 20 * attention, name=f"back_{part}",
        )
        made[part] = turned_grads, bias_grad
        order.add(bias_grad)
        spread("BC"[part], *parts)

    def to_input():
        layer_out, grad_middle, grad_mixed, dense_vectors = made["backward"]
        (grad_middle,) = order.after(grad_middle)
        made["input"] = call(
            functools.partial(input_kernel, factor), count,
            [rows_of(D), edges, whole(2, D), vec, mols_of(3, HALF, WIDE), mols_of(3, HALF, WIDE), weight, weight,
             weight, rows_of(D), whole(8, D), whole(8, wide), whole(8, wide)],
            [rows_of(D), whole(16, D)],
            [shape_of(rows, D, dtype=BF16), shape_of(16, D)],
            [column],
            (*scalars, tokens, kinds, type_table, first_gain, made[0][0], made[1][0], query_weight, key_weight,
             value_weight, grad_middle, dense_vectors, made[0][1], made[1][1]),
            flops=3 * unit, name="input", vmem=40 * 2**20,
        )
        order.add(made["input"][1])

    def own_parts(name, targets, column=0):
        while not transfers[name].own:
            transfers[name].go()
        return [(piece, (0, low, targets, column)) for low, piece in enumerate(transfers[name].own)]

    def other_parts(name, targets, column=0):
        while transfers[name].result is None:
            transfers[name].go()
        return [(piece, (1, low, targets, column)) for low, piece in enumerate(transfers[name].result[0])]

    def into_place(step):
        before, three = (), (0, 1, 2)
        if step == "a":
            found = other_parts("A", (0, 1)) + own_parts("A", (0, 1))
        elif step == "o":
            found = other_parts("O", (0,)) + own_parts("O", (0,))
        elif step == "b":
            found = other_parts("B", three) + own_parts("B", three)
        elif step == "q":
            found, before = own_parts("C", three, HALF), placed["b"]
        else:
            found, before = other_parts("C", three, HALF), placed["q"]
        pieces, parts = zip(*found)
        placed[step] = put_in_place(
            place, order.after(*pieces), parts, {"a": 2, "o": 1}.get(step, 3), before
        )
        order.add(placed[step][0])

    def finish_vectors():
        if "vectors" not in made:
            small = transfers["O"].result[1]
            made["vectors"] = [small[i] for i in (4, 5, 12, 9, 8, 0, 1, 10, 11)] + [small[2:4]]
            order.add(*order.before, *made["vectors"])

    kernels = {"F": dense_forward, "D": dense_backward, "0": lambda: back(0), "1": lambda: back(1), "I": to_input}
    for step in SCHEDULE:
        if step in kernels:
            kernels[step]()
        elif step in "wxyz":
            begin("AOBC"["wxyz".index(step)])
        elif step in transfers:
            transfers[step].go()
            if step == "O" and transfers[step].result is not None:
                finish_vectors()
        else:
            into_place(step)
    outer_grad, inner_grad = placed["a"]
    (output_grad,) = placed["o"]
    query_grad, key_grad, value_grad = placed["r"]
    layer_out = made["backward"][0]
    tokens_grad = made["input"][0]
    finish_vectors()
    return tuple(
        [layer_out, tokens_grad]
        + [grad.reshape(D, D) for grad in (query_grad, key_grad, value_grad, output_grad, inner_grad, outer_grad)]
        + made["vectors"]
    )


def solution(mesh):
    split = P(AXES, None)
    return jax.shard_map(
        functools.partial(per_device, dict(mesh.shape)),
        mesh=mesh,
        in_specs=(split, P(AXES), P(AXES)) + (P(),) * 16 + (split,),
        out_specs=(split, split) + (P(),) * 16,
        check_vma=False,
    )
```
